512 devices in a mesh: rows: 64 (over x, z, core), cols: 8 (over y).
Axes of the slice: x: 4, y: 8, z: 8, core: 2. Of those that a mesh axis runs over, the one named last changes fastest.
Arguments:
- coeffs: bfloat16 [16384, 2048], P('rows'), may hold values from -0.5 to 0.5
- rotation: float32 [2048, 2048], P('rows', 'cols'), may hold values from -6 to 6
- phase_ops: bfloat16 [2, 128, 5, 128, 128], P(None, 'rows'), as said below
- block_links: int32 [128, 5], P('rows'), may hold values from 0 to 1, as said below
- atom_size: int32 [128], P('rows'), may hold values from 1 to 128, 12288 in all
Outputs:
- rotated: float32 [2048, 2048], P('rows', 'cols')
- phase_cos: float32 [2048, 2048], P('rows', 'cols')
- phase_sin: float32 [2048, 2048], P('rows', 'cols')
- orbitals: bfloat16 [16384, 2048], P('rows', 'cols')
The draws below stay inside these ranges and needn't reach their ends.
Inputs may be any that keep to these rules, and one draw needn't show every extreme that they name: block_links[b, 2 + o] equals block_links[(b + o) mod 128, 2 - o], and block_links[b, 2] is 1. Each phase operator is symmetric as a 16384 x 16384 matrix: phase_ops[p, b, 2 + o] is the transpose of phase_ops[p, (b + o) mod 128, 2 - o].
All inputs are finite; a program needn't handle non-finite values. No bound on the sum of `atom_size` on one device may be relied on, other than what follows from the above.
Results may differ from the reference program's by a relative error of at most 0.0049.
Values may be sent and summed in bfloat16 or wider, within the bound.
No kernel may reach another device: no remote copies, remote signals or barrier semaphores. Data moves between devices by JAX's collectives and lax.ppermute only.
A program may use at most 64 MiB of HBM per device.

```python
import math
import jax
import jax.numpy as jnp
import numpy as np
from jax import lax

K = 2048
NB = 16384
BLK = 128
REACH = 2
NBLK = 128
SPAN = 5


def draw_block_links(key, part):
    key = jax.random.fold_in(key, 11)
    upper = jax.random.randint(key, (NBLK, REACH + 1), 0, 2)
    upper = upper.at[:, 0].set(1)
    columns = [jnp.roll(upper[:, offset], offset)[:, None] for offset in range(REACH, 0, -1)]
    columns = columns + [upper[:, offset][:, None] for offset in range(0, REACH + 1)]
    return jnp.concatenate(columns, axis=1).astype(jnp.int32)


def draw_phase_ops(key, part):
    key = jax.random.fold_in(key, 23)
    shape = (2, NBLK, REACH + 1, BLK, BLK)
    factor = (BLK * (2 * REACH + 1)) ** (-0.5)
    raw = jax.random.normal(key, shape, jnp.float32)
    raw = raw * factor
    lower = [jnp.swapaxes(jnp.roll(raw[:, :, offset], offset, axis=1), -1, -2)[:, :, None] for offset in range(REACH, 0, -1)]
    centre = ((raw[:, :, 0] + jnp.swapaxes(raw[:, :, 0], -1, -2)) * 0.70710678)[:, :, None]
    upper = [raw[:, :, offset][:, :, None] for offset in range(1, REACH + 1)]
    return jnp.concatenate(lower + [centre] + upper, axis=2).astype(jnp.bfloat16)


def block_levels(rng, extent, split, least, top_value):
    def one(dim, blocks):
        draws = jax.random.uniform(jax.random.fold_in(jax.random.fold_in(rng, 6), dim), (blocks,), jnp.float32, least / len(split), top_value / len(split))
        return jnp.repeat(jnp.exp(draws), extent[dim] // blocks).reshape((-1,) + (1,) * (len(extent) - dim - 1))

    gain = one(*split[0])
    for cut in split[1:]:
        gain = gain * one(*cut)
    return gain


def length_profile(count, total, bound, skew):
    portions = [(1 << 20) // math.isqrt(standing ** skew) + 1 for standing in range(2, count + 1)]
    rest, holding = total - bound - (count - 1), [1] * (count - 1)
    while rest > 0:
        candidates = [i for i in range(count - 1) if holding[i] < bound]
        mass, remaining = sum([portions[i] for i in candidates]), rest
        for i in candidates:
            extra = min(bound - holding[i], max(1, remaining * portions[i] // mass), rest)
            holding[i] = holding[i] + extra
            rest = rest - extra
    return np.array([bound] + holding)


def ragged_sizes(rng, amount, total, most, skew):
    if amount == 2:
        one = jax.random.randint(rng, (), max(1, total - most), min(most, total - 1) + 1)
        return jnp.stack([one, total - one])
    sizes = jnp.asarray(length_profile(amount, total, most, skew), jnp.int32)
    couples = (amount - 1) // 2
    donor, receiver = sizes[1:1 + 2 * couples:2], sizes[2:2 + 2 * couples:2]
    room = jnp.minimum(donor - 1, most - receiver)
    passed = jax.random.randint(jax.random.fold_in(rng, 1), (couples,), 0, 1 << 20) % (room + 1)
    sizes = sizes.at[1:1 + 2 * couples:2].set(donor - passed).at[2:2 + 2 * couples:2].set(receiver + passed)
    return sizes[jax.random.permutation(jax.random.fold_in(rng, 2), amount)]


def normal_values(rng, extent, scale, most, pieces=(), kind=jnp.bfloat16):
    drawn = scale * jax.random.normal(rng, extent, jnp.float32)
    if pieces:
        drawn = drawn * block_levels(rng, extent, pieces, -0.22, 0.18)
    return jnp.clip(drawn, -most, most).astype(kind)


def setup_inputs(seed: int = 0) -> dict:
    keys = jax.random.split(jax.random.key(seed), 6)
    return {
        "coeffs": normal_values(keys[0], (NB, K), BLK ** -0.5, 0.5, ((0, 64),)),
        "rotation": normal_values(keys[1], (K, K), 1.0, 6.0, ((0, 64), (1, 8)), jnp.float32),
        "phase_ops": draw_phase_ops(jax.random.fold_in(keys[5], 71), 0),
        "block_links": draw_block_links(jax.random.fold_in(keys[5], 71), 0),
        "atom_size": ragged_sizes(keys[4], NBLK, 3 * BLK * NBLK // 4, BLK, 1).astype(jnp.int32),
    }


highest = lax.Precision.HIGHEST

def mat_product(left, right):
    return jnp.dot(left, right, precision=highest, preferred_element_type=jnp.float32)

def reference(coeffs, rotation, phase_ops, block_links, atom_size):
    blocks_all = NB // BLK
    within = jnp.arange(BLK, dtype=jnp.int32)
    live_rows = (within[None, :] < atom_size[:, None]).reshape(NB)
    masked = jnp.where(live_rows[:, None], coeffs, jnp.zeros_like(coeffs))
    grouped = masked.reshape(blocks_all, BLK, K)
    gated = phase_ops * block_links[None, :, :, None, None].astype(jnp.bfloat16)
    applied = jnp.zeros((2, blocks_all, BLK, K), jnp.float32)
    for offset in range(SPAN):
        rolled = jnp.roll(grouped, -(offset - REACH), axis=0).astype(jnp.float32)
        applied = applied + jnp.einsum('pbij,bjk->pbik', gated[:, :, offset].astype(jnp.float32), rolled)
    applied = applied.astype(jnp.bfloat16).reshape(2, NB, K)
    left_side = masked.T.astype(jnp.float32)
    cos_phase = jnp.dot(left_side, applied[0].astype(jnp.float32), preferred_element_type=jnp.float32)
    sin_phase = jnp.dot(left_side, applied[1].astype(jnp.float32), preferred_element_type=jnp.float32)
    diag_cos = jnp.diagonal(cos_phase)
    diag_sin = jnp.diagonal(sin_phase)
    cos_part = cos_phase * (diag_cos[None, :] - diag_cos[:, None])
    sin_part = sin_phase * (diag_sin[None, :] - diag_sin[:, None])
    generator = (cos_part + sin_part) * (0.125 / math.sqrt(K))
    squared = mat_product(generator, generator)
    identity = jnp.eye(K, dtype=jnp.float32)
    forward = identity + generator + 0.5 * squared
    backward = identity - generator + 0.5 * squared
    rotated = mat_product(rotation, forward)
    phase_cos = mat_product(mat_product(backward, cos_phase), forward)
    phase_sin = mat_product(mat_product(backward, sin_phase), forward)
    forward_half = forward.astype(jnp.bfloat16).astype(jnp.float32)
    orbitals = jnp.dot(masked.astype(jnp.float32), forward_half, preferred_element_type=jnp.float32).astype(jnp.bfloat16)
    return (rotated, phase_cos, phase_sin, orbitals)
```

```python
import math

import jax
import jax.numpy as jnp
from jax import lax
from jax.sharding import PartitionSpec as P

bf16 = jnp.bfloat16
f32 = jnp.float32

XS, ZS, CORES = 4, 8, 2


def row_index(x, z, core):
    return (x * ZS + z) * CORES + core


x_groups = [[row_index(x, z, k) for x in range(XS)] for z in range(ZS) for k in range(CORES)]
z_groups = [[row_index(x, z, k) for z in range(ZS)] for x in range(XS) for k in range(CORES)]
xz_groups = [
    [row_index(x, z, k) for x in range(XS) for z in range(ZS)] for k in range(CORES)
]


def swap(cells, axis, groups=None):
    return lax.all_to_all(cells, axis, 0, 0, tiled=True, axis_index_groups=groups)


def spread(cells, count, axis, groups=None):
    return swap(jnp.broadcast_to(cells[None], (count,) + cells.shape), axis, groups)


def other_core(cells):
    count = lax.axis_size("rows")
    return lax.ppermute(cells, "rows", [(i, i ^ 1) for i in range(count)])


def small_product(left, right):
    return jnp.dot(left, right, preferred_element_type=f32)


def three_parts(values):
    parts = []
    for _ in range(3):
        part = lax.reduce_precision(values, 8, 7)
        parts.append(part.astype(bf16))
        values = values - part
    return jnp.stack(parts)


def on_device(coeffs, rotation, phase_ops, block_links, atom_size):
    rows_dev, orbital_count = coeffs.shape
    blocks_dev = phase_ops.shape[1]
    span_blocks = phase_ops.shape[2]
    block_size = phase_ops.shape[3]
    reach_blocks = (span_blocks - 1) // 2
    rows_axis = lax.axis_size("rows")
    cols_axis = lax.axis_size("cols")
    row_count = orbital_count // rows_axis
    col_count = orbital_count // cols_axis
    both = 2 * col_count
    row_start = lax.axis_index("rows") * row_count
    col_start = lax.axis_index("cols") * col_count
    core = lax.axis_index("rows") % CORES
    scale_factor = 0.125 / math.sqrt(orbital_count)

    within = lax.broadcasted_iota(jnp.int32, (blocks_dev, block_size), 1)
    live_rows = (within < atom_size[:, None]).reshape(rows_dev)
    raw_cols = lax.dynamic_slice_in_dim(coeffs, col_start, col_count, 1)
    own_cols = jnp.where(live_rows[:, None], raw_cols, jnp.zeros_like(raw_cols))
    width = reach_blocks * block_size
    up = [(i, (i + 1) % rows_axis) for i in range(rows_axis)]
    down = [((i + 1) % rows_axis, i) for i in range(rows_axis)]
    padded = jnp.concatenate(
        [
            lax.ppermute(own_cols[rows_dev - width :], "rows", up),
            own_cols,
            lax.ppermute(own_cols[:width], "rows", down),
        ],
        axis=0,
    )
    masked = jnp.where(live_rows[:, None], coeffs, jnp.zeros_like(coeffs))
    stacked = jnp.stack(
        [
            padded[offset * block_size : (offset + blocks_dev) * block_size].reshape(
                blocks_dev, block_size, col_count
            )
            for offset in range(span_blocks)
        ],
        axis=1,
    )
    gated = phase_ops * block_links[None, :, :, None, None].astype(bf16)
    applied = jnp.einsum("pbtij,btjk->pbik", gated, stacked, preferred_element_type=f32)
    applied = applied.reshape(2, rows_dev, col_count).astype(bf16)

    product = jnp.einsum("ni,pnj->ipj", masked, applied, preferred_element_type=f32)
    product = product.reshape(XS, ZS, CORES, row_count, both)
    own_half = lax.dynamic_index_in_dim(product, core, 2, keepdims=False)
    far_half = lax.dynamic_index_in_dim(product, 1 - core, 2, keepdims=False)
    diag = jnp.einsum("nj,pnj->pj", own_cols, applied, preferred_element_type=f32)

    def diag_rows(values):
        return jnp.pad(three_parts(values.reshape(both)), ((0, 13), (0, 0)))

    def diag_sum(cells):
        return jnp.sum(cells[:, :3].astype(f32), axis=(0, 1))

    chip_rows = ZS * row_count
    sent = jnp.concatenate(
        [far_half.astype(bf16).reshape(XS * chip_rows, both), diag_rows(diag)], axis=0
    )
    got = other_core(sent)
    diag = diag.reshape(both) + diag_sum(got[None, XS * chip_rows :])
    half = own_half.reshape(XS, chip_rows, both) + got[: XS * chip_rows].reshape(
        XS, chip_rows, both
    ).astype(f32)

    def with_diag(cells, values):
        tail = jnp.broadcast_to(diag_rows(values)[None], (cells.shape[0], 16, both))
        return jnp.concatenate([cells.astype(bf16), tail], axis=1)

    got = swap(with_diag(half, diag), "rows", x_groups)
    diag = diag_sum(got[:, chip_rows:])
    chip = jnp.sum(got[:, :chip_rows].astype(f32), axis=0).reshape(ZS, row_count, both)
    got = swap(with_diag(chip, diag), "rows", z_groups)
    diag = diag_sum(got[:, row_count:])
    z_block = jnp.sum(got[:, :row_count].astype(f32), axis=0)
    z_half = z_block.astype(bf16)

    packed = jnp.concatenate(
        [
            jnp.concatenate([z_half, rotation.astype(bf16)], axis=1),
            jnp.pad(diag_rows(diag), ((0, 0), (0, col_count))),
        ],
        axis=0,
    )
    across = spread(packed, cols_axis, "cols")

    def rows_of(cells):
        return cells.transpose(1, 0, 2).reshape(cells.shape[1], -1)

    z_rows = [
        rows_of(across[:, :row_count, p * col_count : (p + 1) * col_count]) for p in range(2)
    ]
    rot_rows = rows_of(across[:, :row_count, both:])
    diag_all = jnp.sum(across[:, row_count : row_count + 3, :both].astype(f32), axis=1)
    diag_all = diag_all.reshape(cols_axis, 2, col_count).transpose(1, 0, 2).reshape(2, -1)

    def halves(cells):
        away = other_core(cells)
        pair = jnp.where(core == 0, jnp.stack([cells, away], 1), jnp.stack([away, cells], 1))
        return pair.reshape(orbital_count, -1)

    panel = spread(z_half, ZS, "rows", z_groups)
    panel = spread(panel, XS, "rows", x_groups)
    z_cols = halves(panel.reshape(XS * ZS, row_count, both))

    diag_cols = lax.dynamic_slice_in_dim(diag_all, col_start, col_count, 1)
    diag_down = lax.dynamic_slice_in_dim(diag_all, row_start, row_count, 1)

    def generator(cos_block, sin_block, across_diag, down_diag):
        cos_part = cos_block.astype(f32) * (across_diag[0][None, :] - down_diag[0][:, None])
        sin_part = sin_block.astype(f32) * (across_diag[1][None, :] - down_diag[1][:, None])
        return (cos_part + sin_part) * scale_factor

    gen_cols = generator(z_cols[:, :col_count], z_cols[:, col_count:], diag_cols, diag_all)
    gen_cols = gen_cols.astype(bf16)
    gen_rows = generator(z_rows[0], z_rows[1], diag_all, diag_down)
    gen_block = generator(z_block[:, :col_count], z_block[:, col_count:], diag_cols, diag_down)

    square = small_product(gen_rows.astype(bf16), gen_cols)
    step = (gen_block + 0.5 * square).astype(bf16)
    step_cols = spread(step, XS * ZS, "rows", xz_groups)
    square_rows = rows_of(spread(square.astype(bf16), cols_axis, "cols"))
    back_rows = (0.5 * square_rows.astype(f32) - gen_rows).astype(bf16)
    half_block = z_block + small_product(back_rows, z_cols)
    step_cols = halves(step_cols)
    half_across = spread(half_block.astype(bf16), cols_axis, "cols")
    half_rows = [
        rows_of(half_across[:, :, p * col_count : (p + 1) * col_count]) for p in range(2)
    ]
    rotated = rotation + small_product(rot_rows, step_cols)
    orbitals = (own_cols.astype(f32) + small_product(masked, step_cols)).astype(bf16)
    phase_cos = half_block[:, :col_count] + small_product(half_rows[0], step_cols)
    phase_sin = half_block[:, col_count:] + small_product(half_rows[1], step_cols)
    return (rotated, phase_cos, phase_sin, orbitals)


def solution(mesh):
    placed = (
        P("rows", None),
        P("rows", "cols"),
        P(None, "rows", None, None, None),
        P("rows", None),
        P("rows"),
    )
    return jax.shard_map(
        on_device,
        mesh=mesh,
        in_specs=placed,
        out_specs=(P("rows", "cols"), P("rows", "cols"), P("rows", "cols"), P("rows", "cols")),
        check_vma=False,
    )
```

```python
import math

import jax
import jax.numpy as jnp
from jax import lax
from jax.sharding import PartitionSpec as P

bf16 = jnp.bfloat16
f32 = jnp.float32

XS, ZS, CORES = 4, 8, 2


def row_index(x, z, core):
    return (x * ZS + z) * CORES + core


xz_groups = [
    [row_index(x, z, k) for x in range(XS) for z in range(ZS)] for k in range(CORES)
]


def swap(cells, axis, groups=None):
    return lax.all_to_all(cells, axis, 0, 0, tiled=True, axis_index_groups=groups)


def spread(cells, count, axis, groups=None):
    return swap(jnp.broadcast_to(cells[None], (count,) + cells.shape), axis, groups)


def other_core(cells):
    count = lax.axis_size("rows")
    return lax.ppermute(cells, "rows", [(i, i ^ 1) for i in range(count)])


def small_product(left, right):
    return jnp.dot(left, right, preferred_element_type=f32)


def on_device(coeffs, rotation, phase_ops, block_links, atom_size):
    rows_dev, orbital_count = coeffs.shape
    blocks_dev = phase_ops.shape[1]
    span_blocks = phase_ops.shape[2]
    block_size = phase_ops.shape[3]
    reach_blocks = (span_blocks - 1) // 2
    rows_axis = lax.axis_size("rows")
    cols_axis = lax.axis_size("cols")
    row_count = orbital_count // rows_axis
    col_count = orbital_count // cols_axis
    both = 2 * col_count
    row_start = lax.axis_index("rows") * row_count
    col_start = lax.axis_index("cols") * col_count
    core = lax.axis_index("rows") % CORES
    scale_factor = 0.125 / math.sqrt(orbital_count)

    def lanes_out(cells):
        lead, rows, wide = cells.shape[:-2], cells.shape[-2], cells.shape[-1]
        cells = cells.reshape(lead + (rows, wide // 128, 128))
        return jnp.swapaxes(cells, -3, -2).reshape(lead + (rows * wide // 128, 128))

    def lanes_in(cells, rows):
        lead = cells.shape[:-2]
        cells = cells.reshape(lead + (-1, rows, 128))
        return jnp.swapaxes(cells, -3, -2).reshape(lead + (rows, -1))

    within = lax.broadcasted_iota(jnp.int32, (blocks_dev, block_size), 1)
    live_rows = (within < atom_size[:, None]).reshape(rows_dev)
    raw_cols = lax.dynamic_slice_in_dim(coeffs, col_start, col_count, 1)
    own_cols = jnp.where(live_rows[:, None], raw_cols, jnp.zeros_like(raw_cols))
    width = reach_blocks * block_size
    up = [(i, (i + 1) % rows_axis) for i in range(rows_axis)]
    down = [((i + 1) % rows_axis, i) for i in range(rows_axis)]
    padded = jnp.concatenate(
        [
            lax.ppermute(own_cols[rows_dev - width :], "rows", up),
            own_cols,
            lax.ppermute(own_cols[:width], "rows", down),
        ],
        axis=0,
    )
    masked = jnp.where(live_rows[:, None], coeffs, jnp.zeros_like(coeffs))
    turned = masked.T.reshape(XS * ZS, CORES, row_count, rows_dev)
    own_turned = lax.dynamic_index_in_dim(turned, core, 1, keepdims=False)
    far_turned = other_core(lax.dynamic_index_in_dim(turned, 1 - core, 1, keepdims=False))
    stacked = jnp.stack(
        [
            padded[offset * block_size : (offset + blocks_dev) * block_size].reshape(
                blocks_dev, block_size, col_count
            )
            for offset in range(span_blocks)
        ],
        axis=1,
    )
    gated = phase_ops * block_links[None, :, :, None, None].astype(bf16)
    applied = jnp.einsum("pbtij,btjk->bipk", gated, stacked, preferred_element_type=f32)
    applied = applied.reshape(rows_dev, both).astype(bf16)
    far_applied = other_core(applied)

    product = small_product(own_turned.reshape(-1, rows_dev), applied)
    product = product + small_product(far_turned.reshape(-1, rows_dev), far_applied)

    def diag_of(cols, values):
        return jnp.sum(jnp.tile(cols, (1, 2)).astype(f32) * values.astype(f32), axis=0)

    far_cols = jnp.where(core == 0, padded[width + rows_dev :], padded[:width])
    diag = diag_of(own_cols, applied) + diag_of(far_cols, far_applied)

    def two_parts(values):
        high = lax.reduce_precision(values, 8, 7)
        return jnp.stack([high.astype(bf16), (values - high).astype(bf16)]).reshape(-1, 128)

    tail_rows = 2 * both // 128

    def parts_sum(cells):
        cells = cells.astype(f32).reshape(-1, 2, both)
        return cells[:, 0] + cells[:, 1]

    tail = jnp.broadcast_to(two_parts(diag)[None], (XS * ZS, tail_rows, 128))
    pieces = lanes_out(product.astype(bf16).reshape(XS * ZS, row_count, both))
    got = swap(jnp.concatenate([pieces, tail], axis=1), "rows", xz_groups)
    body_rows = row_count * both // 128
    diag = jnp.sum(parts_sum(got[:, body_rows:]), axis=0)
    z_block = lanes_in(jnp.sum(got[:, :body_rows].astype(f32), axis=0), row_count)
    z_half = z_block.astype(bf16)

    packed = jnp.concatenate(
        [lanes_out(z_half), lanes_out(rotation.astype(bf16)), two_parts(diag)], axis=0
    )
    across = spread(packed, cols_axis, "cols")

    def rows_of(cells):
        return cells.transpose(1, 0, 2).reshape(cells.shape[1], -1)

    wide = lanes_in(across[:, :-tail_rows], row_count)
    z_rows = [rows_of(wide[:, :, p * col_count : (p + 1) * col_count]) for p in range(2)]
    rot_rows = rows_of(wide[:, :, both:])
    diag_all = parts_sum(across[:, -tail_rows:])
    diag_all = diag_all.reshape(cols_axis, 2, col_count).transpose(1, 0, 2).reshape(2, -1)

    def halves(cells):
        away = other_core(cells)
        pair = jnp.where(core == 0, jnp.stack([cells, away], 1), jnp.stack([away, cells], 1))
        return pair.reshape(orbital_count, -1)

    panel = spread(z_half, XS * ZS, "rows", xz_groups)
    z_cols = halves(panel)

    diag_cols = lax.dynamic_slice_in_dim(diag_all, col_start, col_count, 1)
    diag_down = lax.dynamic_slice_in_dim(diag_all, row_start, row_count, 1)

    def generator(cos_block, sin_block, across_diag, down_diag):
        cos_part = cos_block.astype(f32) * (across_diag[0][None, :] - down_diag[0][:, None])
        sin_part = sin_block.astype(f32) * (across_diag[1][None, :] - down_diag[1][:, None])
        return (cos_part + sin_part) * scale_factor

    gen_cols = generator(z_cols[:, :col_count], z_cols[:, col_count:], diag_cols, diag_all)
    gen_cols = gen_cols.astype(bf16)
    gen_rows = generator(z_rows[0], z_rows[1], diag_all, diag_down)
    gen_block = generator(z_block[:, :col_count], z_block[:, col_count:], diag_cols, diag_down)

    square = small_product(gen_rows.astype(bf16), gen_cols)
    step = (gen_block + 0.5 * square).astype(bf16)
    step_cols = spread(step, XS * ZS, "rows", xz_groups)
    square_rows = rows_of(spread(square.astype(bf16), cols_axis, "cols"))
    back_rows = (0.5 * square_rows.astype(f32) - gen_rows).astype(bf16)
    half_block = z_block + small_product(back_rows, z_cols)
    step_cols = halves(step_cols)
    half_across = spread(half_block.astype(bf16), cols_axis, "cols")
    half_rows = [
        rows_of(half_across[:, :, p * col_count : (p + 1) * col_count]) for p in range(2)
    ]
    rotated = rotation + small_product(rot_rows, step_cols)
    orbitals = (own_cols.astype(f32) + small_product(masked, step_cols)).astype(bf16)
    phase_cos = half_block[:, :col_count] + small_product(half_rows[0], step_cols)
    phase_sin = half_block[:, col_count:] + small_product(half_rows[1], step_cols)
    return (rotated, phase_cos, phase_sin, orbitals)


def solution(mesh):
    placed = (
        P("rows", None),
        P("rows", "cols"),
        P(None, "rows", None, None, None),
        P("rows", None),
        P("rows"),
    )
    return jax.shard_map(
        on_device,
        mesh=mesh,
        in_specs=placed,
        out_specs=(P("rows", "cols"), P("rows", "cols"), P("rows", "cols"), P("rows", "cols")),
        check_vma=False,
    )
```

```python
import math

import jax
import jax.numpy as jnp
from jax import lax
from jax.sharding import PartitionSpec as P

bf16 = jnp.bfloat16
f32 = jnp.float32

XS, ZS, CORES = 4, 8, 2


def row_index(x, z, core):
    return (x * ZS + z) * CORES + core


x_groups = [[row_index(x, z, k) for x in range(XS)] for z in range(ZS) for k in range(CORES)]
z_groups = [[row_index(x, z, k) for z in range(ZS)] for x in range(XS) for k in range(CORES)]


def swap(cells, axis, groups=None):
    return lax.all_to_all(cells, axis, 0, 0, tiled=True, axis_index_groups=groups)


def spread(cells, count, axis, groups=None):
    return swap(jnp.broadcast_to(cells[None], (count,) + cells.shape), axis, groups)


def other_core(cells):
    count = lax.axis_size("rows")
    return lax.ppermute(cells, "rows", [(i, i ^ 1) for i in range(count)])


def small_product(left, right):
    return jnp.dot(left, right, preferred_element_type=f32)


def on_device(coeffs, rotation, phase_ops, block_links, atom_size):
    rows_dev, orbital_count = coeffs.shape
    blocks_dev = phase_ops.shape[1]
    span_blocks = phase_ops.shape[2]
    block_size = phase_ops.shape[3]
    reach_blocks = (span_blocks - 1) // 2
    rows_axis = lax.axis_size("rows")
    cols_axis = lax.axis_size("cols")
    row_count = orbital_count // rows_axis
    col_count = orbital_count // cols_axis
    both = 2 * col_count
    row_start = lax.axis_index("rows") * row_count
    col_start = lax.axis_index("cols") * col_count
    core = lax.axis_index("rows") % CORES
    scale_factor = 0.125 / math.sqrt(orbital_count)

    within = lax.broadcasted_iota(jnp.int32, (blocks_dev, block_size), 1)
    live_rows = (within < atom_size[:, None]).reshape(rows_dev)
    raw_cols = lax.dynamic_slice_in_dim(coeffs, col_start, col_count, 1)
    own_cols = jnp.where(live_rows[:, None], raw_cols, jnp.zeros_like(raw_cols))
    width = reach_blocks * block_size
    up = [(i, (i + 1) % rows_axis) for i in range(rows_axis)]
    down = [((i + 1) % rows_axis, i) for i in range(rows_axis)]
    padded = jnp.concatenate(
        [
            lax.ppermute(own_cols[rows_dev - width :], "rows", up),
            own_cols,
            lax.ppermute(own_cols[:width], "rows", down),
        ],
        axis=0,
    )
    masked = jnp.where(live_rows[:, None], coeffs, jnp.zeros_like(coeffs))
    turned = masked.T.reshape(XS, ZS, CORES, row_count, rows_dev)

    def turned_half(which):
        half = lax.dynamic_index_in_dim(turned, which, 2, keepdims=False)
        return half.swapaxes(0, 1).reshape(-1, rows_dev)

    own_turned = turned_half(core)
    far_turned = other_core(turned_half(1 - core))
    stacked = jnp.stack(
        [
            padded[offset * block_size : (offset + blocks_dev) * block_size].reshape(
                blocks_dev, block_size, col_count
            )
            for offset in range(span_blocks)
        ],
        axis=1,
    )
    gated = phase_ops * block_links[None, :, :, None, None].astype(bf16)
    applied = jnp.einsum("pbtij,btjk->bipk", gated, stacked, preferred_element_type=f32)
    applied = applied.reshape(rows_dev, both).astype(bf16)
    far_applied = other_core(applied)

    product = small_product(own_turned, applied) + small_product(far_turned, far_applied)

    def diag_of(cols, values):
        return jnp.sum(jnp.tile(cols, (1, 2)).astype(f32) * values.astype(f32), axis=0)

    far_cols = jnp.where(core == 0, padded[width + rows_dev :], padded[:width])
    diag = diag_of(own_cols, applied) + diag_of(far_cols, far_applied)

    def with_diag(cells, values):
        high = lax.reduce_precision(values, 8, 7)
        tail = jnp.stack([high, values - high]).astype(bf16)
        tail = jnp.pad(tail, ((0, 6), (0, 0)))
        tail = jnp.broadcast_to(tail, cells.shape[:-2] + tail.shape)
        return jnp.concatenate([cells.astype(bf16), tail], axis=-2)

    def summed(cells):
        body, tail = cells[:, :-8].astype(f32), cells[:, -8:-6].astype(f32)
        return jnp.sum(body, axis=0), jnp.sum(tail, axis=(0, 1))

    group_rows = XS * row_count
    pieces = with_diag(product.reshape(ZS, group_rows, both), diag)
    chip, diag = summed(swap(pieces, "rows", z_groups))
    chip, diag = summed(spread(with_diag(chip, diag), XS, "rows", x_groups))
    own_x = lax.axis_index("rows") // (ZS * CORES)
    z_block = lax.dynamic_slice_in_dim(chip, own_x * row_count, row_count, 0)

    tail = jnp.pad(diag.reshape(2, col_count), ((0, row_count - 2), (0, 0)))
    packed = jnp.concatenate([z_block, rotation, tail], axis=1)
    across = lax.all_gather(packed, "cols", axis=0)

    def rows_of(cells):
        return cells.transpose(1, 0, 2).reshape(cells.shape[1], -1)

    z_rows = [rows_of(across[:, :, p * col_count : (p + 1) * col_count]) for p in range(2)]
    rot_rows = rows_of(across[:, :, both : both + col_count]).astype(bf16)
    diag_all = across[:, :2, both + col_count :].transpose(1, 0, 2).reshape(2, -1)

    panel = spread(chip.astype(bf16), ZS, "rows", z_groups)
    panel = panel.reshape(ZS, XS, row_count, both)
    away = other_core(panel)
    z_cols = jnp.where(core == 0, jnp.stack([panel, away], 2), jnp.stack([away, panel], 2))
    z_cols = z_cols.swapaxes(0, 1).reshape(orbital_count, both)

    diag_cols = lax.dynamic_slice_in_dim(diag_all, col_start, col_count, 1)
    diag_down = lax.dynamic_slice_in_dim(diag_all, row_start, row_count, 1)

    def generator(cos_block, sin_block, across_diag, down_diag):
        cos_part = cos_block.astype(f32) * (across_diag[0][None, :] - down_diag[0][:, None])
        sin_part = sin_block.astype(f32) * (across_diag[1][None, :] - down_diag[1][:, None])
        return (cos_part + sin_part) * scale_factor

    gen_cols = generator(z_cols[:, :col_count], z_cols[:, col_count:], diag_cols, diag_all)
    gen_cols = gen_cols.astype(bf16)
    gen_rows = generator(z_rows[0], z_rows[1], diag_all, diag_down)
    gen_block = generator(z_block[:, :col_count], z_block[:, col_count:], diag_cols, diag_down)

    def row_panels(block):
        cells = spread(block.astype(bf16), cols_axis, "cols")
        return [
            rows_of(cells[:, :, start : start + col_count])
            for start in range(0, block.shape[1], col_count)
        ]

    square = small_product(gen_rows.astype(bf16), gen_cols)
    first_rot = small_product(rot_rows, gen_cols)
    first_orb = small_product(masked, gen_cols)
    firsts = lax.all_gather(
        jnp.concatenate([first_orb, first_rot], axis=0).astype(bf16), "cols", axis=0
    )
    (square_rows,) = row_panels(square)
    back_rows = (0.5 * square_rows.astype(f32) - gen_rows).astype(bf16)
    half_block = z_block + small_product(back_rows, z_cols)
    half_rows = row_panels(half_block)
    first_cos = small_product(half_rows[0], gen_cols)
    first_sin = small_product(half_rows[1], gen_cols)
    first_rows = row_panels(jnp.concatenate([first_cos, first_sin], axis=1))
    first_rows = jnp.concatenate([rows_of(firsts), *first_rows], axis=0)
    second = 0.5 * small_product(first_rows, gen_cols)
    cuts = [rows_dev, rows_dev + row_count, rows_dev + 2 * row_count]
    second_orb, second_rot, second_cos, second_sin = jnp.split(second, cuts, axis=0)
    rotated = rotation + first_rot + second_rot
    orbitals = (own_cols.astype(f32) + first_orb + second_orb).astype(bf16)
    phase_cos = half_block[:, :col_count] + first_cos + second_cos
    phase_sin = half_block[:, col_count:] + first_sin + second_sin
    return (rotated, phase_cos, phase_sin, orbitals)


def solution(mesh):
    placed = (
        P("rows", None),
        P("rows", "cols"),
        P(None, "rows", None, None, None),
        P("rows", None),
        P("rows"),
    )
    return jax.shard_map(
        on_device,
        mesh=mesh,
        in_specs=placed,
        out_specs=(P("rows", "cols"), P("rows", "cols"), P("rows", "cols"), P("rows", "cols")),
        check_vma=False,
    )
```

```python
import math

import jax
import jax.numpy as jnp
from jax import lax
from jax.sharding import PartitionSpec as P

bf16 = jnp.bfloat16
f32 = jnp.float32

XS, ZS, CORES = 4, 8, 2


def row_index(x, z, core):
    return (x * ZS + z) * CORES + core


x_groups = [[row_index(x, z, k) for x in range(XS)] for z in range(ZS) for k in range(CORES)]
z_groups = [[row_index(x, z, k) for z in range(ZS)] for x in range(XS) for k in range(CORES)]
xz_groups = [
    [row_index(x, z, k) for x in range(XS) for z in range(ZS)] for k in range(CORES)
]


def swap(cells, axis, groups=None):
    return lax.all_to_all(cells, axis, 0, 0, tiled=True, axis_index_groups=groups)


def spread(cells, count, axis, groups=None):
    return swap(jnp.broadcast_to(cells[None], (count,) + cells.shape), axis, groups)


def other_core(cells):
    count = lax.axis_size("rows")
    return lax.ppermute(cells, "rows", [(i, i ^ 1) for i in range(count)])


def small_product(left, right):
    return jnp.dot(left, right, preferred_element_type=f32)


def on_device(coeffs, rotation, phase_ops, block_links, atom_size):
    rows_dev, orbital_count = coeffs.shape
    blocks_dev = phase_ops.shape[1]
    span_blocks = phase_ops.shape[2]
    block_size = phase_ops.shape[3]
    reach_blocks = (span_blocks - 1) // 2
    rows_axis = lax.axis_size("rows")
    cols_axis = lax.axis_size("cols")
    row_count = orbital_count // rows_axis
    col_count = orbital_count // cols_axis
    both = 2 * col_count
    row_start = lax.axis_index("rows") * row_count
    col_start = lax.axis_index("cols") * col_count
    core = lax.axis_index("rows") % CORES
    scale_factor = 0.125 / math.sqrt(orbital_count)

    within = lax.broadcasted_iota(jnp.int32, (blocks_dev, block_size), 1)
    live_rows = (within < atom_size[:, None]).reshape(rows_dev)
    raw_cols = lax.dynamic_slice_in_dim(coeffs, col_start, col_count, 1)
    own_cols = jnp.where(live_rows[:, None], raw_cols, jnp.zeros_like(raw_cols))
    width = reach_blocks * block_size
    up = [(i, (i + 1) % rows_axis) for i in range(rows_axis)]
    down = [((i + 1) % rows_axis, i) for i in range(rows_axis)]
    padded = jnp.concatenate(
        [
            lax.ppermute(own_cols[rows_dev - width :], "rows", up),
            own_cols,
            lax.ppermute(own_cols[:width], "rows", down),
        ],
        axis=0,
    )
    masked = jnp.where(live_rows[:, None], coeffs, jnp.zeros_like(coeffs))
    turned = masked.T.reshape(XS, ZS, CORES, row_count, rows_dev)

    def turned_half(which):
        return lax.dynamic_index_in_dim(turned, which, 2, keepdims=False).reshape(-1, rows_dev)

    own_turned = turned_half(core)
    far_turned = other_core(turned_half(1 - core))
    stacked = jnp.stack(
        [
            padded[offset * block_size : (offset + blocks_dev) * block_size].reshape(
                blocks_dev, block_size, col_count
            )
            for offset in range(span_blocks)
        ],
        axis=1,
    )
    gated = phase_ops * block_links[None, :, :, None, None].astype(bf16)
    applied = jnp.einsum("pbtij,btjk->bipk", gated, stacked, preferred_element_type=f32)
    applied = applied.reshape(rows_dev, both).astype(bf16)
    far_applied = other_core(applied)

    product = small_product(own_turned, applied) + small_product(far_turned, far_applied)

    def diag_of(cols, values):
        return jnp.sum(jnp.tile(cols, (1, 2)).astype(f32) * values.astype(f32), axis=0)

    far_cols = jnp.where(core == 0, padded[width + rows_dev :], padded[:width])
    diag = diag_of(own_cols, applied) + diag_of(far_cols, far_applied)

    def with_diag(cells, values):
        high = lax.reduce_precision(values, 8, 7)
        tail = jnp.stack([high, values - high]).astype(bf16)
        tail = jnp.pad(tail, ((0, 6), (0, 0)))
        tail = jnp.broadcast_to(tail, cells.shape[:-2] + tail.shape)
        return jnp.concatenate([cells.astype(bf16), tail], axis=-2)

    def summed(cells):
        body, tail = cells[:, :-8].astype(f32), cells[:, -8:-6].astype(f32)
        return jnp.sum(body, axis=0), jnp.sum(tail, axis=(0, 1))

    pieces = with_diag(product.reshape(XS, ZS * row_count, both), diag)
    chip, diag = summed(swap(pieces, "rows", x_groups))
    pieces = with_diag(chip.reshape(ZS, row_count, both), diag)
    z_block, diag = summed(swap(pieces, "rows", z_groups))
    z_half = z_block.astype(bf16)

    high = lax.reduce_precision(diag, 8, 7)
    terms = jnp.stack([high, diag - high]).astype(bf16).reshape(-1, 128)
    terms = jnp.pad(terms, ((0, row_count - terms.shape[0]), (0, 0)))
    packed = jnp.concatenate([z_half, rotation.astype(bf16), terms], axis=1)
    across = spread(packed, cols_axis, "cols")

    def rows_of(cells):
        return cells.transpose(1, 0, 2).reshape(cells.shape[1], -1)

    z_rows = [rows_of(across[:, :, p * col_count : (p + 1) * col_count]) for p in range(2)]
    rot_rows = rows_of(across[:, :, both : both + col_count])
    terms = across[:, : 2 * both // 128, both + col_count :].astype(f32)
    terms = terms.reshape(cols_axis, 2, 2, col_count)
    diag_all = jnp.sum(terms, axis=1).transpose(1, 0, 2).reshape(2, -1)

    def halves(cells):
        away = other_core(cells)
        pair = jnp.where(core == 0, jnp.stack([cells, away], 1), jnp.stack([away, cells], 1))
        return pair.reshape(orbital_count, -1)

    panel = spread(z_half, ZS, "rows", z_groups)
    panel = spread(panel, XS, "rows", x_groups)
    panel, diag_all = lax.optimization_barrier((panel, diag_all))
    z_cols = halves(panel.reshape(XS * ZS, row_count, both))

    diag_cols = lax.dynamic_slice_in_dim(diag_all, col_start, col_count, 1)
    diag_down = lax.dynamic_slice_in_dim(diag_all, row_start, row_count, 1)

    def generator(cos_block, sin_block, across_diag, down_diag):
        cos_part = cos_block.astype(f32) * (across_diag[0][None, :] - down_diag[0][:, None])
        sin_part = sin_block.astype(f32) * (across_diag[1][None, :] - down_diag[1][:, None])
        return (cos_part + sin_part) * scale_factor

    gen_cols = generator(z_cols[:, :col_count], z_cols[:, col_count:], diag_cols, diag_all)
    gen_cols = gen_cols.astype(bf16)
    gen_rows = generator(z_rows[0], z_rows[1], diag_all, diag_down)
    gen_block = generator(z_block[:, :col_count], z_block[:, col_count:], diag_cols, diag_down)

    square = small_product(gen_rows.astype(bf16), gen_cols)
    step = (gen_block + 0.5 * square).astype(bf16)
    step_cols = spread(step, XS * ZS, "rows", xz_groups)
    square_rows = rows_of(spread(square.astype(bf16), cols_axis, "cols"))
    back_rows = (0.5 * square_rows.astype(f32) - gen_rows).astype(bf16)
    half_block = z_block + small_product(back_rows, z_cols)
    step_cols = halves(step_cols)
    half_across = spread(half_block.astype(bf16), cols_axis, "cols")
    half_rows = [
        rows_of(half_across[:, :, p * col_count : (p + 1) * col_count]) for p in range(2)
    ]
    rotated = rotation + small_product(rot_rows, step_cols)
    orbitals = (own_cols.astype(f32) + small_product(masked, step_cols)).astype(bf16)
    phase_cos = half_block[:, :col_count] + small_product(half_rows[0], step_cols)
    phase_sin = half_block[:, col_count:] + small_product(half_rows[1], step_cols)
    return (rotated, phase_cos, phase_sin, orbitals)


def solution(mesh):
    placed = (
        P("rows", None),
        P("rows", "cols"),
        P(None, "rows", None, None, None),
        P("rows", None),
        P("rows"),
    )
    return jax.shard_map(
        on_device,
        mesh=mesh,
        in_specs=placed,
        out_specs=(P("rows", "cols"), P("rows", "cols"), P("rows", "cols"), P("rows", "cols")),
        check_vma=False,
    )
```

```python
import math

import jax
import jax.numpy as jnp
from jax import lax
from jax.experimental import pallas as pl
from jax.experimental.pallas import tpu as pltpu
from jax.sharding import PartitionSpec as P

bf16 = jnp.bfloat16
f32 = jnp.float32

XS, ZS, CORES = 4, 8, 2


def row_index(x, z, core):
    return (x * ZS + z) * CORES + core


z_groups = [[row_index(x, z, k) for z in range(ZS)] for x in range(XS) for k in range(CORES)]
xz_groups = [
    [row_index(x, z, k) for x in range(XS) for z in range(ZS)] for k in range(CORES)
]


def swap(cells, axis, groups=None):
    return lax.all_to_all(cells, axis, 0, 0, tiled=True, axis_index_groups=groups)


def spread(cells, count, axis, groups=None):
    return swap(jnp.broadcast_to(cells[None], (count,) + cells.shape), axis, groups)


def other_core(cells):
    count = lax.axis_size("rows")
    return lax.ppermute(cells, "rows", [(i, i ^ 1) for i in range(count)])


def along_x(cells, steps):
    line, count = ZS * CORES, lax.axis_size("rows")
    return lax.ppermute(cells, "rows", [(i, (i + steps * line) % count) for i in range(count)])


def ordered_kernel(place_ref, *refs):
    own_refs, away_ref, out_ref = refs[:XS], refs[XS], refs[XS + 1]
    x, core = place_ref[0], place_ref[1]
    for steps in range(XS):
        source = lax.rem(x + XS - steps, XS)
        out_ref[source, :, core] = own_refs[steps][...]
        out_ref[source, :, 1 - core] = away_ref[steps]


def ordered(place, own, away):
    vmem = pl.BlockSpec(memory_space=pltpu.VMEM)
    shape = (XS, ZS, CORES) + own[0].shape[1:]
    return pl.pallas_call(
        ordered_kernel,
        out_shape=jax.ShapeDtypeStruct(shape, own[0].dtype),
        in_specs=[pl.BlockSpec(memory_space=pltpu.SMEM)] + [vmem] * (XS + 1),
        out_specs=vmem,
        compiler_params=pltpu.CompilerParams(vmem_limit_bytes=24 * 2**20),
    )(place, *own, away)


def small_product(left, right):
    return jnp.dot(left, right, preferred_element_type=f32)


def on_device(coeffs, rotation, phase_ops, block_links, atom_size):
    rows_dev, orbital_count = coeffs.shape
    blocks_dev = phase_ops.shape[1]
    span_blocks = phase_ops.shape[2]
    block_size = phase_ops.shape[3]
    reach_blocks = (span_blocks - 1) // 2
    rows_axis = lax.axis_size("rows")
    cols_axis = lax.axis_size("cols")
    row_count = orbital_count // rows_axis
    col_count = orbital_count // cols_axis
    both = 2 * col_count
    row_start = lax.axis_index("rows") * row_count
    col_start = lax.axis_index("cols") * col_count
    core = lax.axis_index("rows") % CORES
    own_x = lax.axis_index("rows") // (ZS * CORES)
    place = jnp.stack([own_x, core]).astype(jnp.int32)
    scale_factor = 0.125 / math.sqrt(orbital_count)

    within = lax.broadcasted_iota(jnp.int32, (blocks_dev, block_size), 1)
    live_rows = (within < atom_size[:, None]).reshape(rows_dev)
    raw_cols = lax.dynamic_slice_in_dim(coeffs, col_start, col_count, 1)
    own_cols = jnp.where(live_rows[:, None], raw_cols, jnp.zeros_like(raw_cols))
    width = reach_blocks * block_size
    up = [(i, (i + 1) % rows_axis) for i in range(rows_axis)]
    down = [((i + 1) % rows_axis, i) for i in range(rows_axis)]
    padded = jnp.concatenate(
        [
            lax.ppermute(own_cols[rows_dev - width :], "rows", up),
            own_cols,
            lax.ppermute(own_cols[:width], "rows", down),
        ],
        axis=0,
    )
    masked = jnp.where(live_rows[:, None], coeffs, jnp.zeros_like(coeffs))
    turned = masked.T.reshape(XS, ZS, CORES, row_count, rows_dev)

    def turned_half(which):
        return lax.dynamic_index_in_dim(turned, which, 2, keepdims=False).reshape(-1, rows_dev)

    own_turned = turned_half(core)
    far_turned = other_core(turned_half(1 - core))
    stacked = jnp.stack(
        [
            padded[offset * block_size : (offset + blocks_dev) * block_size].reshape(
                blocks_dev, block_size, col_count
            )
            for offset in range(span_blocks)
        ],
        axis=1,
    )
    gated = phase_ops * block_links[None, :, :, None, None].astype(bf16)
    applied = jnp.einsum("pbtij,btjk->bipk", gated, stacked, preferred_element_type=f32)
    applied = applied.reshape(rows_dev, both).astype(bf16)
    far_applied = other_core(applied)

    def diag_of(cols, values):
        return jnp.sum(jnp.tile(cols, (1, 2)).astype(f32) * values.astype(f32), axis=0)

    far_cols = jnp.where(core == 0, padded[width + rows_dev :], padded[:width])
    diag = diag_of(own_cols, applied) + diag_of(far_cols, far_applied)

    def with_diag(cells, values):
        high = lax.reduce_precision(values, 8, 7)
        tail = jnp.stack([high, values - high]).astype(bf16)
        tail = jnp.pad(tail, ((0, 6), (0, 0)))
        tail = jnp.broadcast_to(tail, cells.shape[:-2] + tail.shape)
        return jnp.concatenate([cells.astype(bf16), tail], axis=-2)

    def summed(cells):
        body, tail = cells[:, :-8].astype(f32), cells[:, -8:-6].astype(f32)
        return jnp.sum(body, axis=0), jnp.sum(tail, axis=(0, 1))

    def product(steps):
        start = ((own_x + steps) % XS) * (ZS * row_count)
        own_part = lax.dynamic_slice_in_dim(own_turned, start, ZS * row_count, 0)
        far_part = lax.dynamic_slice_in_dim(far_turned, start, ZS * row_count, 0)
        return small_product(own_part, applied) + small_product(far_part, far_applied)

    got = [along_x(with_diag(product(steps), diag), steps) for steps in (1, 3, 2)]
    chip, diag_rest = summed(jnp.stack(got))
    chip, diag = chip + product(0), diag + diag_rest
    pieces = with_diag(chip.reshape(ZS, row_count, both), diag)
    z_block, diag = summed(swap(pieces, "rows", z_groups))
    z_half = z_block.astype(bf16)

    panel = spread(z_half, ZS, "rows", z_groups)

    high = lax.reduce_precision(diag, 8, 7)
    terms = jnp.stack([high, diag - high]).astype(bf16).reshape(-1, 128)
    terms = jnp.pad(terms, ((0, row_count - terms.shape[0]), (0, 0)))
    packed = jnp.concatenate([z_half, rotation.astype(bf16), terms], axis=1)
    packed, panel = lax.optimization_barrier((packed, panel))
    panels = [panel] + [along_x(panel, steps) for steps in (1, 2, 3)]
    across = spread(packed, cols_axis, "cols")

    def rows_of(cells):
        return cells.transpose(1, 0, 2).reshape(cells.shape[1], -1)

    z_rows = [rows_of(across[:, :, p * col_count : (p + 1) * col_count]) for p in range(2)]
    rot_rows = rows_of(across[:, :, both : both + col_count])
    terms = across[:, : 2 * both // 128, both + col_count :].astype(f32)
    terms = terms.reshape(cols_axis, 2, 2, col_count)
    diag_all = jnp.sum(terms, axis=1).transpose(1, 0, 2).reshape(2, -1)

    z_cols = ordered(place, panels, other_core(jnp.stack(panels)))
    z_cols = z_cols.reshape(orbital_count, both)

    diag_cols = lax.dynamic_slice_in_dim(diag_all, col_start, col_count, 1)
    diag_down = lax.dynamic_slice_in_dim(diag_all, row_start, row_count, 1)

    def generator(cos_block, sin_block, across_diag, down_diag):
        cos_part = cos_block.astype(f32) * (across_diag[0][None, :] - down_diag[0][:, None])
        sin_part = sin_block.astype(f32) * (across_diag[1][None, :] - down_diag[1][:, None])
        return (cos_part + sin_part) * scale_factor

    gen_cols = generator(z_cols[:, :col_count], z_cols[:, col_count:], diag_cols, diag_all)
    gen_cols = gen_cols.astype(bf16)
    gen_rows = generator(z_rows[0], z_rows[1], diag_all, diag_down)
    gen_block = generator(z_block[:, :col_count], z_block[:, col_count:], diag_cols, diag_down)

    square = small_product(gen_rows.astype(bf16), gen_cols)
    step = (gen_block + 0.5 * square).astype(bf16)
    step_cols = spread(step, XS * ZS, "rows", xz_groups)
    square_rows = rows_of(spread(square.astype(bf16), cols_axis, "cols"))
    back_rows = (0.5 * square_rows.astype(f32) - gen_rows).astype(bf16)
    half_block = z_block + small_product(back_rows, z_cols)
    step_away = other_core(step_cols)
    step_cols = jnp.where(
        core == 0, jnp.stack([step_cols, step_away], 1), jnp.stack([step_away, step_cols], 1)
    ).reshape(orbital_count, col_count)
    half_across = spread(half_block.astype(bf16), cols_axis, "cols")
    half_rows = [
        rows_of(half_across[:, :, p * col_count : (p + 1) * col_count]) for p in range(2)
    ]
    rotated = rotation + small_product(rot_rows, step_cols)
    orbitals = (own_cols.astype(f32) + small_product(masked, step_cols)).astype(bf16)
    phase_cos = half_block[:, :col_count] + small_product(half_rows[0], step_cols)
    phase_sin = half_block[:, col_count:] + small_product(half_rows[1], step_cols)
    return (rotated, phase_cos, phase_sin, orbitals)


def solution(mesh):
    placed = (
        P("rows", None),
        P("rows", "cols"),
        P(None, "rows", None, None, None),
        P("rows", None),
        P("rows"),
    )
    return jax.shard_map(
        on_device,
        mesh=mesh,
        in_specs=placed,
        out_specs=(P("rows", "cols"), P("rows", "cols"), P("rows", "cols"), P("rows", "cols")),
        check_vma=False,
    )
```

```python
import functools
import math

import jax
import jax.numpy as jnp
from jax import lax
from jax.experimental import pallas as pl
from jax.experimental.pallas import tpu as pltpu
from jax.sharding import PartitionSpec as P

bf16 = jnp.bfloat16
f32 = jnp.float32

XS, ZS, CORES, COLS = 4, 8, 2, 8


def row_index(x, z, core):
    return (x * ZS + z) * CORES + core


z_groups = [[row_index(x, z, k) for z in range(ZS)] for x in range(XS) for k in range(CORES)]


def swap(cells, axis, groups=None):
    return lax.all_to_all(cells, axis, 0, 0, tiled=True, axis_index_groups=groups)


def other_core(cells):
    count = lax.axis_size("rows")
    return lax.ppermute(cells, "rows", [(i, i ^ 1) for i in range(count)])


def along_x(cells, steps):
    line, count = ZS * CORES, lax.axis_size("rows")
    return lax.ppermute(cells, "rows", [(i, (i + steps * line) % count) for i in range(count)])


def small_product(left, right):
    return jnp.dot(left, right, preferred_element_type=f32)


vmem = pl.BlockSpec(memory_space=pltpu.VMEM)
smem = pl.BlockSpec(memory_space=pltpu.SMEM)
anywhere = pl.BlockSpec(memory_space=pl.ANY)
params = pltpu.CompilerParams(vmem_limit_bytes=32 * 2**20)


def gathered(place_ref, own_refs, away_ref, out_ref, sems):
    x, core = place_ref[0], place_ref[1]
    copies = []
    for steps in range(XS):
        source = lax.rem(x + XS - steps, XS)
        copies.append((own_refs[steps], out_ref.at[source, :, core]))
        copies.append((away_ref.at[steps], out_ref.at[source, :, 1 - core]))
    copies = [pltpu.make_async_copy(*pair, sems.at[i]) for i, pair in enumerate(copies)]
    for copy in copies:
        copy.start()
    return copies


def chunk(panel_ref, k):
    per = ZS * XS // COLS
    cells = panel_ref[k * per // ZS, pl.ds(k * per % ZS, per)]
    return cells.reshape(-1, cells.shape[-1])


def sum_kernel(got_ref, rotation_ref, block_ref, z_ref, packed_ref):
    count, _, wide = z_ref.shape
    total = got_ref[0].astype(f32)
    for i in range(1, count):
        total = total + got_ref[i].astype(f32)
    block = total[:, :wide]
    block_ref[...] = block
    half = block.astype(bf16)
    diag = total[:4, wide:] + total[4:8, wide:]
    high = diag.astype(bf16).astype(f32)
    fill = jnp.zeros((block.shape[0] - 8, 128), f32)
    tail = jnp.concatenate([high, diag - high, fill], axis=0).astype(bf16)
    packed = jnp.concatenate([half, rotation_ref[...].astype(bf16), tail], axis=1)
    for i in range(count):
        z_ref[i] = half
        packed_ref[i] = packed


def square_kernel(
    scale, place_ref, across_ref, own0, own1, own2, own3, away_ref,
    z_ref, rows_ref, square_ref, step_ref, diag_ref, turned_ref, sems,
):
    copies = gathered(place_ref, (own0, own1, own2, own3), away_ref, z_ref, sems)
    mine, low, col = place_ref[2], place_ref[3], place_ref[4]
    rows, width = rows_ref.shape[1:]
    for p in range(2):
        parts = []
        for h in range(width // 128):
            terms = across_ref[:, :, -128:].astype(f32)
            k = p * (width // 128) + h
            parts.append(terms[:, k] + terms[:, 4 + k])
        diag_ref[p] = jnp.concatenate(parts, axis=1)
        turned_ref[p] = diag_ref[p].T
    lane = lax.broadcasted_iota(jnp.int32, (rows, COLS), 1)
    down = [
        jnp.sum(
            jnp.where(lane == mine, turned_ref[p, pl.ds(low, rows), :], 0.0),
            axis=1,
            keepdims=True,
        )
        for p in range(2)
    ]
    for k in range(COLS):
        cells = across_ref[k].astype(f32)
        cos_part = cells[:, :width] * (diag_ref[0, k : k + 1, :] - down[0])
        sin_part = cells[:, width : 2 * width] * (diag_ref[1, k : k + 1, :] - down[1])
        rows_ref[k] = (cos_part + sin_part) * scale
    across_diag = [diag_ref[p, pl.ds(col, 1), :] for p in range(2)]
    for copy in copies:
        copy.wait()
    square = jnp.zeros((rows, width), f32)
    for k in range(COLS):
        cells = chunk(z_ref, k).astype(f32)
        cos_part = cells[:, :width] * (across_diag[0] - turned_ref[0, :, k : k + 1])
        sin_part = cells[:, width:] * (across_diag[1] - turned_ref[1, :, k : k + 1])
        cells = ((cos_part + sin_part) * scale).astype(bf16)
        square = square + small_product(rows_ref[k].astype(bf16), cells)
    step = (rows_ref[col] + 0.5 * square).astype(bf16)
    square = square.astype(bf16)
    for k in range(COLS):
        square_ref[k] = square
        step_ref[k] = step


def half_kernel(square_ref, rows_ref, z_ref, block_ref, half_ref, sent_ref):
    total = block_ref[...]
    for k in range(COLS):
        back = (0.5 * square_ref[k].astype(f32) - rows_ref[k]).astype(bf16)
        total = total + small_product(back, chunk(z_ref, k))
    half_ref[...] = total
    sent = total.astype(bf16)
    for k in range(COLS):
        sent_ref[k] = sent


def final_kernel(
    place_ref, size_ref, half_ref, across_ref, coeffs_ref, rotation_ref, block_ref,
    own0, own1, own2, own3, away_ref,
    rotated_ref, cos_ref, sin_ref, orbitals_ref, step_ref, sems,
):
    copies = gathered(place_ref, (own0, own1, own2, own3), away_ref, step_ref, sems)
    col = place_ref[4]
    width = rotated_ref.shape[1]
    rotated = rotation_ref[...]
    cos_part, sin_part = block_ref[:, :width], block_ref[:, width:]
    start = pl.multiple_of(col * width, width)
    orbitals = coeffs_ref[:, pl.ds(start, width)].astype(f32)
    for copy in copies:
        copy.wait()
    for k in range(COLS):
        step = chunk(step_ref, k)
        cells = half_ref[k]
        cos_part = cos_part + small_product(cells[:, :width], step)
        sin_part = sin_part + small_product(cells[:, width:], step)
        rotated = rotated + small_product(across_ref[k, :, 2 * width : 3 * width], step)
        cells = coeffs_ref[:, k * width : (k + 1) * width]
        orbitals = orbitals + small_product(cells, step)
    rotated_ref[...] = rotated
    cos_ref[...] = cos_part
    sin_ref[...] = sin_part
    blocks = size_ref.shape[0]
    size = orbitals.shape[0] // blocks
    within = lax.broadcasted_iota(jnp.int32, (size, width), 0)
    for b in range(blocks):
        cells = orbitals[b * size : (b + 1) * size]
        cells = jnp.where(within < size_ref[b], cells, 0.0)
        orbitals_ref[b * size : (b + 1) * size, :] = cells.astype(bf16)


def call(kernel, shapes, in_specs, scratch, *operands):
    return pl.pallas_call(
        kernel,
        out_shape=[jax.ShapeDtypeStruct(*shape) for shape in shapes],
        in_specs=in_specs,
        out_specs=[vmem] * len(shapes),
        scratch_shapes=scratch,
        compiler_params=params,
    )(*operands)


def on_device(coeffs, rotation, phase_ops, block_links, atom_size):
    rows_dev, orbital_count = coeffs.shape
    blocks_dev = phase_ops.shape[1]
    span_blocks = phase_ops.shape[2]
    block_size = phase_ops.shape[3]
    reach_blocks = (span_blocks - 1) // 2
    rows_axis = lax.axis_size("rows")
    cols_axis = lax.axis_size("cols")
    row_count = orbital_count // rows_axis
    col_count = orbital_count // cols_axis
    both = 2 * col_count
    col_start = lax.axis_index("cols") * col_count
    core = lax.axis_index("rows") % CORES
    own_x = lax.axis_index("rows") // (ZS * CORES)
    per_col = rows_axis // cols_axis
    own_row = lax.axis_index("rows")
    place = [own_x, core, own_row // per_col, own_row % per_col * row_count]
    place = jnp.stack(place + [lax.axis_index("cols")]).astype(jnp.int32)
    scale_factor = 0.125 / math.sqrt(orbital_count)

    within = lax.broadcasted_iota(jnp.int32, (blocks_dev, block_size), 1)
    live_rows = (within < atom_size[:, None]).reshape(rows_dev)
    raw_cols = lax.dynamic_slice_in_dim(coeffs, col_start, col_count, 1)
    own_cols = jnp.where(live_rows[:, None], raw_cols, jnp.zeros_like(raw_cols))
    width = reach_blocks * block_size
    up = [(i, (i + 1) % rows_axis) for i in range(rows_axis)]
    down = [((i + 1) % rows_axis, i) for i in range(rows_axis)]
    padded = jnp.concatenate(
        [
            lax.ppermute(own_cols[rows_dev - width :], "rows", up),
            own_cols,
            lax.ppermute(own_cols[:width], "rows", down),
        ],
        axis=0,
    )
    turned = coeffs.T.reshape(XS, ZS, CORES, row_count, rows_dev)

    def turned_half(which):
        return lax.dynamic_index_in_dim(turned, which, 2, keepdims=False).reshape(-1, rows_dev)

    own_turned = turned_half(core)
    far_turned = other_core(turned_half(1 - core))
    stacked = jnp.stack(
        [
            padded[offset * block_size : (offset + blocks_dev) * block_size].reshape(
                blocks_dev, block_size, col_count
            )
            for offset in range(span_blocks)
        ],
        axis=1,
    )
    gated = phase_ops * block_links[None, :, :, None, None].astype(bf16)
    applied = jnp.einsum("pbtij,btjk->bipk", gated, stacked, preferred_element_type=f32)
    applied = jnp.where(live_rows[:, None], applied.reshape(rows_dev, both), 0.0).astype(bf16)
    far_applied = other_core(applied)

    def diag_of(cols, values):
        return jnp.sum(jnp.tile(cols, (1, 2)).astype(f32) * values.astype(f32), axis=0)

    far_cols = jnp.where(core == 0, padded[width + rows_dev :], padded[:width])
    diag = diag_of(own_cols, applied) + diag_of(far_cols, far_applied)

    def with_diag(cells, values):
        high = lax.reduce_precision(values, 8, 7)
        tail = jnp.stack([high, values - high]).astype(bf16)
        tail = jnp.pad(tail, ((0, 6), (0, 0)))
        tail = jnp.broadcast_to(tail, cells.shape[:-2] + tail.shape)
        return jnp.concatenate([cells.astype(bf16), tail], axis=-2)

    def summed(cells):
        body, tail = cells[:, :-8].astype(f32), cells[:, -8:-6].astype(f32)
        return jnp.sum(body, axis=0), jnp.sum(tail, axis=(0, 1))

    def product(steps):
        start = ((own_x + steps) % XS) * (ZS * row_count)
        own_part = lax.dynamic_slice_in_dim(own_turned, start, ZS * row_count, 0)
        far_part = lax.dynamic_slice_in_dim(far_turned, start, ZS * row_count, 0)
        return small_product(own_part, applied) + small_product(far_part, far_applied)

    got = [along_x(with_diag(product(steps), diag), steps) for steps in (1, 3, 2)]
    chip, diag_rest = summed(jnp.stack(got))
    chip, diag = chip + product(0), diag + diag_rest
    high = lax.reduce_precision(diag, 8, 7)
    terms = jnp.stack([high, diag - high]).astype(bf16).reshape(-1, 128)
    terms = jnp.pad(terms, ((0, row_count - terms.shape[0]), (0, 0)))
    terms = jnp.broadcast_to(terms[None], (ZS, row_count, 128))
    pieces = chip.astype(bf16).reshape(ZS, row_count, both)
    got = swap(jnp.concatenate([pieces, terms], axis=2), "rows", z_groups)
    z_block, z_sent, packed = call(
        sum_kernel,
        [
            ((row_count, both), f32),
            ((ZS, row_count, both), bf16),
            ((COLS, row_count, both + col_count + 128), bf16),
        ],
        [vmem] * 2,
        [],
        got,
        rotation,
    )

    panel = swap(z_sent, "rows", z_groups)
    packed, panel = lax.optimization_barrier((packed, panel))
    panels = [panel] + [along_x(panel, steps) for steps in (1, 2, 3)]
    across = swap(packed, "cols")
    away = other_core(jnp.stack(panels))
    block = (row_count, col_count)
    z_cols, gen_rows, square, step = call(
        functools.partial(square_kernel, scale_factor),
        [
            ((XS, ZS, CORES, row_count, both), bf16),
            ((COLS,) + block, f32),
            ((COLS,) + block, bf16),
            ((ZS,) + block, bf16),
        ],
        [smem, vmem] + [anywhere] * (XS + 1),
        [
            pltpu.VMEM((2, COLS, col_count), f32),
            pltpu.VMEM((2, col_count, COLS), f32),
            pltpu.SemaphoreType.DMA((2 * XS,)),
        ],
        place,
        across,
        *panels,
        away,
    )

    step = swap(step, "rows", z_groups)
    square, step = lax.optimization_barrier((square, step))
    steps_x = [step] + [along_x(step, steps) for steps in (1, 2, 3)]
    square = swap(square, "cols")
    half_block, half_sent = call(
        half_kernel,
        [((row_count, both), f32), ((COLS, row_count, both), bf16)],
        [vmem] * 4,
        [],
        square,
        gen_rows,
        z_cols,
        z_block,
    )
    step_away = other_core(jnp.stack(steps_x))
    half_rows = swap(half_sent, "cols")
    return tuple(
        call(
            final_kernel,
            [(block, f32)] * 3 + [((rows_dev, col_count), bf16)],
            [smem] * 2 + [vmem] * 5 + [anywhere] * (XS + 1),
            [
                pltpu.VMEM((XS, ZS, CORES, row_count, col_count), bf16),
                pltpu.SemaphoreType.DMA((2 * XS,)),
            ],
            place,
            atom_size,
            half_rows,
            across,
            coeffs,
            rotation,
            half_block,
            *steps_x,
            step_away,
        )
    )


def solution(mesh):
    placed = (
        P("rows", None),
        P("rows", "cols"),
        P(None, "rows", None, None, None),
        P("rows", None),
        P("rows"),
    )
    return jax.shard_map(
        on_device,
        mesh=mesh,
        in_specs=placed,
        out_specs=(P("rows", "cols"), P("rows", "cols"), P("rows", "cols"), P("rows", "cols")),
        check_vma=False,
    )
```

```python
import functools
import math

import jax
import jax.numpy as jnp
from jax import lax
from jax.experimental import pallas as pl
from jax.experimental.pallas import tpu as pltpu
from jax.sharding import PartitionSpec as P

bf16 = jnp.bfloat16
f32 = jnp.float32

XS, ZS, CORES, COLS = 4, 8, 2, 8


def row_index(x, z, core):
    return (x * ZS + z) * CORES + core


z_groups = [[row_index(x, z, k) for z in range(ZS)] for x in range(XS) for k in range(CORES)]


def swap(cells, axis, groups=None):
    return lax.all_to_all(cells, axis, 0, 0, tiled=True, axis_index_groups=groups)


def other_core(cells):
    count = lax.axis_size("rows")
    return lax.ppermute(cells, "rows", [(i, i ^ 1) for i in range(count)])


def along_x(cells, steps):
    line, count = ZS * CORES, lax.axis_size("rows")
    return lax.ppermute(cells, "rows", [(i, (i + steps * line) % count) for i in range(count)])


def small_product(left, right):
    return jnp.dot(left, right, preferred_element_type=f32)


vmem = pl.BlockSpec(memory_space=pltpu.VMEM)
smem = pl.BlockSpec(memory_space=pltpu.SMEM)
anywhere = pl.BlockSpec(memory_space=pl.ANY)


def call(kernel, shapes, in_specs, scratch, *operands, bytes_accessed=2**20):
    return pl.pallas_call(
        kernel,
        out_shape=[jax.ShapeDtypeStruct(*shape) for shape in shapes],
        in_specs=in_specs,
        out_specs=[vmem] * len(shapes),
        scratch_shapes=scratch,
        compiler_params=pltpu.CompilerParams(vmem_limit_bytes=12 * 2**20),
        cost_estimate=pl.CostEstimate(
            flops=0, bytes_accessed=bytes_accessed, transcendentals=0
        ),
    )(*operands)


def within_rows(size_ref, cells):
    blocks = size_ref.shape[0]
    size = cells.shape[0] // blocks
    within = lax.broadcasted_iota(jnp.int32, (size, cells.shape[1]), 0)
    parts = [
        jnp.where(within < size_ref[b], cells[b * size : (b + 1) * size], 0.0)
        for b in range(blocks)
    ]
    return jnp.concatenate(parts, axis=0)


def mask_kernel(place_ref, size_ref, coeffs_ref, cols_ref, slice_ref, sem):
    width = cols_ref.shape[1]
    start = pl.multiple_of(place_ref[4] * width, width)
    copy = pltpu.make_async_copy(coeffs_ref.at[:, pl.ds(start, width)], slice_ref, sem)
    copy.start()
    copy.wait()
    cols_ref[...] = within_rows(size_ref, slice_ref[...].astype(f32)).astype(bf16)


def applied_kernel(size_ref, links_ref, up_ref, cols_ref, down_ref, ops_ref, out_ref, diag_ref):
    phases, blocks, span, size, _ = ops_ref.shape
    width = cols_ref.shape[1]
    padded = jnp.concatenate([up_ref[...], cols_ref[...], down_ref[...]], axis=0)
    first = up_ref.shape[0] - (span - 1) // 2 * size
    own = cols_ref[...].astype(f32)
    for p in range(phases):
        parts = []
        for b in range(blocks):
            gated = [
                ops_ref[p, b, t] * links_ref[b, t].astype(f32).astype(bf16) for t in range(span)
            ]
            start = first + b * size
            near = padded[start : start + span * size]
            parts.append(small_product(jnp.concatenate(gated, axis=1), near))
        total = within_rows(size_ref, jnp.concatenate(parts, axis=0)).astype(bf16)
        out_ref[:, p * width : (p + 1) * width] = total
        sums = jnp.sum(total.astype(f32) * own, axis=0, keepdims=True)
        diag_ref[:, p * width : (p + 1) * width] = sums


def sum_kernel(got_ref, rotation_ref, block_ref, z_ref, packed_ref):
    count, _, wide = z_ref.shape
    total = got_ref[0].astype(f32)
    for i in range(1, count):
        total = total + got_ref[i].astype(f32)
    block = total[:, :wide]
    block_ref[...] = block
    half = block.astype(bf16)
    diag = total[:4, wide:] + total[4:8, wide:]
    high = diag.astype(bf16).astype(f32)
    fill = jnp.zeros((block.shape[0] - 8, 128), f32)
    tail = jnp.concatenate([high, diag - high, fill], axis=0).astype(bf16)
    packed = jnp.concatenate([half, rotation_ref[...].astype(bf16), tail], axis=1)
    for i in range(count):
        z_ref[i] = half
        packed_ref[i] = packed


def gathered(place_ref, own_refs, away_ref, out_ref, sems):
    x, core = place_ref[0], place_ref[1]
    copies = []
    for steps in range(XS):
        source = lax.rem(x + XS - steps, XS)
        copies.append((own_refs[steps], out_ref.at[source, :, core]))
        copies.append((away_ref.at[steps], out_ref.at[source, :, 1 - core]))
    copies = [pltpu.make_async_copy(*pair, sems.at[i]) for i, pair in enumerate(copies)]
    for copy in copies:
        copy.start()
    return copies


def chunk(panel_ref, k):
    per = ZS * XS // COLS
    cells = panel_ref[k * per // ZS, pl.ds(k * per % ZS, per)]
    return cells.reshape(-1, cells.shape[-1])


def rows_kernel(scale, place_ref, across_ref, rows_ref, diag_ref, turned_ref):
    mine, low = place_ref[2], place_ref[3]
    rows, width = rows_ref.shape[1:]
    terms = across_ref[:, :, -128:].astype(f32)
    per = width // 128
    for p in range(2):
        parts = [terms[:, p * per + h] + terms[:, 2 * per + p * per + h] for h in range(per)]
        diag_ref[p] = jnp.concatenate(parts, axis=1)
        turned_ref[p] = diag_ref[p].T
    lane = lax.broadcasted_iota(jnp.int32, (rows, COLS), 1)
    down = [
        jnp.sum(
            jnp.where(lane == mine, turned_ref[p, pl.ds(low, rows), :], 0.0),
            axis=1,
            keepdims=True,
        )
        for p in range(2)
    ]
    for k in range(COLS):
        cells = across_ref[k].astype(f32)
        cos_part = cells[:, :width] * (diag_ref[0, k : k + 1, :] - down[0])
        sin_part = cells[:, width : 2 * width] * (diag_ref[1, k : k + 1, :] - down[1])
        rows_ref[k] = (cos_part + sin_part) * scale


def square_kernel(
    scale, place_ref, rows_ref, diag_ref, turned_ref, own0, own1, own2, own3, away_ref,
    z_ref, square_ref, step_ref, sems,
):
    copies = gathered(place_ref, (own0, own1, own2, own3), away_ref, z_ref, sems)
    col = place_ref[4]
    rows, width = rows_ref.shape[1:]
    across_diag = [diag_ref[p, pl.ds(col, 1), :] for p in range(2)]
    for copy in copies:
        copy.wait()
    square = jnp.zeros((rows, width), f32)
    for k in range(COLS):
        cells = chunk(z_ref, k).astype(f32)
        cos_part = cells[:, :width] * (across_diag[0] - turned_ref[0, :, k : k + 1])
        sin_part = cells[:, width:] * (across_diag[1] - turned_ref[1, :, k : k + 1])
        cells = ((cos_part + sin_part) * scale).astype(bf16)
        square = square + small_product(rows_ref[k].astype(bf16), cells)
    step = (rows_ref[col] + 0.5 * square).astype(bf16)
    square = square.astype(bf16)
    for k in range(COLS):
        square_ref[k] = square
        step_ref[k] = step


def half_kernel(square_ref, rows_ref, z_ref, block_ref, half_ref, sent_ref):
    total = block_ref[...]
    for k in range(COLS):
        back = (0.5 * square_ref[k].astype(f32) - rows_ref[k]).astype(bf16)
        total = total + small_product(back, chunk(z_ref, k))
    half_ref[...] = total
    sent = total.astype(bf16)
    for k in range(COLS):
        sent_ref[k] = sent


def final_kernel(
    place_ref, size_ref, half_ref, across_ref, coeffs_ref, rotation_ref, block_ref,
    own0, own1, own2, own3, away_ref,
    rotated_ref, cos_ref, sin_ref, orbitals_ref, step_ref, sems,
):
    copies = gathered(place_ref, (own0, own1, own2, own3), away_ref, step_ref, sems)
    col = place_ref[4]
    width = rotated_ref.shape[1]
    rotated = rotation_ref[...]
    cos_part, sin_part = block_ref[:, :width], block_ref[:, width:]
    start = pl.multiple_of(col * width, width)
    orbitals = coeffs_ref[:, pl.ds(start, width)].astype(f32)
    for copy in copies:
        copy.wait()
    for k in range(COLS):
        step = chunk(step_ref, k)
        cells = half_ref[k]
        cos_part = cos_part + small_product(cells[:, :width], step)
        sin_part = sin_part + small_product(cells[:, width:], step)
        rotated = rotated + small_product(across_ref[k, :, 2 * width : 3 * width], step)
        cells = coeffs_ref[:, k * width : (k + 1) * width]
        orbitals = orbitals + small_product(cells, step)
    rotated_ref[...] = rotated
    cos_ref[...] = cos_part
    sin_ref[...] = sin_part
    orbitals_ref[...] = within_rows(size_ref, orbitals).astype(bf16)


def on_device(coeffs, rotation, phase_ops, block_links, atom_size):
    rows_dev, orbital_count = coeffs.shape
    span_blocks, block_size = phase_ops.shape[2:4]
    reach_blocks = (span_blocks - 1) // 2
    rows_axis = lax.axis_size("rows")
    cols_axis = lax.axis_size("cols")
    row_count = orbital_count // rows_axis
    col_count = orbital_count // cols_axis
    both = 2 * col_count
    core = lax.axis_index("rows") % CORES
    own_x = lax.axis_index("rows") // (ZS * CORES)
    per_col = rows_axis // cols_axis
    own_row = lax.axis_index("rows")
    place = [own_x, core, own_row // per_col, own_row % per_col * row_count]
    place = jnp.stack(place + [lax.axis_index("cols")]).astype(jnp.int32)
    scale_factor = 0.125 / math.sqrt(orbital_count)

    (own_cols,) = call(
        mask_kernel,
        [((rows_dev, col_count), bf16)],
        [smem] * 2 + [anywhere],
        [pltpu.VMEM((rows_dev, col_count), bf16), pltpu.SemaphoreType.DMA],
        place,
        atom_size,
        coeffs,
    )
    width = reach_blocks * block_size
    up = [(i, (i + 1) % rows_axis) for i in range(rows_axis)]
    down = [((i + 1) % rows_axis, i) for i in range(rows_axis)]
    from_up = lax.ppermute(own_cols[rows_dev - width :], "rows", up)
    from_down = lax.ppermute(own_cols[:width], "rows", down)
    turned = coeffs.T.reshape(XS, ZS, CORES, row_count, rows_dev)

    def turned_half(which):
        return lax.dynamic_index_in_dim(turned, which, 2, keepdims=False).reshape(-1, rows_dev)

    own_turned = turned_half(core)
    far_turned = other_core(turned_half(1 - core))
    applied, own_diag = call(
        applied_kernel,
        [((rows_dev, both), bf16), ((1, both), f32)],
        [smem] * 2 + [vmem] * 4,
        [],
        atom_size,
        block_links,
        from_up,
        own_cols,
        from_down,
        phase_ops,
    )
    far_applied = other_core(applied)

    far_cols = jnp.where(core == 0, from_down[:rows_dev], from_up[-rows_dev:]).astype(f32)
    far_diag = jnp.tile(far_cols, (1, 2)) * far_applied.astype(f32)
    diag = own_diag[0] + jnp.sum(far_diag, axis=0)

    def with_diag(cells, values):
        high = lax.reduce_precision(values, 8, 7)
        tail = jnp.stack([high, values - high]).astype(bf16)
        tail = jnp.pad(tail, ((0, 6), (0, 0)))
        tail = jnp.broadcast_to(tail, cells.shape[:-2] + tail.shape)
        return jnp.concatenate([cells.astype(bf16), tail], axis=-2)

    def summed(cells):
        body, tail = cells[:, :-8].astype(f32), cells[:, -8:-6].astype(f32)
        return jnp.sum(body, axis=0), jnp.sum(tail, axis=(0, 1))

    def product(steps):
        start = ((own_x + steps) % XS) * (ZS * row_count)
        own_part = lax.dynamic_slice_in_dim(own_turned, start, ZS * row_count, 0)
        far_part = lax.dynamic_slice_in_dim(far_turned, start, ZS * row_count, 0)
        return small_product(own_part, applied) + small_product(far_part, far_applied)

    got = [along_x(with_diag(product(steps), diag), steps) for steps in (1, 3, 2)]
    chip, diag_rest = summed(jnp.stack(got))
    chip, diag = chip + product(0), diag + diag_rest
    high = lax.reduce_precision(diag, 8, 7)
    terms = jnp.stack([high, diag - high]).astype(bf16).reshape(-1, 128)
    terms = jnp.pad(terms, ((0, row_count - terms.shape[0]), (0, 0)))
    terms = jnp.broadcast_to(terms[None], (ZS, row_count, 128))
    pieces = chip.astype(bf16).reshape(ZS, row_count, both)
    got = swap(jnp.concatenate([pieces, terms], axis=2), "rows", z_groups)
    z_block, z_sent, packed = call(
        sum_kernel,
        [
            ((row_count, both), f32),
            ((ZS, row_count, both), bf16),
            ((COLS, row_count, both + col_count + 128), bf16),
        ],
        [vmem] * 2,
        [],
        got,
        rotation,
    )

    panel = swap(z_sent, "rows", z_groups)
    packed, panel = lax.optimization_barrier((packed, panel))
    panels = [panel] + [along_x(panel, steps) for steps in (1, 2, 3)]
    across = swap(packed, "cols")
    stacked, across = lax.optimization_barrier((jnp.stack(panels), across))
    away = other_core(stacked)
    block = (row_count, col_count)
    gen_rows, diag_all, turned_diag = call(
        functools.partial(rows_kernel, scale_factor),
        [
            ((COLS,) + block, f32),
            ((2, COLS, col_count), f32),
            ((2, col_count, COLS), f32),
        ],
        [smem, vmem],
        [],
        place,
        across,
        bytes_accessed=2**28,
    )
    z_cols, square, step = call(
        functools.partial(square_kernel, scale_factor),
        [
            ((XS, ZS, CORES, row_count, both), bf16),
            ((COLS,) + block, bf16),
            ((ZS,) + block, bf16),
        ],
        [smem] + [vmem] * 3 + [anywhere] * (XS + 1),
        [pltpu.SemaphoreType.DMA((2 * XS,))],
        place,
        gen_rows,
        diag_all,
        turned_diag,
        *panels,
        away,
    )

    step = swap(step, "rows", z_groups)
    square, step = lax.optimization_barrier((square, step))
    steps_x = [step] + [along_x(step, steps) for steps in (1, 2, 3)]
    square = swap(square, "cols")
    half_block, half_sent = call(
        half_kernel,
        [((row_count, both), f32), ((COLS, row_count, both), bf16)],
        [vmem] * 4,
        [],
        square,
        gen_rows,
        z_cols,
        z_block,
        bytes_accessed=2**26,
    )
    *steps_x, half_sent = lax.optimization_barrier((*steps_x, half_sent))
    step_away = other_core(jnp.stack(steps_x))
    half_rows = swap(half_sent, "cols")
    return tuple(
        call(
            final_kernel,
            [(block, f32)] * 3 + [((rows_dev, col_count), bf16)],
            [smem] * 2 + [vmem] * 5 + [anywhere] * (XS + 1),
            [
                pltpu.VMEM((XS, ZS, CORES, row_count, col_count), bf16),
                pltpu.SemaphoreType.DMA((2 * XS,)),
            ],
            place,
            atom_size,
            half_rows,
            across,
            coeffs,
            rotation,
            half_block,
            *steps_x,
            step_away,
        )
    )


def solution(mesh):
    placed = (
        P("rows", None),
        P("rows", "cols"),
        P(None, "rows", None, None, None),
        P("rows", None),
        P("rows"),
    )
    return jax.shard_map(
        on_device,
        mesh=mesh,
        in_specs=placed,
        out_specs=(P("rows", "cols"), P("rows", "cols"), P("rows", "cols"), P("rows", "cols")),
        check_vma=False,
    )
```

```python
import functools
import math

import jax
import jax.numpy as jnp
from jax import lax
from jax.experimental import pallas as pl
from jax.experimental.pallas import tpu as pltpu
from jax.sharding import PartitionSpec as P

bf16 = jnp.bfloat16
f32 = jnp.float32

XS, ZS, CORES, COLS = 4, 8, 2, 8


def row_index(x, z, core):
    return (x * ZS + z) * CORES + core


z_groups = [[row_index(x, z, k) for z in range(ZS)] for x in range(XS) for k in range(CORES)]


def swap(cells, axis, groups=None):
    return lax.all_to_all(cells, axis, 0, 0, tiled=True, axis_index_groups=groups)


def other_core(cells):
    count = lax.axis_size("rows")
    return lax.ppermute(cells, "rows", [(i, i ^ 1) for i in range(count)])


def along_x(cells, steps):
    line, count = ZS * CORES, lax.axis_size("rows")
    return lax.ppermute(cells, "rows", [(i, (i + steps * line) % count) for i in range(count)])


def small_product(left, right):
    return jnp.dot(left, right, preferred_element_type=f32)


vmem = pl.BlockSpec(memory_space=pltpu.VMEM)
smem = pl.BlockSpec(memory_space=pltpu.SMEM)
hbm = pl.BlockSpec(memory_space=pltpu.HBM)


def call(kernel, shapes, in_specs, scratch, *operands, out_specs=None, bytes_accessed=2**20):
    return pl.pallas_call(
        kernel,
        out_shape=[jax.ShapeDtypeStruct(*shape) for shape in shapes],
        in_specs=in_specs,
        out_specs=out_specs or [vmem] * len(shapes),
        scratch_shapes=scratch,
        compiler_params=pltpu.CompilerParams(vmem_limit_bytes=12 * 2**20),
        cost_estimate=pl.CostEstimate(
            flops=0, bytes_accessed=bytes_accessed, transcendentals=0
        ),
    )(*operands)


def within_rows(size_ref, cells):
    blocks = size_ref.shape[0]
    size = cells.shape[0] // blocks
    within = lax.broadcasted_iota(jnp.int32, (size, cells.shape[1]), 0)
    parts = [
        jnp.where(within < size_ref[b], cells[b * size : (b + 1) * size], 0.0)
        for b in range(blocks)
    ]
    return jnp.concatenate(parts, axis=0)


def turn_kernel(size, place_ref, coeffs_ref, own_ref, far_ref):
    core = place_ref[1]
    lanes = 128
    for start in range(0, coeffs_ref.shape[1], lanes):
        cells = coeffs_ref[:, start : start + lanes].astype(f32).T
        for offset in range(0, lanes, CORES * size):
            first = cells[offset : offset + size]
            second = cells[offset + size : offset + 2 * size]
            rows = pl.ds((start + offset) // CORES, size)
            own_ref[rows, :] = jnp.where(core == 0, first, second).astype(bf16)
            far_ref[rows, :] = jnp.where(core == 0, second, first).astype(bf16)


def applied_kernel(size_ref, links_ref, up_ref, cols_ref, down_ref, ops_ref, out_ref, diag_ref):
    phases, blocks, span, size, _ = ops_ref.shape
    width = cols_ref.shape[1]
    padded = jnp.concatenate([up_ref[...], cols_ref[...], down_ref[...]], axis=0)
    first = up_ref.shape[0] - (span - 1) // 2 * size
    own = cols_ref[...].astype(f32)
    for p in range(phases):
        parts = []
        for b in range(blocks):
            gated = [
                ops_ref[p, b, t] * links_ref[b, t].astype(f32).astype(bf16) for t in range(span)
            ]
            start = first + b * size
            near = padded[start : start + span * size]
            parts.append(small_product(jnp.concatenate(gated, axis=1), near))
        total = within_rows(size_ref, jnp.concatenate(parts, axis=0)).astype(bf16)
        out_ref[:, p * width : (p + 1) * width] = total
        sums = jnp.sum(total.astype(f32) * own, axis=0, keepdims=True)
        diag_ref[:, p * width : (p + 1) * width] = sums


def product_kernel(
    place_ref, own_ref, far_ref, applied_ref, far_applied_ref, up_ref, down_ref, own_diag_ref,
    one_ref, three_ref, two_ref, none_ref, diag_ref,
):
    x, core = place_ref[0], place_ref[1]
    rows, both = none_ref.shape
    width = both // 2
    near = up_ref.shape[0] - far_applied_ref.shape[0]
    up = up_ref[near:, :].astype(f32)
    cols = jnp.where(core == 0, down_ref[: far_applied_ref.shape[0], :].astype(f32), up)
    sums = [
        jnp.sum(
            cols * far_applied_ref[:, p * width : (p + 1) * width].astype(f32),
            axis=0,
            keepdims=True,
        )
        for p in range(2)
    ]
    diag = own_diag_ref[...] + jnp.concatenate(sums, axis=1)
    diag_ref[...] = diag
    high = diag.astype(bf16).astype(f32)
    fill = jnp.zeros((two_ref.shape[0] - rows - 2, both), f32)
    tail = jnp.concatenate([high, diag - high, fill], axis=0).astype(bf16)
    for steps, out_ref in ((2, two_ref), (1, one_ref), (3, three_ref), (0, none_ref)):
        start = pl.multiple_of(lax.rem(x + steps, XS) * rows, rows)
        total = small_product(own_ref[pl.ds(start, rows), :], applied_ref[...])
        total = total + small_product(far_ref[pl.ds(start, rows), :], far_applied_ref[...])
        out_ref[:rows, :] = total.astype(out_ref.dtype)
        if steps:
            out_ref[rows:, :] = tail


def sum_kernel(got_ref, rotation_ref, block_ref, z_ref, packed_ref):
    count, _, wide = z_ref.shape
    total = got_ref[0].astype(f32)
    for i in range(1, count):
        total = total + got_ref[i].astype(f32)
    block = total[:, :wide]
    block_ref[...] = block
    half = block.astype(bf16)
    diag = total[:4, wide:] + total[4:8, wide:]
    high = diag.astype(bf16).astype(f32)
    fill = jnp.zeros((block.shape[0] - 8, 128), f32)
    tail = jnp.concatenate([high, diag - high, fill], axis=0).astype(bf16)
    packed = jnp.concatenate([half, rotation_ref[...].astype(bf16), tail], axis=1)
    for i in range(count):
        z_ref[i] = half
        packed_ref[i] = packed


def gathered(place_ref, own_ref, away_ref, out_ref, sems):
    x, core = place_ref[0], place_ref[1]
    copies = []
    for source in range(XS):
        steps = lax.rem(x + XS - source, XS)
        pairs = ((own_ref, core), (away_ref, 1 - core))
        copies.append(
            [
                pltpu.make_async_copy(
                    ref.at[steps], out_ref.at[source, :, which], sems.at[source, i]
                )
                for i, (ref, which) in enumerate(pairs)
            ]
        )
    for pair in copies:
        for copy in pair:
            copy.start()
    return copies


def landed(copies, k):
    if k * XS % COLS == 0:
        for copy in copies[k * XS // COLS]:
            copy.wait()


def chunk(panel_ref, k):
    per = ZS * XS // COLS
    cells = panel_ref[k * per // ZS, pl.ds(k * per % ZS, per)]
    return cells.reshape(-1, cells.shape[-1])


def rows_kernel(scale, place_ref, across_ref, rows_ref, diag_ref, turned_ref):
    mine, low = place_ref[2], place_ref[3]
    rows, width = rows_ref.shape[1:]
    terms = across_ref[:, :, -128:].astype(f32)
    per = width // 128
    for p in range(2):
        parts = [terms[:, p * per + h] + terms[:, 2 * per + p * per + h] for h in range(per)]
        diag_ref[p] = jnp.concatenate(parts, axis=1)
        turned_ref[p] = diag_ref[p].T
    lane = lax.broadcasted_iota(jnp.int32, (rows, COLS), 1)
    down = [
        jnp.sum(
            jnp.where(lane == mine, turned_ref[p, pl.ds(low, rows), :], 0.0),
            axis=1,
            keepdims=True,
        )
        for p in range(2)
    ]
    for k in range(COLS):
        cells = across_ref[k].astype(f32)
        cos_part = cells[:, :width] * (diag_ref[0, k : k + 1, :] - down[0])
        sin_part = cells[:, width : 2 * width] * (diag_ref[1, k : k + 1, :] - down[1])
        rows_ref[k] = (cos_part + sin_part) * scale


def square_kernel(
    scale, place_ref, rows_ref, diag_ref, turned_ref, own_ref, away_ref,
    kept_ref, square_ref, step_ref, z_ref, sems, kept_sems,
):
    copies = gathered(place_ref, own_ref, away_ref, z_ref, sems)
    kept = [
        pltpu.make_async_copy(z_ref.at[x], kept_ref.at[x], kept_sems.at[x]) for x in range(XS)
    ]
    col = place_ref[4]
    rows, width = rows_ref.shape[1:]
    across_diag = [diag_ref[p, pl.ds(col, 1), :] for p in range(2)]
    square = jnp.zeros((rows, width), f32)
    for k in range(COLS):
        landed(copies, k)
        if k * XS % COLS == 0:
            kept[k * XS // COLS].start()
        cells = chunk(z_ref, k).astype(f32)
        cos_part = cells[:, :width] * (across_diag[0] - turned_ref[0, :, k : k + 1])
        sin_part = cells[:, width:] * (across_diag[1] - turned_ref[1, :, k : k + 1])
        cells = ((cos_part + sin_part) * scale).astype(bf16)
        square = square + small_product(rows_ref[k].astype(bf16), cells)
    step = (rows_ref[col] + 0.5 * square).astype(bf16)
    square = square.astype(bf16)
    for k in range(COLS):
        square_ref[k] = square
        step_ref[k] = step
    for copy in kept:
        copy.wait()


def half_kernel(square_ref, rows_ref, kept_ref, block_ref, half_ref, sent_ref, z_ref, sems):
    copies = [[pltpu.make_async_copy(kept_ref.at[x], z_ref.at[x], sems.at[x])] for x in range(XS)]
    for copy, in copies:
        copy.start()
    total = block_ref[...]
    for k in range(COLS):
        landed(copies, k)
        back = (0.5 * square_ref[k].astype(f32) - rows_ref[k]).astype(bf16)
        total = total + small_product(back, chunk(z_ref, k))
    half_ref[...] = total
    sent = total.astype(bf16)
    for k in range(COLS):
        sent_ref[k] = sent


def final_kernel(
    place_ref, size_ref, half_ref, across_ref, coeffs_ref, rotation_ref, block_ref,
    own_ref, away_ref,
    rotated_ref, cos_ref, sin_ref, orbitals_ref, step_ref, sems,
):
    copies = gathered(place_ref, own_ref, away_ref, step_ref, sems)
    col = place_ref[4]
    width = rotated_ref.shape[1]
    rotated = rotation_ref[...]
    cos_part, sin_part = block_ref[:, :width], block_ref[:, width:]
    start = pl.multiple_of(col * width, width)
    orbitals = coeffs_ref[:, pl.ds(start, width)].astype(f32)
    for k in range(COLS):
        landed(copies, k)
        step = chunk(step_ref, k)
        cells = half_ref[k]
        cos_part = cos_part + small_product(cells[:, :width], step)
        sin_part = sin_part + small_product(cells[:, width:], step)
        rotated = rotated + small_product(across_ref[k, :, 2 * width : 3 * width], step)
        cells = coeffs_ref[:, k * width : (k + 1) * width]
        orbitals = orbitals + small_product(cells, step)
    rotated_ref[...] = rotated
    cos_ref[...] = cos_part
    sin_ref[...] = sin_part
    orbitals_ref[...] = within_rows(size_ref, orbitals).astype(bf16)


def on_device(coeffs, rotation, phase_ops, block_links, atom_size):
    rows_dev, orbital_count = coeffs.shape
    span_blocks, block_size = phase_ops.shape[2:4]
    reach_blocks = (span_blocks - 1) // 2
    rows_axis = lax.axis_size("rows")
    cols_axis = lax.axis_size("cols")
    row_count = orbital_count // rows_axis
    col_count = orbital_count // cols_axis
    both = 2 * col_count
    core = lax.axis_index("rows") % CORES
    own_x = lax.axis_index("rows") // (ZS * CORES)
    per_col = rows_axis // cols_axis
    own_row = lax.axis_index("rows")
    place = [own_x, core, own_row // per_col, own_row % per_col * row_count]
    place = jnp.stack(place + [lax.axis_index("cols")]).astype(jnp.int32)
    scale_factor = 0.125 / math.sqrt(orbital_count)

    within = lax.broadcasted_iota(jnp.int32, (rows_dev // block_size, block_size), 1)
    live_rows = (within < atom_size[:, None]).reshape(rows_dev)
    own_cols = lax.dynamic_slice_in_dim(coeffs, lax.axis_index("cols") * col_count, col_count, 1)
    own_cols = jnp.where(live_rows[:, None], own_cols, jnp.zeros_like(own_cols))
    width = reach_blocks * block_size
    up = [(i, (i + 1) % rows_axis) for i in range(rows_axis)]
    down = [((i + 1) % rows_axis, i) for i in range(rows_axis)]
    from_up = lax.ppermute(own_cols[rows_dev - width :], "rows", up)
    from_down = lax.ppermute(own_cols[:width], "rows", down)
    turn_coeffs, own_cols = lax.optimization_barrier((coeffs, own_cols))
    half_shape = ((orbital_count // CORES, rows_dev), bf16)
    own_turned, far_turned = call(
        functools.partial(turn_kernel, row_count),
        [half_shape] * 2,
        [smem, vmem],
        [],
        place,
        turn_coeffs,
        bytes_accessed=2**26,
    )
    from_up, from_down, far_turned = lax.optimization_barrier((from_up, from_down, far_turned))
    far_turned = other_core(far_turned)
    applied, own_diag = call(
        applied_kernel,
        [((rows_dev, both), bf16), ((1, both), f32)],
        [smem] * 2 + [vmem] * 4,
        [],
        atom_size,
        block_links,
        from_up,
        own_cols,
        from_down,
        phase_ops,
        bytes_accessed=2**22,
    )
    far_applied = other_core(applied)

    plane = ZS * row_count
    sent = ((plane + 16, both), bf16)
    one, three, two, chip, diag = call(
        product_kernel,
        [sent, sent, sent, ((plane, both), f32), ((1, both), f32)],
        [smem] + [vmem] * 7,
        [],
        place,
        own_turned,
        far_turned,
        applied,
        far_applied,
        from_up,
        from_down,
        own_diag,
    )
    got = [along_x(two, 2), along_x(one, 1), along_x(three, 3)]
    got = [cells.astype(f32) for cells in got]
    chip = chip + sum(cells[:plane] for cells in got)
    diag = diag[0] + sum(cells[plane] + cells[plane + 1] for cells in got)
    high = lax.reduce_precision(diag, 8, 7)
    terms = jnp.stack([high, diag - high]).astype(bf16).reshape(-1, 128)
    terms = jnp.pad(terms, ((0, row_count - terms.shape[0]), (0, 0)))
    terms = jnp.broadcast_to(terms[None], (ZS, row_count, 128))
    pieces = chip.astype(bf16).reshape(ZS, row_count, both)
    got = swap(jnp.concatenate([pieces, terms], axis=2), "rows", z_groups)
    z_block, z_sent, packed = call(
        sum_kernel,
        [
            ((row_count, both), f32),
            ((ZS, row_count, both), bf16),
            ((COLS, row_count, both + col_count + 128), bf16),
        ],
        [vmem] * 2,
        [],
        got,
        rotation,
    )

    panel = swap(z_sent, "rows", z_groups)
    packed, panel = lax.optimization_barrier((packed, panel))
    panels = [panel] + [along_x(panel, steps) for steps in (1, 2, 3)]
    across = swap(packed, "cols")
    stacked, across = lax.optimization_barrier((jnp.stack(panels), across))
    away = other_core(stacked)
    block = (row_count, col_count)
    gen_rows, diag_all, turned_diag = call(
        functools.partial(rows_kernel, scale_factor),
        [
            ((COLS,) + block, f32),
            ((2, COLS, col_count), f32),
            ((2, col_count, COLS), f32),
        ],
        [smem, vmem],
        [],
        place,
        across,
        bytes_accessed=2**28,
    )
    z_cols, square, step = call(
        functools.partial(square_kernel, scale_factor),
        [
            ((XS, ZS, CORES, row_count, both), bf16),
            ((COLS,) + block, bf16),
            ((ZS,) + block, bf16),
        ],
        [smem] + [vmem] * 3 + [hbm] * 2,
        [
            pltpu.VMEM((XS, ZS, CORES, row_count, both), bf16),
            pltpu.SemaphoreType.DMA((XS, 2)),
            pltpu.SemaphoreType.DMA((XS,)),
        ],
        place,
        gen_rows,
        diag_all,
        turned_diag,
        stacked,
        away,
        out_specs=[hbm, vmem, vmem],
    )

    step = swap(step, "rows", z_groups)
    square, step = lax.optimization_barrier((square, step))
    steps_x = [step] + [along_x(step, steps) for steps in (1, 2, 3)]
    square = swap(square, "cols")
    half_block, half_sent = call(
        half_kernel,
        [((row_count, both), f32), ((COLS, row_count, both), bf16)],
        [vmem] * 2 + [hbm, vmem],
        [
            pltpu.VMEM((XS, ZS, CORES, row_count, both), bf16),
            pltpu.SemaphoreType.DMA((XS,)),
        ],
        square,
        gen_rows,
        z_cols,
        z_block,
        bytes_accessed=2**26,
    )
    *steps_x, half_sent = lax.optimization_barrier((*steps_x, half_sent))
    step_stack = jnp.stack(steps_x)
    step_away = other_core(step_stack)
    half_rows = swap(half_sent, "cols")
    return tuple(
        call(
            final_kernel,
            [(block, f32)] * 3 + [((rows_dev, col_count), bf16)],
            [smem] * 2 + [vmem] * 5 + [hbm] * 2,
            [
                pltpu.VMEM((XS, ZS, CORES, row_count, col_count), bf16),
                pltpu.SemaphoreType.DMA((XS, 2)),
            ],
            place,
            atom_size,
            half_rows,
            across,
            coeffs,
            rotation,
            half_block,
            step_stack,
            step_away,
        )
    )


def solution(mesh):
    placed = (
        P("rows", None),
        P("rows", "cols"),
        P(None, "rows", None, None, None),
        P("rows", None),
        P("rows"),
    )
    return jax.shard_map(
        on_device,
        mesh=mesh,
        in_specs=placed,
        out_specs=(P("rows", "cols"), P("rows", "cols"), P("rows", "cols"), P("rows", "cols")),
        check_vma=False,
    )
```

```python
import functools
import math

import jax
import jax.numpy as jnp
from jax import lax
from jax.experimental import pallas as pl
from jax.experimental.pallas import tpu as pltpu
from jax.sharding import PartitionSpec as P

bf16 = jnp.bfloat16
f32 = jnp.float32

XS, ZS, CORES, COLS = 4, 8, 2, 8


def row_index(x, z, core):
    return (x * ZS + z) * CORES + core


z_groups = [[row_index(x, z, k) for z in range(ZS)] for x in range(XS) for k in range(CORES)]
plane_groups = [[row_index(x, z, k) for z in range(ZS) for k in range(CORES)] for x in range(XS)]


def swap(cells, axis, groups=None):
    return lax.all_to_all(cells, axis, 0, 0, tiled=True, axis_index_groups=groups)


def other_core(cells):
    count = lax.axis_size("rows")
    return lax.ppermute(cells, "rows", [(i, i ^ 1) for i in range(count)])


def along_x(cells, steps):
    line, count = ZS * CORES, lax.axis_size("rows")
    return lax.ppermute(cells, "rows", [(i, (i + steps * line) % count) for i in range(count)])


def small_product(left, right):
    return jnp.dot(left, right, preferred_element_type=f32)


vmem = pl.BlockSpec(memory_space=pltpu.VMEM)
smem = pl.BlockSpec(memory_space=pltpu.SMEM)
hbm = pl.BlockSpec(memory_space=pltpu.HBM)


def call(kernel, shapes, in_specs, scratch, *operands, bytes_accessed=2**20):
    return pl.pallas_call(
        kernel,
        out_shape=[jax.ShapeDtypeStruct(*shape) for shape in shapes],
        in_specs=in_specs,
        out_specs=[vmem] * len(shapes),
        scratch_shapes=scratch,
        compiler_params=pltpu.CompilerParams(vmem_limit_bytes=12 * 2**20),
        cost_estimate=pl.CostEstimate(
            flops=0, bytes_accessed=bytes_accessed, transcendentals=0
        ),
    )(*operands)


def within_rows(size_ref, cells):
    blocks = size_ref.shape[0]
    size = cells.shape[0] // blocks
    within = lax.broadcasted_iota(jnp.int32, (size, cells.shape[1]), 0)
    parts = [
        jnp.where(within < size_ref[b], cells[b * size : (b + 1) * size], 0.0)
        for b in range(blocks)
    ]
    return jnp.concatenate(parts, axis=0)


def turn_kernel(
    rows, place_ref, size_ref, links_ref, coeffs_ref, ops_ref, own_ref, far_ref, gated_ref
):
    core = place_ref[1]
    lanes = 128
    for start in range(0, coeffs_ref.shape[1], lanes):
        cells = coeffs_ref[:, start : start + lanes].astype(f32).T
        for offset in range(0, lanes, CORES * rows):
            first = cells[offset : offset + rows]
            second = cells[offset + rows : offset + 2 * rows]
            where = pl.ds((start + offset) // CORES, rows)
            own_ref[where, :] = jnp.where(core == 0, first, second).astype(bf16)
            far_ref[where, :] = jnp.where(core == 0, second, first).astype(bf16)
    phases, blocks, span, size, _ = ops_ref.shape
    within = lax.broadcasted_iota(jnp.int32, (size, size), 0)
    for b in range(blocks):
        for t in range(span):
            kept = within < jnp.where(links_ref[b, t] != 0, size_ref[b], 0)
            for p in range(phases):
                cells = jnp.where(kept, ops_ref[p, b, t].astype(f32), 0.0)
                gated_ref[p, b, :, t * size : (t + 1) * size] = cells.astype(bf16)


def applied_kernel(up_ref, cols_ref, down_ref, gated_ref, out_ref, diag_ref):
    phases, blocks, size, depth = gated_ref.shape
    width = cols_ref.shape[1]
    padded = jnp.concatenate([up_ref[...], cols_ref[...], down_ref[...]], axis=0)
    first = up_ref.shape[0] - (depth // size - 1) // 2 * size
    own = cols_ref[...].astype(f32)
    for p in range(phases):
        parts = []
        for b in range(blocks):
            start = first + b * size
            parts.append(small_product(gated_ref[p, b], padded[start : start + depth]))
        total = jnp.concatenate(parts, axis=0).astype(bf16)
        out_ref[:, p * width : (p + 1) * width] = total
        sums = jnp.sum(total.astype(f32) * own, axis=0, keepdims=True)
        diag_ref[:, p * width : (p + 1) * width] = sums


def product_kernel(
    place_ref, own_ref, far_ref, applied_ref, far_applied_ref, up_ref, down_ref, own_diag_ref,
    one_ref, three_ref, two_ref, none_ref, diag_ref,
):
    x, core = place_ref[0], place_ref[1]
    rows, both = none_ref.shape
    width = both // 2
    near = up_ref.shape[0] - far_applied_ref.shape[0]
    up = up_ref[near:, :].astype(f32)
    cols = jnp.where(core == 0, down_ref[: far_applied_ref.shape[0], :].astype(f32), up)
    sums = [
        jnp.sum(
            cols * far_applied_ref[:, p * width : (p + 1) * width].astype(f32),
            axis=0,
            keepdims=True,
        )
        for p in range(2)
    ]
    diag = own_diag_ref[...] + jnp.concatenate(sums, axis=1)
    diag_ref[...] = diag
    high = diag.astype(bf16).astype(f32)
    fill = jnp.zeros((two_ref.shape[0] - rows - 2, both), f32)
    tail = jnp.concatenate([high, diag - high, fill], axis=0).astype(bf16)
    for steps, out_ref in ((2, two_ref), (1, one_ref), (3, three_ref), (0, none_ref)):
        start = pl.multiple_of(lax.rem(x + steps, XS) * rows, rows)
        total = small_product(own_ref[pl.ds(start, rows), :], applied_ref[...])
        total = total + small_product(far_ref[pl.ds(start, rows), :], far_applied_ref[...])
        out_ref[:rows, :] = total.astype(out_ref.dtype)
        if steps:
            out_ref[rows:, :] = tail


def sum_kernel(got_ref, rotation_ref, block_ref, z_ref, packed_ref):
    count, _, wide = z_ref.shape
    total = got_ref[0].astype(f32)
    for i in range(1, count):
        total = total + got_ref[i].astype(f32)
    block = total[:, :wide]
    block_ref[...] = block
    half = block.astype(bf16)
    diag = total[:4, wide:] + total[4:8, wide:]
    high = diag.astype(bf16).astype(f32)
    fill = jnp.zeros((block.shape[0] - 8, 128), f32)
    tail = jnp.concatenate([high, diag - high, fill], axis=0).astype(bf16)
    packed = jnp.concatenate([half, rotation_ref[...].astype(bf16), tail], axis=1)
    for i in range(count):
        z_ref[i] = half
        packed_ref[i] = packed


def gathered(place_ref, own_ref, away_ref, out_ref, sems):
    x, core = place_ref[0], place_ref[1]
    copies = []
    for source in range(XS):
        steps = lax.rem(x + XS - source, XS)
        pairs = ((own_ref, core), (away_ref, 1 - core))
        copies.append(
            [
                pltpu.make_async_copy(
                    ref.at[steps], out_ref.at[source, :, which], sems.at[source, i]
                )
                for i, (ref, which) in enumerate(pairs)
            ]
        )
    for pair in copies:
        for copy in pair:
            copy.start()
    return copies


def landed(copies, k):
    if k * XS % COLS == 0:
        for copy in copies[k * XS // COLS]:
            copy.wait()


def chunk(panel_ref, k):
    per = ZS * XS // COLS
    cells = panel_ref[k * per // ZS, pl.ds(k * per % ZS, per)]
    return cells.reshape(-1, cells.shape[-1])


def square_kernel(
    scale, place_ref, across_ref, own_ref, away_ref,
    z_ref, rows_ref, square_ref, step_ref, diag_ref, turned_ref, sems,
):
    copies = gathered(place_ref, own_ref, away_ref, z_ref, sems)
    mine, low, col = place_ref[2], place_ref[3], place_ref[4]
    rows, width = rows_ref.shape[1:]
    terms = across_ref[:, :, -128:].astype(f32)
    per = width // 128
    for p in range(2):
        parts = [terms[:, p * per + h] + terms[:, 2 * per + p * per + h] for h in range(per)]
        diag_ref[p] = jnp.concatenate(parts, axis=1)
        turned_ref[p] = diag_ref[p].T
    lane = lax.broadcasted_iota(jnp.int32, (rows, COLS), 1)
    down = [
        jnp.sum(
            jnp.where(lane == mine, turned_ref[p, pl.ds(low, rows), :], 0.0),
            axis=1,
            keepdims=True,
        )
        for p in range(2)
    ]
    for k in range(COLS):
        cells = across_ref[k].astype(f32)
        cos_part = cells[:, :width] * (diag_ref[0, k : k + 1, :] - down[0])
        sin_part = cells[:, width : 2 * width] * (diag_ref[1, k : k + 1, :] - down[1])
        rows_ref[k] = (cos_part + sin_part) * scale
    across_diag = [diag_ref[p, pl.ds(col, 1), :] for p in range(2)]
    square = jnp.zeros((rows, width), f32)
    for k in range(COLS):
        landed(copies, k)
        cells = chunk(z_ref, k).astype(f32)
        cos_part = cells[:, :width] * (across_diag[0] - turned_ref[0, :, k : k + 1])
        sin_part = cells[:, width:] * (across_diag[1] - turned_ref[1, :, k : k + 1])
        cells = ((cos_part + sin_part) * scale).astype(bf16)
        square = square + small_product(rows_ref[k].astype(bf16), cells)
    step = (rows_ref[col] + 0.5 * square).astype(bf16)
    square = square.astype(bf16)
    for k in range(square_ref.shape[0]):
        square_ref[k] = square
    for k in range(step_ref.shape[0]):
        step_ref[k] = step


def half_kernel(square_ref, rows_ref, z_ref, block_ref, half_ref, sent_ref):
    total = block_ref[...]
    for k in range(COLS):
        back = (0.5 * square_ref[k].astype(f32) - rows_ref[k]).astype(bf16)
        total = total + small_product(back, chunk(z_ref, k))
    half_ref[...] = total
    sent = total.astype(bf16)
    for k in range(COLS):
        sent_ref[k] = sent


def final_kernel(
    place_ref, size_ref, half_ref, across_ref, coeffs_ref, rotation_ref, block_ref,
    own0, own1, own2, own3,
    rotated_ref, cos_ref, sin_ref, orbitals_ref, step_ref, sems,
):
    copies = [
        pltpu.make_async_copy(ref, step_ref.at[steps], sems.at[steps])
        for steps, ref in enumerate((own0, own1, own2, own3))
    ]
    for copy in copies:
        copy.start()
    col = place_ref[4]
    width = rotated_ref.shape[1]
    rotated = rotation_ref[...]
    cos_part, sin_part = block_ref[:, :width], block_ref[:, width:]
    start = pl.multiple_of(col * width, width)
    orbitals = coeffs_ref[:, pl.ds(start, width)].astype(f32)
    per = COLS // XS
    for steps in range(XS):
        copies[steps].wait()
        source = lax.rem(place_ref[0] + XS - steps, XS)
        count = step_ref.shape[1] // per
        for part in range(per):
            k = source * per + part
            step = step_ref[steps, part * count : (part + 1) * count].reshape(-1, width)
            cells = half_ref[k]
            cos_part = cos_part + small_product(cells[:, :width], step)
            sin_part = sin_part + small_product(cells[:, width:], step)
            rotated = rotated + small_product(across_ref[k, :, 2 * width : 3 * width], step)
            cells = coeffs_ref[:, pl.ds(pl.multiple_of(k * width, width), width)]
            orbitals = orbitals + small_product(cells, step)
    rotated_ref[...] = rotated
    cos_ref[...] = cos_part
    sin_ref[...] = sin_part
    orbitals_ref[...] = within_rows(size_ref, orbitals).astype(bf16)


def on_device(coeffs, rotation, phase_ops, block_links, atom_size):
    rows_dev, orbital_count = coeffs.shape
    span_blocks, block_size = phase_ops.shape[2:4]
    reach_blocks = (span_blocks - 1) // 2
    rows_axis = lax.axis_size("rows")
    cols_axis = lax.axis_size("cols")
    row_count = orbital_count // rows_axis
    col_count = orbital_count // cols_axis
    both = 2 * col_count
    core = lax.axis_index("rows") % CORES
    own_x = lax.axis_index("rows") // (ZS * CORES)
    per_col = rows_axis // cols_axis
    own_row = lax.axis_index("rows")
    place = [own_x, core, own_row // per_col, own_row % per_col * row_count]
    place = jnp.stack(place + [lax.axis_index("cols")]).astype(jnp.int32)
    scale_factor = 0.125 / math.sqrt(orbital_count)

    within = lax.broadcasted_iota(jnp.int32, (rows_dev // block_size, block_size), 1)
    live_rows = (within < atom_size[:, None]).reshape(rows_dev)
    own_cols = lax.dynamic_slice_in_dim(coeffs, lax.axis_index("cols") * col_count, col_count, 1)
    own_cols = jnp.where(live_rows[:, None], own_cols, jnp.zeros_like(own_cols))
    width = reach_blocks * block_size
    up = [(i, (i + 1) % rows_axis) for i in range(rows_axis)]
    down = [((i + 1) % rows_axis, i) for i in range(rows_axis)]
    from_up = lax.ppermute(own_cols[rows_dev - width :], "rows", up)
    from_down = lax.ppermute(own_cols[:width], "rows", down)
    turn_coeffs, own_cols = lax.optimization_barrier((coeffs, own_cols))
    half_shape = ((orbital_count // CORES, rows_dev), bf16)
    phases, blocks = phase_ops.shape[:2]
    own_turned, far_turned, gated = call(
        functools.partial(turn_kernel, row_count),
        [half_shape] * 2 + [((phases, blocks, block_size, span_blocks * block_size), bf16)],
        [smem] * 3 + [vmem] * 2,
        [],
        place,
        atom_size,
        block_links,
        turn_coeffs,
        phase_ops,
        bytes_accessed=2**26,
    )
    from_up, from_down, far_turned = lax.optimization_barrier((from_up, from_down, far_turned))
    far_turned = other_core(far_turned)
    applied, own_diag = call(
        applied_kernel,
        [((rows_dev, both), bf16), ((1, both), f32)],
        [vmem] * 4,
        [],
        from_up,
        own_cols,
        from_down,
        gated,
        bytes_accessed=2**22,
    )
    far_applied = other_core(applied)

    plane = ZS * row_count
    sent = ((plane + 16, both), bf16)
    one, three, two, chip, diag = call(
        product_kernel,
        [sent, sent, sent, ((plane, both), f32), ((1, both), f32)],
        [smem] + [vmem] * 7,
        [],
        place,
        own_turned,
        far_turned,
        applied,
        far_applied,
        from_up,
        from_down,
        own_diag,
    )
    got = [along_x(two, 2), along_x(one, 1), along_x(three, 3)]
    got = [cells.astype(f32) for cells in got]
    chip = chip + sum(cells[:plane] for cells in got)
    diag = diag[0] + sum(cells[plane] + cells[plane + 1] for cells in got)
    high = lax.reduce_precision(diag, 8, 7)
    terms = jnp.stack([high, diag - high]).astype(bf16).reshape(-1, 128)
    terms = jnp.pad(terms, ((0, row_count - terms.shape[0]), (0, 0)))
    terms = jnp.broadcast_to(terms[None], (ZS, row_count, 128))
    pieces = chip.astype(bf16).reshape(ZS, row_count, both)
    got = swap(jnp.concatenate([pieces, terms], axis=2), "rows", z_groups)
    z_block, z_sent, packed = call(
        sum_kernel,
        [
            ((row_count, both), f32),
            ((ZS, row_count, both), bf16),
            ((COLS, row_count, both + col_count + 128), bf16),
        ],
        [vmem] * 2,
        [],
        got,
        rotation,
    )

    panel = swap(z_sent, "rows", z_groups)
    packed, panel = lax.optimization_barrier((packed, panel))
    panels = [panel] + [along_x(panel, steps) for steps in (1, 2, 3)]
    across = swap(packed, "cols")
    stacked, across = lax.optimization_barrier((jnp.stack(panels), across))
    away = other_core(stacked)
    block = (row_count, col_count)
    z_cols, gen_rows, square, step = call(
        functools.partial(square_kernel, scale_factor),
        [
            ((XS, ZS, CORES, row_count, both), bf16),
            ((COLS,) + block, f32),
            ((COLS,) + block, bf16),
            ((ZS * CORES,) + block, bf16),
        ],
        [smem, vmem] + [hbm] * 2,
        [
            pltpu.VMEM((2, COLS, col_count), f32),
            pltpu.VMEM((2, col_count, COLS), f32),
            pltpu.SemaphoreType.DMA((XS, 2)),
        ],
        place,
        across,
        stacked,
        away,
    )

    step = swap(step, "rows", plane_groups)
    square, step = lax.optimization_barrier((square, step))
    steps_x = [step] + [along_x(step, steps) for steps in (1, 2, 3)]
    square = swap(square, "cols")
    half_block, half_sent = call(
        half_kernel,
        [((row_count, both), f32), ((COLS, row_count, both), bf16)],
        [vmem] * 4,
        [],
        square,
        gen_rows,
        z_cols,
        z_block,
        bytes_accessed=2**26,
    )
    half_rows = swap(half_sent, "cols")
    return tuple(
        call(
            final_kernel,
            [(block, f32)] * 3 + [((rows_dev, col_count), bf16)],
            [smem] * 2 + [vmem] * 5 + [hbm] * XS,
            [
                pltpu.VMEM((XS, ZS * CORES) + block, bf16),
                pltpu.SemaphoreType.DMA((XS,)),
            ],
            place,
            atom_size,
            half_rows,
            across,
            coeffs,
            rotation,
            half_block,
            *steps_x,
        )
    )


def solution(mesh):
    placed = (
        P("rows", None),
        P("rows", "cols"),
        P(None, "rows", None, None, None),
        P("rows", None),
        P("rows"),
    )
    return jax.shard_map(
        on_device,
        mesh=mesh,
        in_specs=placed,
        out_specs=(P("rows", "cols"), P("rows", "cols"), P("rows", "cols"), P("rows", "cols")),
        check_vma=False,
    )
```

```python
import functools
import math

import jax
import jax.numpy as jnp
from jax import lax
from jax.experimental import pallas as pl
from jax.experimental.pallas import tpu as pltpu
from jax.sharding import PartitionSpec as P

bf16 = jnp.bfloat16
f32 = jnp.float32

XS, ZS, CORES, COLS = 4, 8, 2, 8


def row_index(x, z, core):
    return (x * ZS + z) * CORES + core


z_groups = [[row_index(x, z, k) for z in range(ZS)] for x in range(XS) for k in range(CORES)]
plane_groups = [[row_index(x, z, k) for z in range(ZS) for k in range(CORES)] for x in range(XS)]


def swap(cells, axis, groups=None):
    return lax.all_to_all(cells, axis, 0, 0, tiled=True, axis_index_groups=groups)


def other_core(cells):
    count = lax.axis_size("rows")
    return lax.ppermute(cells, "rows", [(i, i ^ 1) for i in range(count)])


def along_x(cells, steps):
    line, count = ZS * CORES, lax.axis_size("rows")
    return lax.ppermute(cells, "rows", [(i, (i + steps * line) % count) for i in range(count)])


def small_product(left, right):
    return jnp.dot(left, right, preferred_element_type=f32)


vmem = pl.BlockSpec(memory_space=pltpu.VMEM)
smem = pl.BlockSpec(memory_space=pltpu.SMEM)
hbm = pl.BlockSpec(memory_space=pltpu.HBM)


def call(kernel, shapes, in_specs, scratch, *operands, bytes_accessed=2**20, flops=0):
    return pl.pallas_call(
        kernel,
        out_shape=[jax.ShapeDtypeStruct(*shape) for shape in shapes],
        in_specs=in_specs,
        out_specs=[vmem] * len(shapes),
        scratch_shapes=scratch,
        compiler_params=pltpu.CompilerParams(vmem_limit_bytes=12 * 2**20),
        cost_estimate=pl.CostEstimate(
            flops=flops, bytes_accessed=bytes_accessed, transcendentals=0
        ),
    )(*operands)


def within_rows(size_ref, cells):
    blocks = size_ref.shape[0]
    size = cells.shape[0] // blocks
    within = lax.broadcasted_iota(jnp.int32, (size, cells.shape[1]), 0)
    parts = [
        jnp.where(within < size_ref[b], cells[b * size : (b + 1) * size], 0.0)
        for b in range(blocks)
    ]
    return jnp.concatenate(parts, axis=0)


def turn_kernel(
    rows, place_ref, size_ref, links_ref, coeffs_ref, ops_ref, own_ref, far_ref, gated_ref
):
    core = place_ref[1]
    lanes = 128
    for start in range(0, coeffs_ref.shape[1], lanes):
        cells = coeffs_ref[:, start : start + lanes].astype(f32).T
        for offset in range(0, lanes, CORES * rows):
            first = cells[offset : offset + rows]
            second = cells[offset + rows : offset + 2 * rows]
            where = pl.ds((start + offset) // CORES, rows)
            own_ref[where, :] = jnp.where(core == 0, first, second).astype(bf16)
            far_ref[where, :] = jnp.where(core == 0, second, first).astype(bf16)
    phases, blocks, span, size, _ = ops_ref.shape
    within = lax.broadcasted_iota(jnp.int32, (size, size), 0)
    for b in range(blocks):
        for t in range(span):
            kept = within < jnp.where(links_ref[b, t] != 0, size_ref[b], 0)
            for p in range(phases):
                cells = jnp.where(kept, ops_ref[p, b, t].astype(f32), 0.0)
                gated_ref[p, b, :, t * size : (t + 1) * size] = cells.astype(bf16)


def applied_kernel(up_ref, cols_ref, down_ref, gated_ref, out_ref, diag_ref):
    phases, blocks, size, depth = gated_ref.shape
    width = cols_ref.shape[1]
    padded = jnp.concatenate([up_ref[...], cols_ref[...], down_ref[...]], axis=0)
    first = up_ref.shape[0] - (depth // size - 1) // 2 * size
    own = cols_ref[...].astype(f32)
    for p in range(phases):
        parts = []
        for b in range(blocks):
            start = first + b * size
            parts.append(small_product(gated_ref[p, b], padded[start : start + depth]))
        total = jnp.concatenate(parts, axis=0).astype(bf16)
        out_ref[:, p * width : (p + 1) * width] = total
        sums = jnp.sum(total.astype(f32) * own, axis=0, keepdims=True)
        diag_ref[:, p * width : (p + 1) * width] = sums


def product_kernel(
    place_ref, own_ref, far_ref, applied_ref, far_applied_ref, up_ref, down_ref, own_diag_ref,
    one_ref, three_ref, two_ref, none_ref, diag_ref,
):
    x, core = place_ref[0], place_ref[1]
    rows, both = none_ref.shape
    width = both // 2
    near = up_ref.shape[0] - far_applied_ref.shape[0]
    up = up_ref[near:, :].astype(f32)
    cols = jnp.where(core == 0, down_ref[: far_applied_ref.shape[0], :].astype(f32), up)
    sums = [
        jnp.sum(
            cols * far_applied_ref[:, p * width : (p + 1) * width].astype(f32),
            axis=0,
            keepdims=True,
        )
        for p in range(2)
    ]
    diag = own_diag_ref[...] + jnp.concatenate(sums, axis=1)
    diag_ref[...] = diag
    high = diag.astype(bf16).astype(f32)
    fill = jnp.zeros((two_ref.shape[0] - rows - 2, both), f32)
    tail = jnp.concatenate([high, diag - high, fill], axis=0).astype(bf16)
    for steps, out_ref in ((2, two_ref), (1, one_ref), (3, three_ref), (0, none_ref)):
        start = pl.multiple_of(lax.rem(x + steps, XS) * rows, rows)
        total = small_product(own_ref[pl.ds(start, rows), :], applied_ref[...])
        total = total + small_product(far_ref[pl.ds(start, rows), :], far_applied_ref[...])
        out_ref[:rows, :] = total.astype(out_ref.dtype)
        if steps:
            out_ref[rows:, :] = tail


def sum_kernel(got_ref, rotation_ref, block_ref, z_ref, packed_ref):
    count, _, wide = z_ref.shape
    total = got_ref[0].astype(f32)
    for i in range(1, count):
        total = total + got_ref[i].astype(f32)
    block = total[:, :wide]
    block_ref[...] = block
    half = block.astype(bf16)
    diag = total[:4, wide:] + total[4:8, wide:]
    high = diag.astype(bf16).astype(f32)
    fill = jnp.zeros((block.shape[0] - 8, 128), f32)
    tail = jnp.concatenate([high, diag - high, fill], axis=0).astype(bf16)
    packed = jnp.concatenate([half, rotation_ref[...].astype(bf16), tail], axis=1)
    for i in range(count):
        z_ref[i] = half
        packed_ref[i] = packed


def gathered(place_ref, own_ref, away_ref, out_ref, sems):
    x, core = place_ref[0], place_ref[1]
    copies = []
    for source in range(XS):
        steps = lax.rem(x + XS - source, XS)
        pairs = ((own_ref, core), (away_ref, 1 - core))
        copies.append(
            [
                pltpu.make_async_copy(
                    ref.at[steps], out_ref.at[source, :, which], sems.at[source, i]
                )
                for i, (ref, which) in enumerate(pairs)
            ]
        )
    for pair in copies:
        for copy in pair:
            copy.start()
    return copies


def landed(copies, k):
    if k * XS % COLS == 0:
        for copy in copies[k * XS // COLS]:
            copy.wait()


def chunk(panel_ref, k):
    per = ZS * XS // COLS
    cells = panel_ref[k * per // ZS, pl.ds(k * per % ZS, per)]
    return cells.reshape(-1, cells.shape[-1])


def square_kernel(
    scale, place_ref, across_ref, own_ref, away_ref,
    z_ref, rows_ref, square_ref, step_ref, diag_ref, turned_ref, sems,
):
    copies = gathered(place_ref, own_ref, away_ref, z_ref, sems)
    mine, low, col = place_ref[2], place_ref[3], place_ref[4]
    rows, width = rows_ref.shape[1:]
    terms = across_ref[:, :, -128:].astype(f32)
    per = width // 128
    for p in range(2):
        parts = [terms[:, p * per + h] + terms[:, 2 * per + p * per + h] for h in range(per)]
        diag_ref[p] = jnp.concatenate(parts, axis=1)
        turned_ref[p] = diag_ref[p].T
    lane = lax.broadcasted_iota(jnp.int32, (rows, COLS), 1)
    down = [
        jnp.sum(
            jnp.where(lane == mine, turned_ref[p, pl.ds(low, rows), :], 0.0),
            axis=1,
            keepdims=True,
        )
        for p in range(2)
    ]
    for k in range(COLS):
        cells = across_ref[k].astype(f32)
        cos_part = cells[:, :width] * (diag_ref[0, k : k + 1, :] - down[0])
        sin_part = cells[:, width : 2 * width] * (diag_ref[1, k : k + 1, :] - down[1])
        rows_ref[k] = (cos_part + sin_part) * scale
    across_diag = [diag_ref[p, pl.ds(col, 1), :] for p in range(2)]
    square = jnp.zeros((rows, width), f32)
    for k in range(COLS):
        landed(copies, k)
        cells = chunk(z_ref, k).astype(f32)
        cos_part = cells[:, :width] * (across_diag[0] - turned_ref[0, :, k : k + 1])
        sin_part = cells[:, width:] * (across_diag[1] - turned_ref[1, :, k : k + 1])
        cells = ((cos_part + sin_part) * scale).astype(bf16)
        square = square + small_product(rows_ref[k].astype(bf16), cells)
    step = (rows_ref[col] + 0.5 * square).astype(bf16)
    square = square.astype(bf16)
    for k in range(square_ref.shape[0]):
        square_ref[k] = square
    for k in range(step_ref.shape[0]):
        step_ref[k] = step


def half_kernel(square_ref, rows_ref, z_ref, block_ref, half_ref, sent_ref):
    total = block_ref[...]
    for k in range(COLS):
        back = (0.5 * square_ref[k].astype(f32) - rows_ref[k]).astype(bf16)
        total = total + small_product(back, chunk(z_ref, k))
    half_ref[...] = total
    sent = total.astype(bf16)
    for k in range(COLS):
        sent_ref[k] = sent


def pieces_of(place_ref, refs, step_ref, sems):
    copies = [
        pltpu.make_async_copy(ref, step_ref.at[steps], sems.at[steps])
        for steps, ref in enumerate(refs)
    ]
    for copy in copies:
        copy.start()
    width = step_ref.shape[-1]
    per = COLS // XS
    count = step_ref.shape[1] // per
    for steps in range(XS):
        copies[steps].wait()
        source = lax.rem(place_ref[0] + XS - steps, XS)
        for part in range(per):
            cells = step_ref[steps, part * count : (part + 1) * count]
            yield source * per + part, cells.reshape(-1, width)


def orbitals_kernel(
    place_ref, size_ref, across_ref, coeffs_ref, rotation_ref, own0, own1, own2, own3,
    rotated_ref, orbitals_ref, step_ref, sems,
):
    width = rotated_ref.shape[1]
    rotated = rotation_ref[...]
    start = pl.multiple_of(place_ref[4] * width, width)
    orbitals = coeffs_ref[:, pl.ds(start, width)].astype(f32)
    for k, step in pieces_of(place_ref, (own0, own1, own2, own3), step_ref, sems):
        rotated = rotated + small_product(across_ref[k, :, 2 * width : 3 * width], step)
        cells = coeffs_ref[:, pl.ds(pl.multiple_of(k * width, width), width)]
        orbitals = orbitals + small_product(cells, step)
    rotated_ref[...] = rotated
    orbitals_ref[...] = within_rows(size_ref, orbitals).astype(bf16)


def phases_kernel(
    place_ref, half_ref, block_ref, own0, own1, own2, own3, cos_ref, sin_ref, step_ref, sems
):
    width = cos_ref.shape[1]
    cos_part, sin_part = block_ref[:, :width], block_ref[:, width:]
    for k, step in pieces_of(place_ref, (own0, own1, own2, own3), step_ref, sems):
        cells = half_ref[k]
        cos_part = cos_part + small_product(cells[:, :width], step)
        sin_part = sin_part + small_product(cells[:, width:], step)
    cos_ref[...] = cos_part
    sin_ref[...] = sin_part


def on_device(coeffs, rotation, phase_ops, block_links, atom_size):
    rows_dev, orbital_count = coeffs.shape
    span_blocks, block_size = phase_ops.shape[2:4]
    reach_blocks = (span_blocks - 1) // 2
    rows_axis = lax.axis_size("rows")
    cols_axis = lax.axis_size("cols")
    row_count = orbital_count // rows_axis
    col_count = orbital_count // cols_axis
    both = 2 * col_count
    core = lax.axis_index("rows") % CORES
    own_x = lax.axis_index("rows") // (ZS * CORES)
    per_col = rows_axis // cols_axis
    own_row = lax.axis_index("rows")
    place = [own_x, core, own_row // per_col, own_row % per_col * row_count]
    place = jnp.stack(place + [lax.axis_index("cols")]).astype(jnp.int32)
    scale_factor = 0.125 / math.sqrt(orbital_count)

    within = lax.broadcasted_iota(jnp.int32, (rows_dev // block_size, block_size), 1)
    live_rows = (within < atom_size[:, None]).reshape(rows_dev)
    own_cols = lax.dynamic_slice_in_dim(coeffs, lax.axis_index("cols") * col_count, col_count, 1)
    own_cols = jnp.where(live_rows[:, None], own_cols, jnp.zeros_like(own_cols))
    width = reach_blocks * block_size
    up = [(i, (i + 1) % rows_axis) for i in range(rows_axis)]
    down = [((i + 1) % rows_axis, i) for i in range(rows_axis)]
    from_up = lax.ppermute(own_cols[rows_dev - width :], "rows", up)
    from_down = lax.ppermute(own_cols[:width], "rows", down)
    turn_coeffs, own_cols = lax.optimization_barrier((coeffs, own_cols))
    half_shape = ((orbital_count // CORES, rows_dev), bf16)
    phases, blocks = phase_ops.shape[:2]
    own_turned, far_turned, gated = call(
        functools.partial(turn_kernel, row_count),
        [half_shape] * 2 + [((phases, blocks, block_size, span_blocks * block_size), bf16)],
        [smem] * 3 + [vmem] * 2,
        [],
        place,
        atom_size,
        block_links,
        turn_coeffs,
        phase_ops,
        bytes_accessed=2**26,
    )
    from_up, from_down, far_turned = lax.optimization_barrier((from_up, from_down, far_turned))
    far_turned = other_core(far_turned)
    applied, own_diag = call(
        applied_kernel,
        [((rows_dev, both), bf16), ((1, both), f32)],
        [vmem] * 4,
        [],
        from_up,
        own_cols,
        from_down,
        gated,
        bytes_accessed=2**22,
    )
    far_applied = other_core(applied)

    plane = ZS * row_count
    sent = ((plane + 16, both), bf16)
    one, three, two, chip, diag = call(
        product_kernel,
        [sent, sent, sent, ((plane, both), f32), ((1, both), f32)],
        [smem] + [vmem] * 7,
        [],
        place,
        own_turned,
        far_turned,
        applied,
        far_applied,
        from_up,
        from_down,
        own_diag,
    )
    got = [along_x(two, 2), along_x(one, 1), along_x(three, 3)]
    got = [cells.astype(f32) for cells in got]
    chip = chip + sum(cells[:plane] for cells in got)
    diag = diag[0] + sum(cells[plane] + cells[plane + 1] for cells in got)
    high = lax.reduce_precision(diag, 8, 7)
    terms = jnp.stack([high, diag - high]).astype(bf16).reshape(-1, 128)
    terms = jnp.pad(terms, ((0, row_count - terms.shape[0]), (0, 0)))
    terms = jnp.broadcast_to(terms[None], (ZS, row_count, 128))
    pieces = chip.astype(bf16).reshape(ZS, row_count, both)
    got = swap(jnp.concatenate([pieces, terms], axis=2), "rows", z_groups)
    z_block, z_sent, packed = call(
        sum_kernel,
        [
            ((row_count, both), f32),
            ((ZS, row_count, both), bf16),
            ((COLS, row_count, both + col_count + 128), bf16),
        ],
        [vmem] * 2,
        [],
        got,
        rotation,
    )

    panel = swap(z_sent, "rows", z_groups)
    packed, panel = lax.optimization_barrier((packed, panel))
    panels = [panel] + [along_x(panel, steps) for steps in (1, 2, 3)]
    across = swap(packed, "cols")
    stacked, across = lax.optimization_barrier((jnp.stack(panels), across))
    away = other_core(stacked)
    block = (row_count, col_count)
    z_cols, gen_rows, square, step = call(
        functools.partial(square_kernel, scale_factor),
        [
            ((XS, ZS, CORES, row_count, both), bf16),
            ((COLS,) + block, f32),
            ((COLS,) + block, bf16),
            ((ZS * CORES,) + block, bf16),
        ],
        [smem, vmem] + [hbm] * 2,
        [
            pltpu.VMEM((2, COLS, col_count), f32),
            pltpu.VMEM((2, col_count, COLS), f32),
            pltpu.SemaphoreType.DMA((XS, 2)),
        ],
        place,
        across,
        stacked,
        away,
    )

    step = swap(step, "rows", plane_groups)
    square, step = lax.optimization_barrier((square, step))
    steps_x = [step] + [along_x(step, steps) for steps in (1, 2, 3)]
    square = swap(square, "cols")
    half_block, half_sent = call(
        half_kernel,
        [((row_count, both), f32), ((COLS, row_count, both), bf16)],
        [vmem] * 4,
        [],
        square,
        gen_rows,
        z_cols,
        z_block,
        flops=2**35,
    )
    half_rows = swap(half_sent, "cols")
    panel_scratch = [
        pltpu.VMEM((XS, ZS * CORES) + block, bf16),
        pltpu.SemaphoreType.DMA((XS,)),
    ]
    rotated, orbitals = call(
        orbitals_kernel,
        [(block, f32), ((rows_dev, col_count), bf16)],
        [smem] * 2 + [vmem] * 3 + [hbm] * XS,
        panel_scratch,
        place,
        atom_size,
        across,
        coeffs,
        rotation,
        *steps_x,
        flops=2**32,
    )
    phase_cos, phase_sin = call(
        phases_kernel,
        [(block, f32)] * 2,
        [smem] + [vmem] * 2 + [hbm] * XS,
        panel_scratch,
        place,
        half_rows,
        half_block,
        *steps_x,
    )
    return (rotated, phase_cos, phase_sin, orbitals)


def solution(mesh):
    placed = (
        P("rows", None),
        P("rows", "cols"),
        P(None, "rows", None, None, None),
        P("rows", None),
        P("rows"),
    )
    return jax.shard_map(
        on_device,
        mesh=mesh,
        in_specs=placed,
        out_specs=(P("rows", "cols"), P("rows", "cols"), P("rows", "cols"), P("rows", "cols")),
        check_vma=False,
    )
```

```python
import functools
import math

import jax
import jax.numpy as jnp
from jax import lax
from jax.experimental import pallas as pl
from jax.experimental.pallas import tpu as pltpu
from jax.sharding import PartitionSpec as P

bf16 = jnp.bfloat16
f32 = jnp.float32

XS, ZS, CORES, COLS = 4, 8, 2, 8


def row_index(x, z, core):
    return (x * ZS + z) * CORES + core


z_groups = [[row_index(x, z, k) for z in range(ZS)] for x in range(XS) for k in range(CORES)]
z_order = [4, 5, 6, 7, 0, 1, 2, 3]
col_order = [4, 5, 6, 7, 3, 2, 1, 0]
plane_groups = [[row_index(x, z, k) for z in z_order for k in range(CORES)] for x in range(XS)]


def swap(cells, axis, groups=None):
    return lax.all_to_all(cells, axis, 0, 0, tiled=True, axis_index_groups=groups)


def other_core(cells):
    count = lax.axis_size("rows")
    return lax.ppermute(cells, "rows", [(i, i ^ 1) for i in range(count)])


def along_x(cells, steps):
    line, count = ZS * CORES, lax.axis_size("rows")
    return lax.ppermute(cells, "rows", [(i, (i + steps * line) % count) for i in range(count)])


def small_product(left, right):
    return jnp.dot(left, right, preferred_element_type=f32)


vmem = pl.BlockSpec(memory_space=pltpu.VMEM)
smem = pl.BlockSpec(memory_space=pltpu.SMEM)
hbm = pl.BlockSpec(memory_space=pltpu.HBM)


def call(kernel, shapes, in_specs, scratch, *operands, bytes_accessed=2**20, flops=0):
    return pl.pallas_call(
        kernel,
        out_shape=[jax.ShapeDtypeStruct(*shape) for shape in shapes],
        in_specs=in_specs,
        out_specs=[vmem] * len(shapes),
        scratch_shapes=scratch,
        compiler_params=pltpu.CompilerParams(vmem_limit_bytes=12 * 2**20),
        cost_estimate=pl.CostEstimate(
            flops=flops, bytes_accessed=bytes_accessed, transcendentals=0
        ),
    )(*operands)


def within_rows(size_ref, cells):
    blocks = size_ref.shape[0]
    size = cells.shape[0] // blocks
    within = lax.broadcasted_iota(jnp.int32, (size, cells.shape[1]), 0)
    parts = [
        jnp.where(within < size_ref[b], cells[b * size : (b + 1) * size], 0.0)
        for b in range(blocks)
    ]
    return jnp.concatenate(parts, axis=0)


def turn_kernel(
    rows, place_ref, links_ref, live_ref, coeffs_ref, ops_ref, own_ref, far_ref, gated_ref
):
    core = place_ref[1]
    lanes = 128
    live = live_ref[...] > 0
    for start in range(0, coeffs_ref.shape[1], lanes):
        cells = coeffs_ref[:, start : start + lanes].astype(f32).T
        for offset in range(0, lanes, CORES * rows):
            first = cells[offset : offset + rows]
            second = cells[offset + rows : offset + 2 * rows]
            where = pl.ds((start + offset) // CORES, rows)
            own = jnp.where(core == 0, first, second)
            far = jnp.where(core == 0, second, first)
            own_ref[where, :] = jnp.where(live, own, 0.0).astype(bf16)
            far_ref[where, :] = jnp.where(live, far, 0.0).astype(bf16)
    phases, blocks, span, size, _ = ops_ref.shape
    for b in range(blocks):
        for t in range(span):
            link = links_ref[b, t] != 0
            for p in range(phases):
                cells = jnp.where(link, ops_ref[p, b, t].astype(f32), 0.0)
                gated_ref[p, b, :, t * size : (t + 1) * size] = cells.astype(bf16)


def applied_kernel(up_ref, cols_ref, down_ref, gated_ref, out_ref, diag_ref):
    phases, blocks, size, depth = gated_ref.shape
    width = cols_ref.shape[1]
    padded = jnp.concatenate([up_ref[...], cols_ref[...], down_ref[...]], axis=0)
    first = up_ref.shape[0] - (depth // size - 1) // 2 * size
    own = cols_ref[...].astype(f32)
    for p in range(phases):
        parts = []
        for b in range(blocks):
            start = first + b * size
            parts.append(small_product(gated_ref[p, b], padded[start : start + depth]))
        total = jnp.concatenate(parts, axis=0).astype(bf16)
        out_ref[:, p * width : (p + 1) * width] = total
        sums = jnp.sum(total.astype(f32) * own, axis=0, keepdims=True)
        diag_ref[:, p * width : (p + 1) * width] = sums


def product_kernel(
    place_ref, own_ref, far_ref, applied_ref, far_applied_ref, up_ref, down_ref, own_diag_ref,
    one_ref, three_ref, two_ref, none_ref, diag_ref,
):
    x, core = place_ref[0], place_ref[1]
    rows, both = none_ref.shape
    width = both // 2
    near = up_ref.shape[0] - far_applied_ref.shape[0]
    up = up_ref[near:, :].astype(f32)
    cols = jnp.where(core == 0, down_ref[: far_applied_ref.shape[0], :].astype(f32), up)
    sums = [
        jnp.sum(
            cols * far_applied_ref[:, p * width : (p + 1) * width].astype(f32),
            axis=0,
            keepdims=True,
        )
        for p in range(2)
    ]
    diag = own_diag_ref[...] + jnp.concatenate(sums, axis=1)
    diag_ref[...] = diag
    high = diag.astype(bf16).astype(f32)
    fill = jnp.zeros((two_ref.shape[0] - rows - 2, both), f32)
    tail = jnp.concatenate([high, diag - high, fill], axis=0).astype(bf16)
    for steps, out_ref in ((2, two_ref), (1, one_ref), (3, three_ref), (0, none_ref)):
        start = pl.multiple_of(lax.rem(x + steps, XS) * rows, rows)
        total = small_product(own_ref[pl.ds(start, rows), :], applied_ref[...])
        total = total + small_product(far_ref[pl.ds(start, rows), :], far_applied_ref[...])
        out_ref[:rows, :] = total.astype(out_ref.dtype)
        if steps:
            out_ref[rows:, :] = tail


def sum_kernel(got_ref, rotation_ref, block_ref, z_ref, packed_ref):
    count, _, wide = z_ref.shape
    total = got_ref[0].astype(f32)
    for i in range(1, count):
        total = total + got_ref[i].astype(f32)
    block = total[:, :wide]
    block_ref[...] = block
    half = block.astype(bf16)
    diag = total[:4, wide:] + total[4:8, wide:]
    high = diag.astype(bf16).astype(f32)
    fill = jnp.zeros((block.shape[0] - 8, 128), f32)
    tail = jnp.concatenate([high, diag - high, fill], axis=0).astype(bf16)
    packed = jnp.concatenate([half, rotation_ref[...].astype(bf16), tail], axis=1)
    for i in range(count):
        z_ref[i] = half
        packed_ref[i] = packed


def gathered(place_ref, own_ref, away_ref, out_ref, sems):
    x, core = place_ref[0], place_ref[1]
    copies = []
    for source in range(XS):
        steps = lax.rem(x + XS - source, XS)
        pairs = ((own_ref, core), (away_ref, 1 - core))
        copies.append(
            [
                pltpu.make_async_copy(
                    ref.at[steps], out_ref.at[source, :, which], sems.at[source, i]
                )
                for i, (ref, which) in enumerate(pairs)
            ]
        )
    for pair in copies:
        for copy in pair:
            copy.start()
    return copies


def landed(copies, k):
    if k * XS % COLS == 0:
        for copy in copies[k * XS // COLS]:
            copy.wait()


def chunk(panel_ref, k):
    per = ZS * XS // COLS
    cells = panel_ref[k * per // ZS, pl.ds(k * per % ZS, per)]
    return cells.reshape(-1, cells.shape[-1])


def square_kernel(
    scale, place_ref, across_ref, block_ref, own_ref, away_ref,
    base_ref, sent_ref, step_ref, z_ref, rows_ref, diag_ref, turned_ref, sems,
):
    copies = gathered(place_ref, own_ref, away_ref, z_ref, sems)
    mine, low, col = place_ref[2], place_ref[3], place_ref[4]
    rows, width = rows_ref.shape[1:]
    terms = across_ref[:, :, -128:].astype(f32)
    per = width // 128
    for p in range(2):
        parts = [terms[:, p * per + h] + terms[:, 2 * per + p * per + h] for h in range(per)]
        diag_ref[p] = jnp.concatenate(parts, axis=1)
        turned_ref[p] = diag_ref[p].T
    lane = lax.broadcasted_iota(jnp.int32, (rows, COLS), 1)
    down = [
        jnp.sum(
            jnp.where(lane == mine, turned_ref[p, pl.ds(low, rows), :], 0.0),
            axis=1,
            keepdims=True,
        )
        for p in range(2)
    ]
    for k in range(COLS):
        cells = across_ref[k].astype(f32)
        cos_part = cells[:, :width] * (diag_ref[0, k : k + 1, :] - down[0])
        sin_part = cells[:, width : 2 * width] * (diag_ref[1, k : k + 1, :] - down[1])
        rows_ref[k] = (cos_part + sin_part) * scale
    across_diag = [diag_ref[p, pl.ds(col, 1), :] for p in range(2)]
    square = jnp.zeros((rows, width), f32)
    base = block_ref[...]
    for k in range(COLS):
        landed(copies, k)
        near = rows_ref[k].astype(bf16)
        panel = chunk(z_ref, k)
        base = base - small_product(near, panel)
        cells = panel.astype(f32)
        cos_part = cells[:, :width] * (across_diag[0] - turned_ref[0, :, k : k + 1])
        sin_part = cells[:, width:] * (across_diag[1] - turned_ref[1, :, k : k + 1])
        cells = ((cos_part + sin_part) * scale).astype(bf16)
        square = square + small_product(near, cells)
    base_ref[...] = base
    step = (rows_ref[col] + 0.5 * square).astype(bf16)
    for k in range(step_ref.shape[0]):
        step_ref[k] = step
    square = square.astype(bf16)
    for k in range(COLS):
        panel = chunk(z_ref, k)
        for p in range(2):
            cells = lax.dot_general(
                square,
                panel[:, p * width : (p + 1) * width],
                (((1,), (1,)), ((), ())),
                preferred_element_type=f32,
            )
            sent_ref[k, :, p * width : (p + 1) * width] = cells.astype(bf16)


def half_kernel(got_ref, base_ref, half_ref, sent_ref):
    total = got_ref[0].astype(f32)
    for k in range(1, COLS):
        total = total + got_ref[k].astype(f32)
    total = base_ref[...] + 0.5 * total
    half_ref[...] = total
    sent = total.astype(bf16)
    for k in range(COLS):
        sent_ref[k] = sent


def pieces_of(place_ref, refs, step_ref, sems):
    copies = [
        pltpu.make_async_copy(ref, step_ref.at[steps], sems.at[steps])
        for steps, ref in enumerate(refs)
    ]
    for copy in copies:
        copy.start()
    width = step_ref.shape[-1]
    per = COLS // XS
    count = step_ref.shape[1] // per
    for steps in range(XS):
        copies[steps].wait()
        source = lax.rem(place_ref[0] + XS - steps, XS)
        for part in range(per):
            first = z_order.index(part * ZS // per) * CORES
            cells = step_ref[steps, first : first + count]
            yield source * per + part, cells.reshape(-1, width)


def orbitals_kernel(
    place_ref, size_ref, across_ref, coeffs_ref, rotation_ref, own0, own1, own2, own3,
    rotated_ref, orbitals_ref, step_ref, sems,
):
    width = rotated_ref.shape[1]
    rotated = rotation_ref[...]
    start = pl.multiple_of(place_ref[4] * width, width)
    orbitals = coeffs_ref[:, pl.ds(start, width)].astype(f32)
    for k, step in pieces_of(place_ref, (own0, own1, own2, own3), step_ref, sems):
        rotated = rotated + small_product(across_ref[k, :, 2 * width : 3 * width], step)
        cells = coeffs_ref[:, pl.ds(pl.multiple_of(k * width, width), width)]
        orbitals = orbitals + small_product(cells, step)
    rotated_ref[...] = rotated
    orbitals_ref[...] = within_rows(size_ref, orbitals).astype(bf16)


def phases_kernel(
    place_ref, half_ref, block_ref, own0, own1, own2, own3, cos_ref, sin_ref, step_ref, sems
):
    width = cos_ref.shape[1]
    cos_part, sin_part = block_ref[:, :width], block_ref[:, width:]
    for k, step in pieces_of(place_ref, (own0, own1, own2, own3), step_ref, sems):
        where = sum(jnp.where(k == col, i, 0) for i, col in enumerate(col_order))
        cells = half_ref[where]
        cos_part = cos_part + small_product(cells[:, :width], step)
        sin_part = sin_part + small_product(cells[:, width:], step)
    cos_ref[...] = cos_part
    sin_ref[...] = sin_part


def on_device(coeffs, rotation, phase_ops, block_links, atom_size):
    rows_dev, orbital_count = coeffs.shape
    span_blocks, block_size = phase_ops.shape[2:4]
    reach_blocks = (span_blocks - 1) // 2
    rows_axis = lax.axis_size("rows")
    cols_axis = lax.axis_size("cols")
    row_count = orbital_count // rows_axis
    col_count = orbital_count // cols_axis
    both = 2 * col_count
    core = lax.axis_index("rows") % CORES
    own_x = lax.axis_index("rows") // (ZS * CORES)
    per_col = rows_axis // cols_axis
    own_row = lax.axis_index("rows")
    place = [own_x, core, own_row // per_col, own_row % per_col * row_count]
    place = jnp.stack(place + [lax.axis_index("cols")]).astype(jnp.int32)
    scale_factor = 0.125 / math.sqrt(orbital_count)

    within = lax.broadcasted_iota(jnp.int32, (rows_dev // block_size, block_size), 1)
    live_rows = (within < atom_size[:, None]).reshape(rows_dev)
    own_cols = lax.dynamic_slice_in_dim(coeffs, lax.axis_index("cols") * col_count, col_count, 1)
    own_cols = jnp.where(live_rows[:, None], own_cols, jnp.zeros_like(own_cols))
    width = reach_blocks * block_size
    up = [(i, (i + 1) % rows_axis) for i in range(rows_axis)]
    down = [((i + 1) % rows_axis, i) for i in range(rows_axis)]
    from_up = lax.ppermute(own_cols[rows_dev - width :], "rows", up)
    from_down = lax.ppermute(own_cols[:width], "rows", down)
    turn_coeffs, own_cols, live_rows = lax.optimization_barrier((coeffs, own_cols, live_rows))
    half_shape = ((orbital_count // CORES, rows_dev), bf16)
    phases, blocks = phase_ops.shape[:2]
    own_turned, far_turned, gated = call(
        functools.partial(turn_kernel, row_count),
        [half_shape] * 2 + [((phases, blocks, block_size, span_blocks * block_size), bf16)],
        [smem] * 2 + [vmem] * 3,
        [],
        place,
        block_links,
        live_rows.astype(f32)[None, :],
        turn_coeffs,
        phase_ops,
        bytes_accessed=2**26,
    )
    from_up, from_down, far_turned = lax.optimization_barrier((from_up, from_down, far_turned))
    far_turned = other_core(far_turned)
    applied, own_diag = call(
        applied_kernel,
        [((rows_dev, both), bf16), ((1, both), f32)],
        [vmem] * 4,
        [],
        from_up,
        own_cols,
        from_down,
        gated,
        bytes_accessed=2**22,
    )
    far_applied = other_core(applied)

    plane = ZS * row_count
    sent = ((plane + 16, both), bf16)
    one, three, two, chip, diag = call(
        product_kernel,
        [sent, sent, sent, ((plane, both), f32), ((1, both), f32)],
        [smem] + [vmem] * 7,
        [],
        place,
        own_turned,
        far_turned,
        applied,
        far_applied,
        from_up,
        from_down,
        own_diag,
    )
    got = [along_x(two, 2), along_x(one, 1), along_x(three, 3)]
    got = [cells.astype(f32) for cells in got]
    chip = chip + sum(cells[:plane] for cells in got)
    diag = diag[0] + sum(cells[plane] + cells[plane + 1] for cells in got)
    high = lax.reduce_precision(diag, 8, 7)
    terms = jnp.stack([high, diag - high]).astype(bf16).reshape(-1, 128)
    terms = jnp.pad(terms, ((0, row_count - terms.shape[0]), (0, 0)))
    terms = jnp.broadcast_to(terms[None], (ZS, row_count, 128))
    pieces = chip.astype(bf16).reshape(ZS, row_count, both)
    got = swap(jnp.concatenate([pieces, terms], axis=2), "rows", z_groups)
    z_block, z_sent, packed = call(
        sum_kernel,
        [
            ((row_count, both), f32),
            ((ZS, row_count, both), bf16),
            ((COLS, row_count, both + col_count + 128), bf16),
        ],
        [vmem] * 2,
        [],
        got,
        rotation,
    )

    panel = swap(z_sent, "rows", z_groups)
    packed, panel = lax.optimization_barrier((packed, panel))
    panels = [panel] + [along_x(panel, steps) for steps in (1, 2, 3)]
    across = swap(packed, "cols")
    stacked, across = lax.optimization_barrier((jnp.stack(panels), across))
    away = other_core(stacked)
    block = (row_count, col_count)
    base, square, step = call(
        functools.partial(square_kernel, scale_factor),
        [
            ((row_count, both), f32),
            ((COLS, row_count, both), bf16),
            ((ZS * CORES,) + block, bf16),
        ],
        [smem] + [vmem] * 2 + [hbm] * 2,
        [
            pltpu.VMEM((XS, ZS, CORES, row_count, both), bf16),
            pltpu.VMEM((COLS,) + block, f32),
            pltpu.VMEM((2, COLS, col_count), f32),
            pltpu.VMEM((2, col_count, COLS), f32),
            pltpu.SemaphoreType.DMA((XS, 2)),
        ],
        place,
        across,
        z_block,
        stacked,
        away,
    )

    step = swap(step, "rows", plane_groups)
    square, step = lax.optimization_barrier((square, step))
    steps_x = [step] + [along_x(step, steps) for steps in (1, 2, 3)]
    square = swap(square, "cols")
    half_block, half_sent = call(
        half_kernel,
        [((row_count, both), f32), ((COLS, row_count, both), bf16)],
        [vmem] * 2,
        [],
        square,
        base,
        flops=2**35,
    )
    half_rows = swap(half_sent, "cols", [col_order])
    panel_scratch = [
        pltpu.VMEM((XS, ZS * CORES) + block, bf16),
        pltpu.SemaphoreType.DMA((XS,)),
    ]
    rotated, orbitals = call(
        orbitals_kernel,
        [(block, f32), ((rows_dev, col_count), bf16)],
        [smem] * 2 + [vmem] * 3 + [hbm] * XS,
        panel_scratch,
        place,
        atom_size,
        across,
        coeffs,
        rotation,
        *steps_x,
        flops=2**32,
    )
    phase_cos, phase_sin = call(
        phases_kernel,
        [(block, f32)] * 2,
        [smem] + [vmem] * 2 + [hbm] * XS,
        panel_scratch,
        place,
        half_rows,
        half_block,
        *steps_x,
    )
    return (rotated, phase_cos, phase_sin, orbitals)


def solution(mesh):
    placed = (
        P("rows", None),
        P("rows", "cols"),
        P(None, "rows", None, None, None),
        P("rows", None),
        P("rows"),
    )
    return jax.shard_map(
        on_device,
        mesh=mesh,
        in_specs=placed,
        out_specs=(P("rows", "cols"), P("rows", "cols"), P("rows", "cols"), P("rows", "cols")),
        check_vma=False,
    )
```

```python
import functools
import math

import jax
import jax.numpy as jnp
from jax import lax
from jax.experimental import pallas as pl
from jax.experimental.pallas import tpu as pltpu
from jax.sharding import PartitionSpec as P

bf16 = jnp.bfloat16
f32 = jnp.float32

XS, ZS, CORES, COLS = 4, 8, 2, 8


def row_index(x, z, core):
    return (x * ZS + z) * CORES + core


z_groups = [[row_index(x, z, k) for z in range(ZS)] for x in range(XS) for k in range(CORES)]
z_order = [4, 5, 6, 7, 0, 1, 2, 3]
col_order = [4, 5, 6, 7, 3, 2, 1, 0]
plane_groups = [[row_index(x, z, k) for z in z_order for k in range(CORES)] for x in range(XS)]


def swap(cells, axis, groups=None):
    return lax.all_to_all(cells, axis, 0, 0, tiled=True, axis_index_groups=groups)


def other_core(cells):
    count = lax.axis_size("rows")
    return lax.ppermute(cells, "rows", [(i, i ^ 1) for i in range(count)])


def along_x(cells, steps):
    line, count = ZS * CORES, lax.axis_size("rows")
    return lax.ppermute(cells, "rows", [(i, (i + steps * line) % count) for i in range(count)])


def small_product(left, right):
    return jnp.dot(left, right, preferred_element_type=f32)


vmem = pl.BlockSpec(memory_space=pltpu.VMEM)
smem = pl.BlockSpec(memory_space=pltpu.SMEM)
hbm = pl.BlockSpec(memory_space=pltpu.HBM)


def call(kernel, shapes, in_specs, scratch, *operands, bytes_accessed=2**20, flops=0):
    return pl.pallas_call(
        kernel,
        out_shape=[jax.ShapeDtypeStruct(*shape) for shape in shapes],
        in_specs=in_specs,
        out_specs=[vmem] * len(shapes),
        scratch_shapes=scratch,
        compiler_params=pltpu.CompilerParams(vmem_limit_bytes=12 * 2**20),
        cost_estimate=pl.CostEstimate(
            flops=flops, bytes_accessed=bytes_accessed, transcendentals=0
        ),
    )(*operands)


def within_rows(size_ref, cells):
    blocks = size_ref.shape[0]
    size = cells.shape[0] // blocks
    within = lax.broadcasted_iota(jnp.int32, (size, cells.shape[1]), 0)
    parts = [
        jnp.where(within < size_ref[b], cells[b * size : (b + 1) * size], 0.0)
        for b in range(blocks)
    ]
    return jnp.concatenate(parts, axis=0)


def turn_kernel(
    rows, place_ref, links_ref, live_ref, coeffs_ref, ops_ref, own_ref, far_ref, gated_ref
):
    core = place_ref[1]
    lanes = 128
    live = live_ref[...] > 0
    for start in range(0, coeffs_ref.shape[1], lanes):
        cells = coeffs_ref[:, start : start + lanes].astype(f32).T
        for offset in range(0, lanes, CORES * rows):
            first = cells[offset : offset + rows]
            second = cells[offset + rows : offset + 2 * rows]
            where = pl.ds((start + offset) // CORES, rows)
            own = jnp.where(core == 0, first, second)
            far = jnp.where(core == 0, second, first)
            own_ref[where, :] = jnp.where(live, own, 0.0).astype(bf16)
            far_ref[where, :] = jnp.where(live, far, 0.0).astype(bf16)
    phases, blocks, span, size, _ = ops_ref.shape
    for b in range(blocks):
        for t in range(span):
            link = links_ref[b, t] != 0
            for p in range(phases):
                cells = jnp.where(link, ops_ref[p, b, t].astype(f32), 0.0)
                gated_ref[p, b, :, t * size : (t + 1) * size] = cells.astype(bf16)


def applied_kernel(up_ref, cols_ref, down_ref, gated_ref, out_ref, diag_ref):
    phases, blocks, size, depth = gated_ref.shape
    width = cols_ref.shape[1]
    padded = jnp.concatenate([up_ref[...], cols_ref[...], down_ref[...]], axis=0)
    first = up_ref.shape[0] - (depth // size - 1) // 2 * size
    own = cols_ref[...].astype(f32)
    for p in range(phases):
        parts = []
        for b in range(blocks):
            start = first + b * size
            parts.append(small_product(gated_ref[p, b], padded[start : start + depth]))
        total = jnp.concatenate(parts, axis=0).astype(bf16)
        out_ref[:, p * width : (p + 1) * width] = total
        sums = jnp.sum(total.astype(f32) * own, axis=0, keepdims=True)
        diag_ref[:, p * width : (p + 1) * width] = sums


def product_kernel(
    place_ref, own_ref, far_ref, applied_ref, far_applied_ref, up_ref, down_ref, own_diag_ref,
    one_ref, three_ref, two_ref, none_ref, diag_ref,
):
    x, core = place_ref[0], place_ref[1]
    rows, both = none_ref.shape
    width = both // 2
    near = up_ref.shape[0] - far_applied_ref.shape[0]
    up = up_ref[near:, :].astype(f32)
    cols = jnp.where(core == 0, down_ref[: far_applied_ref.shape[0], :].astype(f32), up)
    sums = [
        jnp.sum(
            cols * far_applied_ref[:, p * width : (p + 1) * width].astype(f32),
            axis=0,
            keepdims=True,
        )
        for p in range(2)
    ]
    diag = own_diag_ref[...] + jnp.concatenate(sums, axis=1)
    diag_ref[...] = diag
    high = diag.astype(bf16).astype(f32)
    fill = jnp.zeros((two_ref.shape[0] - rows - 2, both), f32)
    tail = jnp.concatenate([high, diag - high, fill], axis=0).astype(bf16)
    for steps, out_ref in ((2, two_ref), (1, one_ref), (3, three_ref), (0, none_ref)):
        start = pl.multiple_of(lax.rem(x + steps, XS) * rows, rows)
        total = small_product(own_ref[pl.ds(start, rows), :], applied_ref[...])
        total = total + small_product(far_ref[pl.ds(start, rows), :], far_applied_ref[...])
        out_ref[:rows, :] = total.astype(out_ref.dtype)
        if steps:
            out_ref[rows:, :] = tail


def sum_kernel(got_ref, rotation_ref, block_ref, z_ref, packed_ref):
    count, _, wide = z_ref.shape
    total = got_ref[0].astype(f32)
    for i in range(1, count):
        total = total + got_ref[i].astype(f32)
    block = total[:, :wide]
    block_ref[...] = block
    half = block.astype(bf16)
    diag = total[:4, wide:] + total[4:8, wide:]
    high = diag.astype(bf16).astype(f32)
    fill = jnp.zeros((block.shape[0] - 8, 128), f32)
    tail = jnp.concatenate([high, diag - high, fill], axis=0).astype(bf16)
    packed = jnp.concatenate([half, rotation_ref[...].astype(bf16), tail], axis=1)
    for i in range(count):
        z_ref[i] = half
        packed_ref[i] = packed


def gathered(place_ref, own_ref, away_ref, out_ref, sems):
    x, core = place_ref[0], place_ref[1]
    copies = []
    for source in range(XS):
        steps = lax.rem(x + XS - source, XS)
        pairs = ((own_ref, core), (away_ref, 1 - core))
        copies.append(
            [
                pltpu.make_async_copy(
                    ref.at[steps], out_ref.at[source, :, which], sems.at[source, i]
                )
                for i, (ref, which) in enumerate(pairs)
            ]
        )
    for pair in copies:
        for copy in pair:
            copy.start()
    return copies


def landed(copies, k):
    if k * XS % COLS == 0:
        for copy in copies[k * XS // COLS]:
            copy.wait()


def chunk(panel_ref, k):
    per = ZS * XS // COLS
    cells = panel_ref[k * per // ZS, pl.ds(k * per % ZS, per)]
    return cells.reshape(-1, cells.shape[-1])


def square_kernel(
    scale, place_ref, across_ref, block_ref, own_ref, away_ref,
    base_ref, sent_ref, step_ref, z_ref, rows_ref, diag_ref, turned_ref, sems,
):
    copies = gathered(place_ref, own_ref, away_ref, z_ref, sems)
    mine, low, col = place_ref[2], place_ref[3], place_ref[4]
    rows, width = rows_ref.shape[1:]
    terms = across_ref[:, :, -128:].astype(f32)
    per = width // 128
    for p in range(2):
        parts = [terms[:, p * per + h] + terms[:, 2 * per + p * per + h] for h in range(per)]
        diag_ref[p] = jnp.concatenate(parts, axis=1)
        turned_ref[p] = diag_ref[p].T
    lane = lax.broadcasted_iota(jnp.int32, (rows, COLS), 1)
    down = [
        jnp.sum(
            jnp.where(lane == mine, turned_ref[p, pl.ds(low, rows), :], 0.0),
            axis=1,
            keepdims=True,
        )
        for p in range(2)
    ]
    for k in range(COLS):
        cells = across_ref[k].astype(f32)
        cos_part = cells[:, :width] * (diag_ref[0, k : k + 1, :] - down[0])
        sin_part = cells[:, width : 2 * width] * (diag_ref[1, k : k + 1, :] - down[1])
        rows_ref[k] = (cos_part + sin_part) * scale
    across_diag = [diag_ref[p, pl.ds(col, 1), :] for p in range(2)]
    square = jnp.zeros((rows, width), f32)
    base = block_ref[...]
    for k in range(COLS):
        landed(copies, k)
        near = rows_ref[k].astype(bf16)
        panel = chunk(z_ref, k)
        base = base - small_product(near, panel)
        cells = panel.astype(f32)
        cos_part = cells[:, :width] * (across_diag[0] - turned_ref[0, :, k : k + 1])
        sin_part = cells[:, width:] * (across_diag[1] - turned_ref[1, :, k : k + 1])
        cells = ((cos_part + sin_part) * scale).astype(bf16)
        square = square + small_product(near, cells)
    base_ref[...] = base
    step = (rows_ref[col] + 0.5 * square).astype(bf16)
    for k in range(step_ref.shape[0]):
        step_ref[k] = step
    square = square.astype(bf16)
    for k in range(COLS):
        panel = chunk(z_ref, k)
        for p in range(2):
            cells = lax.dot_general(
                square,
                panel[:, p * width : (p + 1) * width],
                (((1,), (1,)), ((), ())),
                preferred_element_type=f32,
            )
            sent_ref[k, :, p * width : (p + 1) * width] = cells.astype(bf16)


def half_kernel(got_ref, base_ref, half_ref, sent_ref):
    total = got_ref[0].astype(f32)
    for k in range(1, COLS):
        total = total + got_ref[k].astype(f32)
    total = base_ref[...] + 0.5 * total
    half_ref[...] = total
    sent = total.astype(bf16)
    for k in range(COLS):
        sent_ref[k] = sent


def pieces_of(place_ref, refs, step_ref, sems):
    copies = [
        pltpu.make_async_copy(ref, step_ref.at[steps], sems.at[steps])
        for steps, ref in enumerate(refs)
    ]
    for copy in copies:
        copy.start()
    width = step_ref.shape[-1]
    per = COLS // XS
    count = step_ref.shape[1] // per
    for steps in range(XS):
        copies[steps].wait()
        source = lax.rem(place_ref[0] + XS - steps, XS)
        for part in range(per):
            first = z_order.index(part * ZS // per) * CORES
            cells = step_ref[steps, first : first + count]
            yield source * per + part, cells.reshape(-1, width)


def orbitals_kernel(
    place_ref, size_ref, across_ref, coeffs_ref, rotation_ref, own0, own1, own2, own3,
    rotated_ref, orbitals_ref, step_ref, sems,
):
    width = rotated_ref.shape[1]
    rotated = rotation_ref[...]
    start = pl.multiple_of(place_ref[4] * width, width)
    orbitals = coeffs_ref[:, pl.ds(start, width)].astype(f32)
    for k, step in pieces_of(place_ref, (own0, own1, own2, own3), step_ref, sems):
        rotated = rotated + small_product(across_ref[k, :, 2 * width : 3 * width], step)
        cells = coeffs_ref[:, pl.ds(pl.multiple_of(k * width, width), width)]
        orbitals = orbitals + small_product(cells, step)
    rotated_ref[...] = rotated
    orbitals_ref[...] = within_rows(size_ref, orbitals).astype(bf16)


def phases_kernel(
    place_ref, half_ref, block_ref, own0, own1, own2, own3, cos_ref, sin_ref, step_ref, sems
):
    width = cos_ref.shape[1]
    cos_part, sin_part = block_ref[:, :width], block_ref[:, width:]
    for k, step in pieces_of(place_ref, (own0, own1, own2, own3), step_ref, sems):
        where = sum(jnp.where(k == col, i, 0) for i, col in enumerate(col_order))
        cells = half_ref[where]
        cos_part = cos_part + small_product(cells[:, :width], step)
        sin_part = sin_part + small_product(cells[:, width:], step)
    cos_ref[...] = cos_part
    sin_ref[...] = sin_part


def on_device(coeffs, rotation, phase_ops, block_links, atom_size):
    rows_dev, orbital_count = coeffs.shape
    span_blocks, block_size = phase_ops.shape[2:4]
    reach_blocks = (span_blocks - 1) // 2
    rows_axis = lax.axis_size("rows")
    cols_axis = lax.axis_size("cols")
    row_count = orbital_count // rows_axis
    col_count = orbital_count // cols_axis
    both = 2 * col_count
    core = lax.axis_index("rows") % CORES
    own_x = lax.axis_index("rows") // (ZS * CORES)
    per_col = rows_axis // cols_axis
    own_row = lax.axis_index("rows")
    place = [own_x, core, own_row // per_col, own_row % per_col * row_count]
    place = jnp.stack(place + [lax.axis_index("cols")]).astype(jnp.int32)
    scale_factor = 0.125 / math.sqrt(orbital_count)

    within = lax.broadcasted_iota(jnp.int32, (rows_dev // block_size, block_size), 1)
    live_rows = (within < atom_size[:, None]).reshape(rows_dev)
    own_cols = lax.dynamic_slice_in_dim(coeffs, lax.axis_index("cols") * col_count, col_count, 1)
    own_cols = jnp.where(live_rows[:, None], own_cols, jnp.zeros_like(own_cols))
    width = reach_blocks * block_size
    up = [(i, (i + 1) % rows_axis) for i in range(rows_axis)]
    down = [((i + 1) % rows_axis, i) for i in range(rows_axis)]
    from_up = lax.ppermute(own_cols[rows_dev - width :], "rows", up)
    from_down = lax.ppermute(own_cols[:width], "rows", down)
    turn_coeffs, own_cols, live_rows = lax.optimization_barrier((coeffs, own_cols, live_rows))
    half_shape = ((orbital_count // CORES, rows_dev), bf16)
    phases, blocks = phase_ops.shape[:2]
    own_turned, far_turned, gated = call(
        functools.partial(turn_kernel, row_count),
        [half_shape] * 2 + [((phases, blocks, block_size, span_blocks * block_size), bf16)],
        [smem] * 2 + [vmem] * 3,
        [],
        place,
        block_links,
        live_rows.astype(f32)[None, :],
        turn_coeffs,
        phase_ops,
        bytes_accessed=2**26,
    )
    from_down, from_up, far_turned = lax.optimization_barrier((from_down, from_up, far_turned))
    far_turned = other_core(far_turned)
    applied, own_diag = call(
        applied_kernel,
        [((rows_dev, both), bf16), ((1, both), f32)],
        [vmem] * 4,
        [],
        from_up,
        own_cols,
        from_down,
        gated,
        bytes_accessed=2**22,
    )
    far_applied = other_core(applied)

    plane = ZS * row_count
    sent = ((plane + 16, both), bf16)
    one, three, two, chip, diag = call(
        product_kernel,
        [sent, sent, sent, ((plane, both), f32), ((1, both), f32)],
        [smem] + [vmem] * 7,
        [],
        place,
        own_turned,
        far_turned,
        applied,
        far_applied,
        from_up,
        from_down,
        own_diag,
    )
    got = [along_x(two, 2), along_x(one, 1), along_x(three, 3)]
    got = [cells.astype(f32) for cells in got]
    chip = chip + sum(cells[:plane] for cells in got)
    diag = diag[0] + sum(cells[plane] + cells[plane + 1] for cells in got)
    high = lax.reduce_precision(diag, 8, 7)
    terms = jnp.stack([high, diag - high]).astype(bf16).reshape(-1, 128)
    terms = jnp.pad(terms, ((0, row_count - terms.shape[0]), (0, 0)))
    terms = jnp.broadcast_to(terms[None], (ZS, row_count, 128))
    pieces = chip.astype(bf16).reshape(ZS, row_count, both)
    got = swap(jnp.concatenate([pieces, terms], axis=2), "rows", z_groups)
    z_block, z_sent, packed = call(
        sum_kernel,
        [
            ((row_count, both), f32),
            ((ZS, row_count, both), bf16),
            ((COLS, row_count, both + col_count + 128), bf16),
        ],
        [vmem] * 2,
        [],
        got,
        rotation,
    )

    panel = swap(z_sent, "rows", z_groups)
    packed, panel = lax.optimization_barrier((packed, panel))
    panels = [panel] + [along_x(panel, steps) for steps in (1, 2, 3)]
    across = swap(packed, "cols")
    stacked, across = lax.optimization_barrier((jnp.stack(panels), across))
    away = other_core(stacked)
    block = (row_count, col_count)
    base, square, step = call(
        functools.partial(square_kernel, scale_factor),
        [
            ((row_count, both), f32),
            ((COLS, row_count, both), bf16),
            ((ZS * CORES,) + block, bf16),
        ],
        [smem] + [vmem] * 2 + [hbm] * 2,
        [
            pltpu.VMEM((XS, ZS, CORES, row_count, both), bf16),
            pltpu.VMEM((COLS,) + block, f32),
            pltpu.VMEM((2, COLS, col_count), f32),
            pltpu.VMEM((2, col_count, COLS), f32),
            pltpu.SemaphoreType.DMA((XS, 2)),
        ],
        place,
        across,
        z_block,
        stacked,
        away,
    )

    step = swap(step, "rows", plane_groups)
    square, step = lax.optimization_barrier((square, step))
    steps_x = [step] + [along_x(step, steps) for steps in (1, 2, 3)]
    square = swap(square, "cols")
    half_block, half_sent = call(
        half_kernel,
        [((row_count, both), f32), ((COLS, row_count, both), bf16)],
        [vmem] * 2,
        [],
        square,
        base,
        flops=2**35,
    )
    half_rows = swap(half_sent, "cols", [col_order])
    panel_scratch = [
        pltpu.VMEM((XS, ZS * CORES) + block, bf16),
        pltpu.SemaphoreType.DMA((XS,)),
    ]
    rotated, orbitals = call(
        orbitals_kernel,
        [(block, f32), ((rows_dev, col_count), bf16)],
        [smem] * 2 + [vmem] * 3 + [hbm] * XS,
        panel_scratch,
        place,
        atom_size,
        across,
        coeffs,
        rotation,
        *steps_x,
        flops=2**32,
    )
    phase_cos, phase_sin = call(
        phases_kernel,
        [(block, f32)] * 2,
        [smem] + [vmem] * 2 + [hbm] * XS,
        panel_scratch,
        place,
        half_rows,
        half_block,
        *steps_x,
    )
    return (rotated, phase_cos, phase_sin, orbitals)


def solution(mesh):
    placed = (
        P("rows", None),
        P("rows", "cols"),
        P(None, "rows", None, None, None),
        P("rows", None),
        P("rows"),
    )
    return jax.shard_map(
        on_device,
        mesh=mesh,
        in_specs=placed,
        out_specs=(P("rows", "cols"), P("rows", "cols"), P("rows", "cols"), P("rows", "cols")),
        check_vma=False,
    )
```

```python
import functools
import math

import jax
import jax.numpy as jnp
from jax import lax
from jax.experimental import pallas as pl
from jax.experimental.pallas import tpu as pltpu
from jax.sharding import PartitionSpec as P

bf16 = jnp.bfloat16
f32 = jnp.float32

XS, ZS, CORES, COLS = 4, 8, 2, 8


def row_index(x, z, core):
    return (x * ZS + z) * CORES + core


z_groups = [[row_index(x, z, k) for z in range(ZS)] for x in range(XS) for k in range(CORES)]
z_order = [4, 5, 6, 7, 0, 1, 2, 3]
col_order = [4, 5, 6, 7, 3, 2, 1, 0]
plane_groups = [[row_index(x, z, k) for z in z_order for k in range(CORES)] for x in range(XS)]


def swap(cells, axis, groups=None):
    return lax.all_to_all(cells, axis, 0, 0, tiled=True, axis_index_groups=groups)


def other_core(cells):
    count = lax.axis_size("rows")
    return lax.ppermute(cells, "rows", [(i, i ^ 1) for i in range(count)])


def along_x(cells, steps):
    line, count = ZS * CORES, lax.axis_size("rows")
    return lax.ppermute(cells, "rows", [(i, (i + steps * line) % count) for i in range(count)])


def small_product(left, right):
    return jnp.dot(left, right, preferred_element_type=f32)


vmem = pl.BlockSpec(memory_space=pltpu.VMEM)
smem = pl.BlockSpec(memory_space=pltpu.SMEM)


def call(kernel, shapes, in_specs, scratch, *operands, bytes_accessed=2**20, flops=0):
    return pl.pallas_call(
        kernel,
        out_shape=[jax.ShapeDtypeStruct(*shape) for shape in shapes],
        in_specs=in_specs,
        out_specs=[vmem] * len(shapes),
        scratch_shapes=scratch,
        compiler_params=pltpu.CompilerParams(vmem_limit_bytes=12 * 2**20),
        cost_estimate=pl.CostEstimate(
            flops=flops, bytes_accessed=bytes_accessed, transcendentals=0
        ),
    )(*operands)


def within_rows(size_ref, cells):
    blocks = size_ref.shape[0]
    size = cells.shape[0] // blocks
    within = lax.broadcasted_iota(jnp.int32, (size, cells.shape[1]), 0)
    parts = [
        jnp.where(within < size_ref[b], cells[b * size : (b + 1) * size], 0.0)
        for b in range(blocks)
    ]
    return jnp.concatenate(parts, axis=0)


def turn_kernel(
    rows, place_ref, links_ref, live_ref, coeffs_ref, ops_ref, own_ref, far_ref, gated_ref
):
    core = place_ref[1]
    lanes = 128
    live = live_ref[...] > 0
    for start in range(0, coeffs_ref.shape[1], lanes):
        cells = coeffs_ref[:, start : start + lanes].astype(f32).T
        for offset in range(0, lanes, CORES * rows):
            first = cells[offset : offset + rows]
            second = cells[offset + rows : offset + 2 * rows]
            where = pl.ds((start + offset) // CORES, rows)
            own = jnp.where(core == 0, first, second)
            far = jnp.where(core == 0, second, first)
            own_ref[where, :] = jnp.where(live, own, 0.0).astype(bf16)
            far_ref[where, :] = jnp.where(live, far, 0.0).astype(bf16)
    phases, blocks, span, size, _ = ops_ref.shape
    for b in range(blocks):
        for t in range(span):
            link = links_ref[b, t] != 0
            for p in range(phases):
                cells = jnp.where(link, ops_ref[p, b, t].astype(f32), 0.0)
                gated_ref[p, b, :, t * size : (t + 1) * size] = cells.astype(bf16)


def applied_kernel(up_ref, cols_ref, down_ref, gated_ref, out_ref, diag_ref):
    phases, blocks, size, depth = gated_ref.shape
    width = cols_ref.shape[1]
    padded = jnp.concatenate([up_ref[...], cols_ref[...], down_ref[...]], axis=0)
    first = up_ref.shape[0] - (depth // size - 1) // 2 * size
    own = cols_ref[...].astype(f32)
    for p in range(phases):
        parts = []
        for b in range(blocks):
            start = first + b * size
            parts.append(small_product(gated_ref[p, b], padded[start : start + depth]))
        total = jnp.concatenate(parts, axis=0).astype(bf16)
        out_ref[:, p * width : (p + 1) * width] = total
        sums = jnp.sum(total.astype(f32) * own, axis=0, keepdims=True)
        diag_ref[:, p * width : (p + 1) * width] = sums


def product_kernel(
    place_ref, own_ref, far_ref, applied_ref, far_applied_ref, up_ref, down_ref, own_diag_ref,
    one_ref, three_ref, two_ref, none_ref, diag_ref,
):
    x, core = place_ref[0], place_ref[1]
    rows, both = none_ref.shape
    width = both // 2
    near = up_ref.shape[0] - far_applied_ref.shape[0]
    up = up_ref[near:, :].astype(f32)
    cols = jnp.where(core == 0, down_ref[: far_applied_ref.shape[0], :].astype(f32), up)
    sums = [
        jnp.sum(
            cols * far_applied_ref[:, p * width : (p + 1) * width].astype(f32),
            axis=0,
            keepdims=True,
        )
        for p in range(2)
    ]
    diag = own_diag_ref[...] + jnp.concatenate(sums, axis=1)
    diag_ref[...] = diag
    high = diag.astype(bf16).astype(f32)
    fill = jnp.zeros((two_ref.shape[0] - rows - 2, both), f32)
    tail = jnp.concatenate([high, diag - high, fill], axis=0).astype(bf16)
    for steps, out_ref in ((2, two_ref), (1, one_ref), (3, three_ref), (0, none_ref)):
        start = pl.multiple_of(lax.rem(x + steps, XS) * rows, rows)
        total = small_product(own_ref[pl.ds(start, rows), :], applied_ref[...])
        total = total + small_product(far_ref[pl.ds(start, rows), :], far_applied_ref[...])
        out_ref[:rows, :] = total.astype(out_ref.dtype)
        if steps:
            out_ref[rows:, :] = tail


def sum_kernel(got_ref, rotation_ref, block_ref, z_ref, packed_ref):
    count, _, wide = z_ref.shape
    total = got_ref[0].astype(f32)
    for i in range(1, count):
        total = total + got_ref[i].astype(f32)
    block = total[:, :wide]
    block_ref[...] = block
    half = block.astype(bf16)
    diag = total[:4, wide:] + total[4:8, wide:]
    high = diag.astype(bf16).astype(f32)
    fill = jnp.zeros((block.shape[0] - 8, 128), f32)
    tail = jnp.concatenate([high, diag - high, fill], axis=0).astype(bf16)
    packed = jnp.concatenate([half, rotation_ref[...].astype(bf16), tail], axis=1)
    for i in range(count):
        z_ref[i] = half
        packed_ref[i] = packed


def chunk(place_ref, own_ref, away_ref, k):
    core = place_ref[1]
    per = ZS * XS // COLS
    steps = lax.rem(place_ref[0] + XS - k * per // ZS, XS)
    parts = []
    for z in range(k * per % ZS, k * per % ZS + per):
        own, away = own_ref[steps, z], away_ref[steps, z]
        parts += [jnp.where(core == 0, own, away), jnp.where(core == 0, away, own)]
    return jnp.concatenate(parts, axis=0)


def square_kernel(
    scale, place_ref, across_ref, block_ref, own_ref, away_ref,
    base_ref, sent_ref, step_ref, rows_ref, diag_ref, turned_ref,
):
    mine, low, col = place_ref[2], place_ref[3], place_ref[4]
    rows, width = rows_ref.shape[1:]
    terms = across_ref[:, :, -128:].astype(f32)
    per = width // 128
    for p in range(2):
        parts = [terms[:, p * per + h] + terms[:, 2 * per + p * per + h] for h in range(per)]
        diag_ref[p] = jnp.concatenate(parts, axis=1)
        turned_ref[p] = diag_ref[p].T
    lane = lax.broadcasted_iota(jnp.int32, (rows, COLS), 1)
    down = [
        jnp.sum(
            jnp.where(lane == mine, turned_ref[p, pl.ds(low, rows), :], 0.0),
            axis=1,
            keepdims=True,
        )
        for p in range(2)
    ]
    for k in range(COLS):
        cells = across_ref[k].astype(f32)
        cos_part = cells[:, :width] * (diag_ref[0, k : k + 1, :] - down[0])
        sin_part = cells[:, width : 2 * width] * (diag_ref[1, k : k + 1, :] - down[1])
        rows_ref[k] = (cos_part + sin_part) * scale
    across_diag = [diag_ref[p, pl.ds(col, 1), :] for p in range(2)]
    square = jnp.zeros((rows, width), f32)
    base = block_ref[...]
    for k in range(COLS):
        near = rows_ref[k].astype(bf16)
        panel = chunk(place_ref, own_ref, away_ref, k)
        base = base - small_product(near, panel)
        cells = panel.astype(f32)
        cos_part = cells[:, :width] * (across_diag[0] - turned_ref[0, :, k : k + 1])
        sin_part = cells[:, width:] * (across_diag[1] - turned_ref[1, :, k : k + 1])
        cells = ((cos_part + sin_part) * scale).astype(bf16)
        square = square + small_product(near, cells)
    base_ref[...] = base
    step = (rows_ref[col] + 0.5 * square).astype(bf16)
    for k in range(step_ref.shape[0]):
        step_ref[k] = step
    square = square.astype(bf16)
    for k in range(COLS):
        panel = chunk(place_ref, own_ref, away_ref, k)
        for p in range(2):
            cells = lax.dot_general(
                square,
                panel[:, p * width : (p + 1) * width],
                (((1,), (1,)), ((), ())),
                preferred_element_type=f32,
            )
            sent_ref[k, :, p * width : (p + 1) * width] = cells.astype(bf16)


def half_kernel(got_ref, base_ref, half_ref, sent_ref):
    total = got_ref[0].astype(f32)
    for k in range(1, COLS):
        total = total + got_ref[k].astype(f32)
    total = base_ref[...] + 0.5 * total
    half_ref[...] = total
    sent = total.astype(bf16)
    for k in range(COLS):
        sent_ref[k] = sent


def pieces_of(place_ref, refs):
    width = refs[0].shape[-1]
    per = COLS // XS
    count = refs[0].shape[0] // per
    for steps, ref in enumerate(refs):
        source = lax.rem(place_ref[0] + XS - steps, XS)
        for part in range(per):
            first = z_order.index(part * ZS // per) * CORES
            yield source * per + part, ref[first : first + count].reshape(-1, width)


def orbitals_kernel(
    place_ref, size_ref, across_ref, coeffs_ref, rotation_ref, own0, own1, own2, own3,
    rotated_ref, orbitals_ref,
):
    width = rotated_ref.shape[1]
    rotated = rotation_ref[...]
    start = pl.multiple_of(place_ref[4] * width, width)
    orbitals = coeffs_ref[:, pl.ds(start, width)].astype(f32)
    for k, step in pieces_of(place_ref, (own0, own1, own2, own3)):
        rotated = rotated + small_product(across_ref[k, :, 2 * width : 3 * width], step)
        cells = coeffs_ref[:, pl.ds(pl.multiple_of(k * width, width), width)]
        orbitals = orbitals + small_product(cells, step)
    rotated_ref[...] = rotated
    orbitals_ref[...] = within_rows(size_ref, orbitals).astype(bf16)


def phases_kernel(
    place_ref, half_ref, block_ref, own0, own1, own2, own3, cos_ref, sin_ref
):
    width = cos_ref.shape[1]
    total = jnp.concatenate([block_ref[:, :width], block_ref[:, width:]], axis=0)
    for k, step in pieces_of(place_ref, (own0, own1, own2, own3)):
        where = sum(jnp.where(k == col, i, 0) for i, col in enumerate(col_order))
        cells = half_ref[where]
        cells = jnp.concatenate([cells[:, :width], cells[:, width:]], axis=0)
        total = total + small_product(cells, step)
    rows = cos_ref.shape[0]
    cos_ref[...] = total[:rows]
    sin_ref[...] = total[rows:]


def on_device(coeffs, rotation, phase_ops, block_links, atom_size):
    rows_dev, orbital_count = coeffs.shape
    span_blocks, block_size = phase_ops.shape[2:4]
    reach_blocks = (span_blocks - 1) // 2
    rows_axis = lax.axis_size("rows")
    cols_axis = lax.axis_size("cols")
    row_count = orbital_count // rows_axis
    col_count = orbital_count // cols_axis
    both = 2 * col_count
    core = lax.axis_index("rows") % CORES
    own_x = lax.axis_index("rows") // (ZS * CORES)
    per_col = rows_axis // cols_axis
    own_row = lax.axis_index("rows")
    place = [own_x, core, own_row // per_col, own_row % per_col * row_count]
    place = jnp.stack(place + [lax.axis_index("cols")]).astype(jnp.int32)
    scale_factor = 0.125 / math.sqrt(orbital_count)

    within = lax.broadcasted_iota(jnp.int32, (rows_dev // block_size, block_size), 1)
    live_rows = (within < atom_size[:, None]).reshape(rows_dev)
    own_cols = lax.dynamic_slice_in_dim(coeffs, lax.axis_index("cols") * col_count, col_count, 1)
    own_cols = jnp.where(live_rows[:, None], own_cols, jnp.zeros_like(own_cols))
    width = reach_blocks * block_size
    up = [(i, (i + 1) % rows_axis) for i in range(rows_axis)]
    down = [((i + 1) % rows_axis, i) for i in range(rows_axis)]
    from_up = lax.ppermute(own_cols[rows_dev - width :], "rows", up)
    from_down = lax.ppermute(own_cols[:width], "rows", down)
    turn_coeffs, own_cols, live_rows = lax.optimization_barrier((coeffs, own_cols, live_rows))
    half_shape = ((orbital_count // CORES, rows_dev), bf16)
    phases, blocks = phase_ops.shape[:2]
    own_turned, far_turned, gated = call(
        functools.partial(turn_kernel, row_count),
        [half_shape] * 2 + [((phases, blocks, block_size, span_blocks * block_size), bf16)],
        [smem] * 2 + [vmem] * 3,
        [],
        place,
        block_links,
        live_rows.astype(f32)[None, :],
        turn_coeffs,
        phase_ops,
        bytes_accessed=2**26,
    )
    from_down, from_up, far_turned = lax.optimization_barrier((from_down, from_up, far_turned))
    far_turned = other_core(far_turned)
    applied, own_diag = call(
        applied_kernel,
        [((rows_dev, both), bf16), ((1, both), f32)],
        [vmem] * 4,
        [],
        from_up,
        own_cols,
        from_down,
        gated,
        bytes_accessed=2**22,
    )
    far_applied = other_core(applied)

    plane = ZS * row_count
    sent = ((plane + 16, both), bf16)
    one, three, two, chip, diag = call(
        product_kernel,
        [sent, sent, sent, ((plane, both), f32), ((1, both), f32)],
        [smem] + [vmem] * 7,
        [],
        place,
        own_turned,
        far_turned,
        applied,
        far_applied,
        from_up,
        from_down,
        own_diag,
    )
    got = [along_x(two, 2), along_x(one, 1), along_x(three, 3)]
    got = [cells.astype(f32) for cells in got]
    chip = chip + sum(cells[:plane] for cells in got)
    diag = diag[0] + sum(cells[plane] + cells[plane + 1] for cells in got)
    high = lax.reduce_precision(diag, 8, 7)
    terms = jnp.stack([high, diag - high]).astype(bf16).reshape(-1, 128)
    terms = jnp.pad(terms, ((0, row_count - terms.shape[0]), (0, 0)))
    terms = jnp.broadcast_to(terms[None], (ZS, row_count, 128))
    pieces = chip.astype(bf16).reshape(ZS, row_count, both)
    got = swap(jnp.concatenate([pieces, terms], axis=2), "rows", z_groups)
    z_block, z_sent, packed = call(
        sum_kernel,
        [
            ((row_count, both), f32),
            ((ZS, row_count, both), bf16),
            ((COLS, row_count, both + col_count + 128), bf16),
        ],
        [vmem] * 2,
        [],
        got,
        rotation,
    )

    panel = swap(z_sent, "rows", z_groups)
    packed, panel = lax.optimization_barrier((packed, panel))
    panels = [panel] + [along_x(panel, steps) for steps in (1, 2, 3)]
    across = swap(packed, "cols")
    stacked, across = lax.optimization_barrier((jnp.stack(panels), across))
    away = other_core(stacked)
    block = (row_count, col_count)
    base, square, step = call(
        functools.partial(square_kernel, scale_factor),
        [
            ((row_count, both), f32),
            ((COLS, row_count, both), bf16),
            ((ZS * CORES,) + block, bf16),
        ],
        [smem] + [vmem] * 4,
        [
            pltpu.VMEM((COLS,) + block, f32),
            pltpu.VMEM((2, COLS, col_count), f32),
            pltpu.VMEM((2, col_count, COLS), f32),
        ],
        place,
        across,
        z_block,
        stacked,
        away,
    )

    step = swap(step, "rows", plane_groups)
    square, step = lax.optimization_barrier((square, step))
    steps_x = [step] + [along_x(step, steps) for steps in (1, 2, 3)]
    square = swap(square, "cols")
    half_block, half_sent = call(
        half_kernel,
        [((row_count, both), f32), ((COLS, row_count, both), bf16)],
        [vmem] * 2,
        [],
        square,
        base,
        flops=2**35,
    )
    half_rows = swap(half_sent, "cols", [col_order])
    rotated, orbitals = call(
        orbitals_kernel,
        [(block, f32), ((rows_dev, col_count), bf16)],
        [smem] * 2 + [vmem] * (3 + XS),
        [],
        place,
        atom_size,
        across,
        coeffs,
        rotation,
        *steps_x,
        flops=2**32,
    )
    phase_cos, phase_sin = call(
        phases_kernel,
        [(block, f32)] * 2,
        [smem] + [vmem] * (2 + XS),
        [],
        place,
        half_rows,
        half_block,
        *steps_x,
    )
    return (rotated, phase_cos, phase_sin, orbitals)


def solution(mesh):
    placed = (
        P("rows", None),
        P("rows", "cols"),
        P(None, "rows", None, None, None),
        P("rows", None),
        P("rows"),
    )
    return jax.shard_map(
        on_device,
        mesh=mesh,
        in_specs=placed,
        out_specs=(P("rows", "cols"), P("rows", "cols"), P("rows", "cols"), P("rows", "cols")),
        check_vma=False,
    )
```

```python
import functools
import math

import jax
import jax.numpy as jnp
from jax import lax
from jax.experimental import pallas as pl
from jax.experimental.pallas import tpu as pltpu
from jax.sharding import PartitionSpec as P

bf16 = jnp.bfloat16
f32 = jnp.float32

XS, ZS, CORES, COLS = 4, 8, 2, 8
x_steps = (0, 1, 3, 2)


def row_index(x, z, core):
    return (x * ZS + z) * CORES + core


z_groups = [[row_index(x, z, k) for z in range(ZS)] for x in range(XS) for k in range(CORES)]
z_order = [7, 6, 5, 4, 3, 2, 1, 0]
col_order = [4, 5, 6, 7, 3, 2, 1, 0]
plane_groups = [[row_index(x, z, k) for z in z_order for k in range(CORES)] for x in range(XS)]


def swap(cells, axis, groups=None):
    return lax.all_to_all(cells, axis, 0, 0, tiled=True, axis_index_groups=groups)


def other_core(cells):
    count = lax.axis_size("rows")
    return lax.ppermute(cells, "rows", [(i, i ^ 1) for i in range(count)])


def along_x(cells, steps):
    line, count = ZS * CORES, lax.axis_size("rows")
    return lax.ppermute(cells, "rows", [(i, (i + steps * line) % count) for i in range(count)])


def small_product(left, right):
    return jnp.dot(left, right, preferred_element_type=f32)


vmem = pl.BlockSpec(memory_space=pltpu.VMEM)
smem = pl.BlockSpec(memory_space=pltpu.SMEM)


def call(kernel, shapes, in_specs, scratch, *operands, bytes_accessed=2**20, flops=0):
    return pl.pallas_call(
        kernel,
        out_shape=[jax.ShapeDtypeStruct(*shape) for shape in shapes],
        in_specs=in_specs,
        out_specs=[vmem] * len(shapes),
        scratch_shapes=scratch,
        compiler_params=pltpu.CompilerParams(vmem_limit_bytes=12 * 2**20),
        cost_estimate=pl.CostEstimate(
            flops=flops, bytes_accessed=bytes_accessed, transcendentals=0
        ),
    )(*operands)


def within_rows(size_ref, cells):
    blocks = size_ref.shape[0]
    size = cells.shape[0] // blocks
    within = lax.broadcasted_iota(jnp.int32, (size, cells.shape[1]), 0)
    parts = [
        jnp.where(within < size_ref[b], cells[b * size : (b + 1) * size], 0.0)
        for b in range(blocks)
    ]
    return jnp.concatenate(parts, axis=0)


def turn_kernel(
    rows, place_ref, links_ref, live_ref, coeffs_ref, ops_ref, own_ref, far_ref, gated_ref
):
    core = place_ref[1]
    lanes = 128
    live = live_ref[...] > 0
    for start in range(0, coeffs_ref.shape[1], lanes):
        cells = coeffs_ref[:, start : start + lanes].astype(f32).T
        for offset in range(0, lanes, CORES * rows):
            first = cells[offset : offset + rows]
            second = cells[offset + rows : offset + 2 * rows]
            where = pl.ds((start + offset) // CORES, rows)
            own = jnp.where(core == 0, first, second)
            far = jnp.where(core == 0, second, first)
            own_ref[where, :] = jnp.where(live, own, 0.0).astype(bf16)
            far_ref[where, :] = jnp.where(live, far, 0.0).astype(bf16)
    phases, blocks, span, size, _ = ops_ref.shape
    for b in range(blocks):
        for t in range(span):
            link = links_ref[b, t] != 0
            for p in range(phases):
                cells = jnp.where(link, ops_ref[p, b, t].astype(f32), 0.0)
                gated_ref[p, b, :, t * size : (t + 1) * size] = cells.astype(bf16)


def applied_kernel(up_ref, cols_ref, down_ref, gated_ref, out_ref, diag_ref):
    phases, blocks, size, depth = gated_ref.shape
    width = cols_ref.shape[1]
    padded = jnp.concatenate([up_ref[...], cols_ref[...], down_ref[...]], axis=0)
    first = up_ref.shape[0] - (depth // size - 1) // 2 * size
    own = cols_ref[...].astype(f32)
    for p in range(phases):
        parts = []
        for b in range(blocks):
            start = first + b * size
            parts.append(small_product(gated_ref[p, b], padded[start : start + depth]))
        total = jnp.concatenate(parts, axis=0).astype(bf16)
        out_ref[:, p * width : (p + 1) * width] = total
        sums = jnp.sum(total.astype(f32) * own, axis=0, keepdims=True)
        diag_ref[:, p * width : (p + 1) * width] = sums


def product_kernel(
    place_ref, own_ref, far_ref, applied_ref, far_applied_ref, up_ref, down_ref, own_diag_ref,
    one_ref, three_ref, two_ref, none_ref, diag_ref,
):
    x, core = place_ref[0], place_ref[1]
    rows, both = none_ref.shape
    width = both // 2
    near = up_ref.shape[0] - far_applied_ref.shape[0]
    up = up_ref[near:, :].astype(f32)
    cols = jnp.where(core == 0, down_ref[: far_applied_ref.shape[0], :].astype(f32), up)
    sums = [
        jnp.sum(
            cols * far_applied_ref[:, p * width : (p + 1) * width].astype(f32),
            axis=0,
            keepdims=True,
        )
        for p in range(2)
    ]
    diag = own_diag_ref[...] + jnp.concatenate(sums, axis=1)
    diag_ref[...] = diag
    high = diag.astype(bf16).astype(f32)
    fill = jnp.zeros((two_ref.shape[0] - rows - 2, both), f32)
    tail = jnp.concatenate([high, diag - high, fill], axis=0).astype(bf16)
    for steps, out_ref in ((2, two_ref), (1, one_ref), (3, three_ref), (0, none_ref)):
        start = pl.multiple_of(lax.rem(x + steps, XS) * rows, rows)
        total = small_product(own_ref[pl.ds(start, rows), :], applied_ref[...])
        total = total + small_product(far_ref[pl.ds(start, rows), :], far_applied_ref[...])
        out_ref[:rows, :] = total.astype(out_ref.dtype)
        if steps:
            out_ref[rows:, :] = tail


def sum_kernel(got_ref, rotation_ref, block_ref, z_ref, packed_ref):
    count, _, wide = z_ref.shape
    total = got_ref[0].astype(f32)
    for i in range(1, count):
        total = total + got_ref[i].astype(f32)
    block = total[:, :wide]
    block_ref[...] = block
    half = block.astype(bf16)
    diag = total[:4, wide:] + total[4:8, wide:]
    high = diag.astype(bf16).astype(f32)
    fill = jnp.zeros((block.shape[0] - 8, 128), f32)
    tail = jnp.concatenate([high, diag - high, fill], axis=0).astype(bf16)
    packed = jnp.concatenate([half, rotation_ref[...].astype(bf16), tail], axis=1)
    for i in range(count):
        z_ref[i] = half
        packed_ref[i] = packed


def chunk(place_ref, own_ref, away_ref, k):
    core = place_ref[1]
    per = ZS * XS // COLS
    steps = lax.rem(place_ref[0] + XS - k * per // ZS, XS)
    where = sum(jnp.where(steps == step, i, 0) for i, step in enumerate(x_steps))
    parts = []
    for z in range(k * per % ZS, k * per % ZS + per):
        own, away = own_ref[where, z], away_ref[where, z]
        parts += [jnp.where(core == 0, own, away), jnp.where(core == 0, away, own)]
    return jnp.concatenate(parts, axis=0)


def rows_kernel(scale, place_ref, across_ref, rows_ref, diag_ref, turned_ref):
    mine, low = place_ref[2], place_ref[3]
    rows, width = rows_ref.shape[1:]
    terms = across_ref[:, :, -128:].astype(f32)
    per = width // 128
    for p in range(2):
        parts = [terms[:, p * per + h] + terms[:, 2 * per + p * per + h] for h in range(per)]
        diag_ref[p] = jnp.concatenate(parts, axis=1)
        turned_ref[p] = diag_ref[p].T
    lane = lax.broadcasted_iota(jnp.int32, (rows, COLS), 1)
    down = [
        jnp.sum(
            jnp.where(lane == mine, turned_ref[p, pl.ds(low, rows), :], 0.0),
            axis=1,
            keepdims=True,
        )
        for p in range(2)
    ]
    for k in range(COLS):
        cells = across_ref[k].astype(f32)
        cos_part = cells[:, :width] * (diag_ref[0, k : k + 1, :] - down[0])
        sin_part = cells[:, width : 2 * width] * (diag_ref[1, k : k + 1, :] - down[1])
        rows_ref[k] = (cos_part + sin_part) * scale


def square_kernel(
    scale, place_ref, rows_ref, diag_ref, turned_ref, block_ref, own_ref, away_ref,
    base_ref, sent_ref, step_ref,
):
    col = place_ref[4]
    rows, width = rows_ref.shape[1:]
    across_diag = [diag_ref[p, pl.ds(col, 1), :] for p in range(2)]
    square = jnp.zeros((rows, width), f32)
    base = block_ref[...]
    for k in range(COLS):
        near = rows_ref[k].astype(bf16)
        panel = chunk(place_ref, own_ref, away_ref, k)
        base = base - small_product(near, panel)
        cells = panel.astype(f32)
        cos_part = cells[:, :width] * (across_diag[0] - turned_ref[0, :, k : k + 1])
        sin_part = cells[:, width:] * (across_diag[1] - turned_ref[1, :, k : k + 1])
        cells = ((cos_part + sin_part) * scale).astype(bf16)
        square = square + small_product(near, cells)
    base_ref[...] = base
    step = (rows_ref[col] + 0.5 * square).astype(bf16)
    for k in range(step_ref.shape[0]):
        step_ref[k] = step
    square = square.astype(bf16)
    for k in range(COLS):
        panel = chunk(place_ref, own_ref, away_ref, k)
        for p in range(2):
            cells = lax.dot_general(
                square,
                panel[:, p * width : (p + 1) * width],
                (((1,), (1,)), ((), ())),
                preferred_element_type=f32,
            )
            sent_ref[k, :, p * width : (p + 1) * width] = cells.astype(bf16)


def half_kernel(got_ref, base_ref, half_ref, sent_ref):
    total = got_ref[0].astype(f32)
    for k in range(1, COLS):
        total = total + got_ref[k].astype(f32)
    total = base_ref[...] + 0.5 * total
    half_ref[...] = total
    sent = total.astype(bf16)
    for k in range(COLS):
        sent_ref[k] = sent


def pieces_of(place_ref, refs):
    width = refs[0].shape[-1]
    per = COLS // XS
    for steps, ref in zip(x_steps, refs):
        source = lax.rem(place_ref[0] + XS - steps, XS)
        for part in range(per):
            places = [
                z_order.index(z) * CORES
                for z in range(part * ZS // per, (part + 1) * ZS // per)
            ]
            cells = [ref[first : first + CORES].reshape(-1, width) for first in places]
            yield source * per + part, jnp.concatenate(cells, axis=0)


def orbitals_kernel(
    place_ref, size_ref, across_ref, coeffs_ref, rotation_ref, own0, own1, own2, own3,
    rotated_ref, orbitals_ref,
):
    width = rotated_ref.shape[1]
    rotated = rotation_ref[...]
    start = pl.multiple_of(place_ref[4] * width, width)
    orbitals = coeffs_ref[:, pl.ds(start, width)].astype(f32)
    for k, step in pieces_of(place_ref, (own0, own1, own2, own3)):
        rotated = rotated + small_product(across_ref[k, :, 2 * width : 3 * width], step)
        cells = coeffs_ref[:, pl.ds(pl.multiple_of(k * width, width), width)]
        orbitals = orbitals + small_product(cells, step)
    rotated_ref[...] = rotated
    orbitals_ref[...] = within_rows(size_ref, orbitals).astype(bf16)


def phases_kernel(
    place_ref, half_ref, block_ref, own0, own1, own2, own3, cos_ref, sin_ref
):
    width = cos_ref.shape[1]
    total = jnp.concatenate([block_ref[:, :width], block_ref[:, width:]], axis=0)
    for k, step in pieces_of(place_ref, (own0, own1, own2, own3)):
        where = sum(jnp.where(k == col, i, 0) for i, col in enumerate(col_order))
        cells = half_ref[where]
        cells = jnp.concatenate([cells[:, :width], cells[:, width:]], axis=0)
        total = total + small_product(cells, step)
    rows = cos_ref.shape[0]
    cos_ref[...] = total[:rows]
    sin_ref[...] = total[rows:]


def on_device(coeffs, rotation, phase_ops, block_links, atom_size):
    rows_dev, orbital_count = coeffs.shape
    span_blocks, block_size = phase_ops.shape[2:4]
    reach_blocks = (span_blocks - 1) // 2
    rows_axis = lax.axis_size("rows")
    cols_axis = lax.axis_size("cols")
    row_count = orbital_count // rows_axis
    col_count = orbital_count // cols_axis
    both = 2 * col_count
    core = lax.axis_index("rows") % CORES
    own_x = lax.axis_index("rows") // (ZS * CORES)
    per_col = rows_axis // cols_axis
    own_row = lax.axis_index("rows")
    place = [own_x, core, own_row // per_col, own_row % per_col * row_count]
    place = jnp.stack(place + [lax.axis_index("cols")]).astype(jnp.int32)
    scale_factor = 0.125 / math.sqrt(orbital_count)

    within = lax.broadcasted_iota(jnp.int32, (rows_dev // block_size, block_size), 1)
    live_rows = (within < atom_size[:, None]).reshape(rows_dev)
    own_cols = lax.dynamic_slice_in_dim(coeffs, lax.axis_index("cols") * col_count, col_count, 1)
    own_cols = jnp.where(live_rows[:, None], own_cols, jnp.zeros_like(own_cols))
    width = reach_blocks * block_size
    up = [(i, (i + 1) % rows_axis) for i in range(rows_axis)]
    down = [((i + 1) % rows_axis, i) for i in range(rows_axis)]
    from_up = lax.ppermute(own_cols[rows_dev - width :], "rows", up)
    from_down = lax.ppermute(own_cols[:width], "rows", down)
    turn_coeffs, own_cols, live_rows = lax.optimization_barrier((coeffs, own_cols, live_rows))
    half_shape = ((orbital_count // CORES, rows_dev), bf16)
    phases, blocks = phase_ops.shape[:2]
    own_turned, far_turned, gated = call(
        functools.partial(turn_kernel, row_count),
        [half_shape] * 2 + [((phases, blocks, block_size, span_blocks * block_size), bf16)],
        [smem] * 2 + [vmem] * 3,
        [],
        place,
        block_links,
        live_rows.astype(f32)[None, :],
        turn_coeffs,
        phase_ops,
        bytes_accessed=2**26,
    )
    from_down, from_up, far_turned = lax.optimization_barrier((from_down, from_up, far_turned))
    far_turned = other_core(far_turned)
    applied, own_diag = call(
        applied_kernel,
        [((rows_dev, both), bf16), ((1, both), f32)],
        [vmem] * 4,
        [],
        from_up,
        own_cols,
        from_down,
        gated,
        bytes_accessed=2**22,
    )
    far_applied = other_core(applied)

    plane = ZS * row_count
    sent = ((plane + 16, both), bf16)
    one, three, two, chip, diag = call(
        product_kernel,
        [sent, sent, sent, ((plane, both), f32), ((1, both), f32)],
        [smem] + [vmem] * 7,
        [],
        place,
        own_turned,
        far_turned,
        applied,
        far_applied,
        from_up,
        from_down,
        own_diag,
    )
    got = [along_x(two, 2), along_x(one, 1), along_x(three, 3)]
    got = [cells.astype(f32) for cells in got]
    chip = chip + sum(cells[:plane] for cells in got)
    diag = diag[0] + sum(cells[plane] + cells[plane + 1] for cells in got)
    high = lax.reduce_precision(diag, 8, 7)
    terms = jnp.stack([high, diag - high]).astype(bf16).reshape(-1, 128)
    terms = jnp.pad(terms, ((0, row_count - terms.shape[0]), (0, 0)))
    terms = jnp.broadcast_to(terms[None], (ZS, row_count, 128))
    pieces = chip.astype(bf16).reshape(ZS, row_count, both)
    got = swap(jnp.concatenate([pieces, terms], axis=2), "rows", z_groups)
    z_block, z_sent, packed = call(
        sum_kernel,
        [
            ((row_count, both), f32),
            ((ZS, row_count, both), bf16),
            ((COLS, row_count, both + col_count + 128), bf16),
        ],
        [vmem] * 2,
        [],
        got,
        rotation,
    )

    panel = swap(z_sent, "rows", z_groups)
    packed, panel = lax.optimization_barrier((packed, panel))
    panels = [panel] + [along_x(panel, steps) for steps in x_steps[1:]]
    across = swap(packed, "cols")
    stacked, across = lax.optimization_barrier((jnp.stack(panels), across))
    away = other_core(stacked)
    block = (row_count, col_count)
    gen_rows, diag_all, turned_diag = call(
        functools.partial(rows_kernel, scale_factor),
        [
            ((COLS,) + block, f32),
            ((2, COLS, col_count), f32),
            ((2, col_count, COLS), f32),
        ],
        [smem, vmem],
        [],
        place,
        across,
        flops=2**33,
    )
    base, square, step = call(
        functools.partial(square_kernel, scale_factor),
        [
            ((row_count, both), f32),
            ((COLS, row_count, both), bf16),
            ((ZS * CORES,) + block, bf16),
        ],
        [smem] + [vmem] * 6,
        [],
        place,
        gen_rows,
        diag_all,
        turned_diag,
        z_block,
        stacked,
        away,
    )

    step = swap(step, "rows", plane_groups)
    square, step = lax.optimization_barrier((square, step))
    steps_x = [step] + [along_x(step, steps) for steps in x_steps[1:]]
    square = swap(square, "cols")
    half_block, half_sent = call(
        half_kernel,
        [((row_count, both), f32), ((COLS, row_count, both), bf16)],
        [vmem] * 2,
        [],
        square,
        base,
        flops=2**35,
    )
    half_rows = swap(half_sent, "cols", [col_order])
    rotated, orbitals = call(
        orbitals_kernel,
        [(block, f32), ((rows_dev, col_count), bf16)],
        [smem] * 2 + [vmem] * (3 + XS),
        [],
        place,
        atom_size,
        across,
        coeffs,
        rotation,
        *steps_x,
        flops=2**32,
    )
    phase_cos, phase_sin = call(
        phases_kernel,
        [(block, f32)] * 2,
        [smem] + [vmem] * (2 + XS),
        [],
        place,
        half_rows,
        half_block,
        *steps_x,
    )
    return (rotated, phase_cos, phase_sin, orbitals)


def solution(mesh):
    placed = (
        P("rows", None),
        P("rows", "cols"),
        P(None, "rows", None, None, None),
        P("rows", None),
        P("rows"),
    )
    return jax.shard_map(
        on_device,
        mesh=mesh,
        in_specs=placed,
        out_specs=(P("rows", "cols"), P("rows", "cols"), P("rows", "cols"), P("rows", "cols")),
        check_vma=False,
    )
```

```python
import functools
import math

import jax
import jax.numpy as jnp
from jax import lax
from jax.experimental import pallas as pl
from jax.experimental.pallas import tpu as pltpu
from jax.sharding import PartitionSpec as P

bf16 = jnp.bfloat16
f32 = jnp.float32

XS, ZS, CORES, COLS = 4, 8, 2, 8
x_steps = (0, 1, 3, 2)


def row_index(x, z, core):
    return (x * ZS + z) * CORES + core


z_groups = [[row_index(x, z, k) for z in range(ZS)] for x in range(XS) for k in range(CORES)]
z_order = [7, 6, 5, 4, 3, 2, 1, 0]
col_order = [4, 5, 6, 7, 3, 2, 1, 0]
plane_groups = [[row_index(x, z, k) for z in z_order for k in range(CORES)] for x in range(XS)]


def swap(cells, axis, groups=None):
    return lax.all_to_all(cells, axis, 0, 0, tiled=True, axis_index_groups=groups)


def other_core(cells):
    count = lax.axis_size("rows")
    return lax.ppermute(cells, "rows", [(i, i ^ 1) for i in range(count)])


def along_x(cells, steps):
    line, count = ZS * CORES, lax.axis_size("rows")
    return lax.ppermute(cells, "rows", [(i, (i + steps * line) % count) for i in range(count)])


def small_product(left, right):
    return jnp.dot(left, right, preferred_element_type=f32)


vmem = pl.BlockSpec(memory_space=pltpu.VMEM)
smem = pl.BlockSpec(memory_space=pltpu.SMEM)


def call(kernel, shapes, in_specs, scratch, *operands, bytes_accessed=2**20, flops=0):
    return pl.pallas_call(
        kernel,
        out_shape=[jax.ShapeDtypeStruct(*shape) for shape in shapes],
        in_specs=in_specs,
        out_specs=[vmem] * len(shapes),
        scratch_shapes=scratch,
        compiler_params=pltpu.CompilerParams(vmem_limit_bytes=12 * 2**20),
        cost_estimate=pl.CostEstimate(
            flops=flops, bytes_accessed=bytes_accessed, transcendentals=0
        ),
    )(*operands)


def within_rows(size_ref, cells):
    blocks = size_ref.shape[0]
    size = cells.shape[0] // blocks
    within = lax.broadcasted_iota(jnp.int32, (size, cells.shape[1]), 0)
    parts = [
        jnp.where(within < size_ref[b], cells[b * size : (b + 1) * size], 0.0)
        for b in range(blocks)
    ]
    return jnp.concatenate(parts, axis=0)


def turn_kernel(
    rows, place_ref, links_ref, live_ref, coeffs_ref, ops_ref, own_ref, far_ref, gated_ref
):
    core = place_ref[1]
    lanes = 128
    live = live_ref[...] > 0
    for start in range(0, coeffs_ref.shape[1], lanes):
        cells = coeffs_ref[:, start : start + lanes].astype(f32).T
        for offset in range(0, lanes, CORES * rows):
            first = cells[offset : offset + rows]
            second = cells[offset + rows : offset + 2 * rows]
            where = pl.ds((start + offset) // CORES, rows)
            own = jnp.where(core == 0, first, second)
            far = jnp.where(core == 0, second, first)
            own_ref[where, :] = jnp.where(live, own, 0.0).astype(bf16)
            far_ref[where, :] = jnp.where(live, far, 0.0).astype(bf16)
    phases, blocks, span, size, _ = ops_ref.shape
    for b in range(blocks):
        for t in range(span):
            link = links_ref[b, t] != 0
            for p in range(phases):
                cells = jnp.where(link, ops_ref[p, b, t].astype(f32), 0.0)
                gated_ref[p, b, :, t * size : (t + 1) * size] = cells.astype(bf16)


def applied_kernel(up_ref, cols_ref, down_ref, gated_ref, out_ref, diag_ref):
    phases, blocks, size, depth = gated_ref.shape
    width = cols_ref.shape[1]
    padded = jnp.concatenate([up_ref[...], cols_ref[...], down_ref[...]], axis=0)
    first = up_ref.shape[0] - (depth // size - 1) // 2 * size
    own = cols_ref[...].astype(f32)
    for p in range(phases):
        parts = []
        for b in range(blocks):
            start = first + b * size
            parts.append(small_product(gated_ref[p, b], padded[start : start + depth]))
        total = jnp.concatenate(parts, axis=0).astype(bf16)
        out_ref[:, p * width : (p + 1) * width] = total
        sums = jnp.sum(total.astype(f32) * own, axis=0, keepdims=True)
        diag_ref[:, p * width : (p + 1) * width] = sums


def own_kernel(place_ref, own_ref, applied_ref, part_ref):
    rows = part_ref.shape[1]
    for steps in range(XS):
        start = pl.multiple_of(lax.rem(place_ref[0] + steps, XS) * rows, rows)
        part_ref[steps] = small_product(own_ref[pl.ds(start, rows), :], applied_ref[...])


def product_kernel(
    place_ref, part_ref, far_ref, far_applied_ref, up_ref, down_ref, own_diag_ref,
    one_ref, three_ref, two_ref, none_ref, diag_ref,
):
    x, core = place_ref[0], place_ref[1]
    rows, both = none_ref.shape
    width = both // 2
    near = up_ref.shape[0] - far_applied_ref.shape[0]
    up = up_ref[near:, :].astype(f32)
    cols = jnp.where(core == 0, down_ref[: far_applied_ref.shape[0], :].astype(f32), up)
    sums = [
        jnp.sum(
            cols * far_applied_ref[:, p * width : (p + 1) * width].astype(f32),
            axis=0,
            keepdims=True,
        )
        for p in range(2)
    ]
    diag = own_diag_ref[...] + jnp.concatenate(sums, axis=1)
    diag_ref[...] = diag
    high = diag.astype(bf16).astype(f32)
    fill = jnp.zeros((two_ref.shape[0] - rows - 2, both), f32)
    tail = jnp.concatenate([high, diag - high, fill], axis=0).astype(bf16)
    for steps, out_ref in ((2, two_ref), (1, one_ref), (3, three_ref), (0, none_ref)):
        start = pl.multiple_of(lax.rem(x + steps, XS) * rows, rows)
        total = small_product(far_ref[pl.ds(start, rows), :], far_applied_ref[...])
        total = part_ref[steps] + total
        out_ref[:rows, :] = total.astype(out_ref.dtype)
        if steps:
            out_ref[rows:, :] = tail


def sum_kernel(got_ref, rotation_ref, block_ref, z_ref, packed_ref):
    count, _, wide = z_ref.shape
    total = got_ref[0].astype(f32)
    for i in range(1, count):
        total = total + got_ref[i].astype(f32)
    block = total[:, :wide]
    block_ref[...] = block
    half = block.astype(bf16)
    diag = total[:4, wide:] + total[4:8, wide:]
    high = diag.astype(bf16).astype(f32)
    fill = jnp.zeros((block.shape[0] - 8, 128), f32)
    tail = jnp.concatenate([high, diag - high, fill], axis=0).astype(bf16)
    packed = jnp.concatenate([half, rotation_ref[...].astype(bf16), tail], axis=1)
    for i in range(count):
        z_ref[i] = half
        packed_ref[i] = packed


def chunk(place_ref, own_ref, away_ref, k):
    core = place_ref[1]
    per = ZS * XS // COLS
    steps = lax.rem(place_ref[0] + XS - k * per // ZS, XS)
    where = sum(jnp.where(steps == step, i, 0) for i, step in enumerate(x_steps))
    parts = []
    for z in range(k * per % ZS, k * per % ZS + per):
        own, away = own_ref[where, z], away_ref[where, z]
        parts += [jnp.where(core == 0, own, away), jnp.where(core == 0, away, own)]
    return jnp.concatenate(parts, axis=0)


def rows_kernel(scale, place_ref, across_ref, rows_ref, diag_ref, turned_ref):
    mine, low = place_ref[2], place_ref[3]
    rows, width = rows_ref.shape[1:]
    terms = across_ref[:, :, -128:].astype(f32)
    per = width // 128
    for p in range(2):
        parts = [terms[:, p * per + h] + terms[:, 2 * per + p * per + h] for h in range(per)]
        diag_ref[p] = jnp.concatenate(parts, axis=1) * scale
        turned_ref[p] = diag_ref[p].T
    lane = lax.broadcasted_iota(jnp.int32, (rows, COLS), 1)
    down = [
        jnp.sum(
            jnp.where(lane == mine, turned_ref[p, pl.ds(low, rows), :], 0.0),
            axis=1,
            keepdims=True,
        )
        for p in range(2)
    ]
    for k in range(COLS):
        cells = across_ref[k].astype(f32)
        cos_part = cells[:, :width] * (diag_ref[0, k : k + 1, :] - down[0])
        sin_part = cells[:, width : 2 * width] * (diag_ref[1, k : k + 1, :] - down[1])
        rows_ref[k] = cos_part + sin_part


def square_kernel(
    place_ref, rows_ref, diag_ref, turned_ref, block_ref, own_ref, away_ref,
    base_ref, sent_ref, step_ref,
):
    col = place_ref[4]
    rows, width = rows_ref.shape[1:]
    across_diag = [diag_ref[p, pl.ds(col, 1), :] for p in range(2)]
    square = jnp.zeros((rows, width), f32)
    base = block_ref[...]
    for k in range(COLS):
        near = rows_ref[k].astype(bf16)
        panel = chunk(place_ref, own_ref, away_ref, k)
        base = base - small_product(near, panel)
        cells = panel.astype(f32)
        cos_part = cells[:, :width] * (across_diag[0] - turned_ref[0, :, k : k + 1])
        sin_part = cells[:, width:] * (across_diag[1] - turned_ref[1, :, k : k + 1])
        cells = (cos_part + sin_part).astype(bf16)
        square = square + small_product(near, cells)
    base_ref[...] = base
    step = (rows_ref[col] + 0.5 * square).astype(bf16)
    for k in range(step_ref.shape[0]):
        step_ref[k] = step
    square = square.astype(bf16)
    for k in range(COLS):
        panel = chunk(place_ref, own_ref, away_ref, k)
        for p in range(2):
            cells = lax.dot_general(
                square,
                panel[:, p * width : (p + 1) * width],
                (((1,), (1,)), ((), ())),
                preferred_element_type=f32,
            )
            sent_ref[k, :, p * width : (p + 1) * width] = cells.astype(bf16)


def half_kernel(got_ref, base_ref, half_ref, sent_ref):
    total = got_ref[0].astype(f32)
    for k in range(1, COLS):
        total = total + got_ref[k].astype(f32)
    total = base_ref[...] + 0.5 * total
    half_ref[...] = total
    sent = total.astype(bf16)
    for k in range(COLS):
        sent_ref[k] = sent


def pieces_of(place_ref, refs):
    width = refs[0].shape[-1]
    per = COLS // XS
    for steps, ref in zip(x_steps, refs):
        source = lax.rem(place_ref[0] + XS - steps, XS)
        for part in range(per):
            places = [
                z_order.index(z) * CORES
                for z in range(part * ZS // per, (part + 1) * ZS // per)
            ]
            cells = [ref[first : first + CORES].reshape(-1, width) for first in places]
            yield source * per + part, jnp.concatenate(cells, axis=0)


def orbitals_kernel(
    place_ref, size_ref, across_ref, coeffs_ref, rotation_ref, own0, own1, own2, own3,
    rotated_ref, orbitals_ref,
):
    width = rotated_ref.shape[1]
    rotated = rotation_ref[...]
    start = pl.multiple_of(place_ref[4] * width, width)
    orbitals = coeffs_ref[:, pl.ds(start, width)].astype(f32)
    for k, step in pieces_of(place_ref, (own0, own1, own2, own3)):
        rotated = rotated + small_product(across_ref[k, :, 2 * width : 3 * width], step)
        cells = coeffs_ref[:, pl.ds(pl.multiple_of(k * width, width), width)]
        orbitals = orbitals + small_product(cells, step)
    rotated_ref[...] = rotated
    orbitals_ref[...] = within_rows(size_ref, orbitals).astype(bf16)


def phases_kernel(
    place_ref, half_ref, block_ref, own0, own1, own2, own3, cos_ref, sin_ref
):
    width = cos_ref.shape[1]
    total = jnp.concatenate([block_ref[:, :width], block_ref[:, width:]], axis=0)
    for k, step in pieces_of(place_ref, (own0, own1, own2, own3)):
        where = sum(jnp.where(k == col, i, 0) for i, col in enumerate(col_order))
        cells = half_ref[where]
        cells = jnp.concatenate([cells[:, :width], cells[:, width:]], axis=0)
        total = total + small_product(cells, step)
    rows = cos_ref.shape[0]
    cos_ref[...] = total[:rows]
    sin_ref[...] = total[rows:]


def on_device(coeffs, rotation, phase_ops, block_links, atom_size):
    rows_dev, orbital_count = coeffs.shape
    span_blocks, block_size = phase_ops.shape[2:4]
    reach_blocks = (span_blocks - 1) // 2
    rows_axis = lax.axis_size("rows")
    cols_axis = lax.axis_size("cols")
    row_count = orbital_count // rows_axis
    col_count = orbital_count // cols_axis
    both = 2 * col_count
    core = lax.axis_index("rows") % CORES
    own_x = lax.axis_index("rows") // (ZS * CORES)
    per_col = rows_axis // cols_axis
    own_row = lax.axis_index("rows")
    place = [own_x, core, own_row // per_col, own_row % per_col * row_count]
    place = jnp.stack(place + [lax.axis_index("cols")]).astype(jnp.int32)
    scale_factor = 0.125 / math.sqrt(orbital_count)

    within = lax.broadcasted_iota(jnp.int32, (rows_dev // block_size, block_size), 1)
    live_rows = (within < atom_size[:, None]).reshape(rows_dev)
    own_cols = lax.dynamic_slice_in_dim(coeffs, lax.axis_index("cols") * col_count, col_count, 1)
    own_cols = jnp.where(live_rows[:, None], own_cols, jnp.zeros_like(own_cols))
    width = reach_blocks * block_size
    up = [(i, (i + 1) % rows_axis) for i in range(rows_axis)]
    down = [((i + 1) % rows_axis, i) for i in range(rows_axis)]
    from_up = lax.ppermute(own_cols[rows_dev - width :], "rows", up)
    from_down = lax.ppermute(own_cols[:width], "rows", down)
    turn_coeffs, own_cols, live_rows = lax.optimization_barrier((coeffs, own_cols, live_rows))
    half_shape = ((orbital_count // CORES, rows_dev), bf16)
    phases, blocks = phase_ops.shape[:2]
    own_turned, far_turned, gated = call(
        functools.partial(turn_kernel, row_count),
        [half_shape] * 2 + [((phases, blocks, block_size, span_blocks * block_size), bf16)],
        [smem] * 2 + [vmem] * 3,
        [],
        place,
        block_links,
        live_rows.astype(f32)[None, :],
        turn_coeffs,
        phase_ops,
        bytes_accessed=2**26,
    )
    from_down, from_up, far_turned = lax.optimization_barrier((from_down, from_up, far_turned))
    far_turned = other_core(far_turned)
    applied, own_diag = call(
        applied_kernel,
        [((rows_dev, both), bf16), ((1, both), f32)],
        [vmem] * 4,
        [],
        from_up,
        own_cols,
        from_down,
        gated,
        bytes_accessed=2**22,
    )
    far_applied = other_core(applied)

    plane = ZS * row_count
    (part,) = call(
        own_kernel,
        [((XS, plane, both), f32)],
        [smem] + [vmem] * 2,
        [],
        place,
        own_turned,
        applied,
        flops=2**32,
    )
    sent = ((plane + 16, both), bf16)
    one, three, two, chip, diag = call(
        product_kernel,
        [sent, sent, sent, ((plane, both), f32), ((1, both), f32)],
        [smem] + [vmem] * 6,
        [],
        place,
        part,
        far_turned,
        far_applied,
        from_up,
        from_down,
        own_diag,
    )
    got = [along_x(two, 2), along_x(one, 1), along_x(three, 3)]
    got = [cells.astype(f32) for cells in got]
    chip = chip + sum(cells[:plane] for cells in got)
    diag = diag[0] + sum(cells[plane] + cells[plane + 1] for cells in got)
    high = lax.reduce_precision(diag, 8, 7)
    terms = jnp.stack([high, diag - high]).astype(bf16).reshape(-1, 128)
    terms = jnp.pad(terms, ((0, row_count - terms.shape[0]), (0, 0)))
    terms = jnp.broadcast_to(terms[None], (ZS, row_count, 128))
    pieces = chip.astype(bf16).reshape(ZS, row_count, both)
    got = swap(jnp.concatenate([pieces, terms], axis=2), "rows", z_groups)
    z_block, z_sent, packed = call(
        sum_kernel,
        [
            ((row_count, both), f32),
            ((ZS, row_count, both), bf16),
            ((COLS, row_count, both + col_count + 128), bf16),
        ],
        [vmem] * 2,
        [],
        got,
        rotation,
    )

    panel = swap(z_sent, "rows", z_groups)
    packed, panel = lax.optimization_barrier((packed, panel))
    panels = [panel] + [along_x(panel, steps) for steps in x_steps[1:]]
    across = swap(packed, "cols")
    stacked, across = lax.optimization_barrier((jnp.stack(panels), across))
    away = other_core(stacked)
    block = (row_count, col_count)
    gen_rows, diag_all, turned_diag = call(
        functools.partial(rows_kernel, scale_factor),
        [
            ((COLS,) + block, f32),
            ((2, COLS, col_count), f32),
            ((2, col_count, COLS), f32),
        ],
        [smem, vmem],
        [],
        place,
        across,
        flops=2**33,
    )
    base, square, step = call(
        square_kernel,
        [
            ((row_count, both), f32),
            ((COLS, row_count, both), bf16),
            ((ZS * CORES,) + block, bf16),
        ],
        [smem] + [vmem] * 6,
        [],
        place,
        gen_rows,
        diag_all,
        turned_diag,
        z_block,
        stacked,
        away,
    )

    step = swap(step, "rows", plane_groups)
    square, step = lax.optimization_barrier((square, step))
    steps_x = [step] + [along_x(step, steps) for steps in x_steps[1:]]
    square = swap(square, "cols")
    half_block, half_sent = call(
        half_kernel,
        [((row_count, both), f32), ((COLS, row_count, both), bf16)],
        [vmem] * 2,
        [],
        square,
        base,
        flops=2**35,
    )
    half_rows = swap(half_sent, "cols", [col_order])
    rotated, orbitals = call(
        orbitals_kernel,
        [(block, f32), ((rows_dev, col_count), bf16)],
        [smem] * 2 + [vmem] * (3 + XS),
        [],
        place,
        atom_size,
        across,
        coeffs,
        rotation,
        *steps_x,
        flops=2**32,
    )
    phase_cos, phase_sin = call(
        phases_kernel,
        [(block, f32)] * 2,
        [smem] + [vmem] * (2 + XS),
        [],
        place,
        half_rows,
        half_block,
        *steps_x,
    )
    return (rotated, phase_cos, phase_sin, orbitals)


def solution(mesh):
    placed = (
        P("rows", None),
        P("rows", "cols"),
        P(None, "rows", None, None, None),
        P("rows", None),
        P("rows"),
    )
    return jax.shard_map(
        on_device,
        mesh=mesh,
        in_specs=placed,
        out_specs=(P("rows", "cols"), P("rows", "cols"), P("rows", "cols"), P("rows", "cols")),
        check_vma=False,
    )
```
